32 devices in a mesh: dp: 8 (over z, core), seq: 4 (over y, x).
Axes of the slice: x: 2, y: 2, z: 4, core: 2. Of those that a mesh axis runs over, the one named last changes fastest.
Arguments:
- image_tokens: bfloat16 [32, 1024, 1024], P('dp', 'seq'), may hold values from -6 to 6
- text_states: bfloat16 [32, 128, 1024], P('dp', 'seq'), may hold values from -6 to 6
- text_lengths: int32 [32], P('dp'), may hold values from 8 to 128, as said below
- out_grad: bfloat16 [32, 1024, 1024], P('dp', 'seq'), may hold values from -6 to 6
- norm1_gain: bfloat16 [1024], P(('dp', 'seq')), may hold values from 0.5 to 1.5
- norm1_bias: bfloat16 [1024], P(('dp', 'seq')), may hold values from -1.75 to 1.75
- self_qkv: bfloat16 [1024, 3072], P(('dp', 'seq')), may hold values from -0.1875 to 0.1875
- self_bias_qv: bfloat16 [2048], P(('dp', 'seq')), may hold values from -1.75 to 1.75
- self_out: bfloat16 [1024, 1024], P(('dp', 'seq')), may hold values from -0.75 to 0.75
- self_out_bias: bfloat16 [1024], P(('dp', 'seq')), may hold values from -1.75 to 1.75
- norm2_gain: bfloat16 [1024], P(('dp', 'seq')), may hold values from 0.5 to 1.5
- norm2_bias: bfloat16 [1024], P(('dp', 'seq')), may hold values from -1.75 to 1.75
- cross_query: bfloat16 [1024, 1024], P(('dp', 'seq')), may hold values from -0.1875 to 0.1875
- cross_kv: bfloat16 [1024, 2048], P(('dp', 'seq')), may hold values from -0.1875 to 0.1875
- cross_bias_qv: bfloat16 [2048], P(('dp', 'seq')), may hold values from -1.75 to 1.75
- cross_out: bfloat16 [1024, 1024], P(('dp', 'seq')), may hold values from -0.375 to 0.375
- cross_out_bias: bfloat16 [1024], P(('dp', 'seq')), may hold values from -1.75 to 1.75
- norm3_gain: bfloat16 [1024], P(('dp', 'seq')), may hold values from 0.5 to 1.5
- norm3_bias: bfloat16 [1024], P(('dp', 'seq')), may hold values from -1.75 to 1.75
- mlp_in: bfloat16 [1024, 4096], P(('dp', 'seq')), may hold values from -0.1875 to 0.1875
- mlp_in_bias: bfloat16 [4096], P(('dp', 'seq')), may hold values from -1.75 to 1.75
- mlp_out: bfloat16 [4096, 1024], P(('dp', 'seq')), may hold values from -0.09375 to 0.09375
- mlp_out_bias: bfloat16 [1024], P(('dp', 'seq')), may hold values from -1.75 to 1.75
Outputs:
- block_output: bfloat16 [32, 1024, 1024], P('dp', 'seq')
- image_grad: float32 [32, 1024, 1024], P('dp', 'seq')
- text_grad: float32 [32, 128, 1024], P('dp', 'seq')
- norm1_gain_grad: float32 [1024], P(('dp', 'seq'))
- norm1_bias_grad: float32 [1024], P(('dp', 'seq'))
- self_qkv_grad: float32 [1024, 3072], P(('dp', 'seq'))
- self_bias_qv_grad: float32 [2048], P(('dp', 'seq'))
- self_out_grad: float32 [1024, 1024], P(('dp', 'seq'))
- self_out_bias_grad: float32 [1024], P(('dp', 'seq'))
- norm2_gain_grad: float32 [1024], P(('dp', 'seq'))
- norm2_bias_grad: float32 [1024], P(('dp', 'seq'))
- cross_query_grad: float32 [1024, 1024], P(('dp', 'seq'))
- cross_kv_grad: float32 [1024, 2048], P(('dp', 'seq'))
- cross_bias_qv_grad: float32 [2048], P(('dp', 'seq'))
- cross_out_grad: float32 [1024, 1024], P(('dp', 'seq'))
- cross_out_bias_grad: float32 [1024], P(('dp', 'seq'))
- norm3_gain_grad: float32 [1024], P(('dp', 'seq'))
- norm3_bias_grad: float32 [1024], P(('dp', 'seq'))
- mlp_in_grad: float32 [1024, 4096], P(('dp', 'seq'))
- mlp_in_bias_grad: float32 [4096], P(('dp', 'seq'))
- mlp_out_grad: float32 [4096, 1024], P(('dp', 'seq'))
- mlp_out_bias_grad: float32 [1024], P(('dp', 'seq'))
The draws below stay inside these ranges and needn't reach their ends.
Inputs may be any that keep to these rules, and one draw needn't show every extreme that they name: `text_lengths`: prompt positions at or beyond an image's length are padding. In every draw some image has exactly 128 prompt tokens and some exactly 8.
All inputs are finite; a program needn't handle non-finite values.
Results may differ from the reference program's by a relative error of at most 0.025.
Values may be sent and summed in bfloat16 or wider, within the bound.
No kernel may reach another device: no remote copies, remote signals or barrier semaphores. Data moves between devices by JAX's collectives and lax.ppermute only.
A program may use at most 256 MiB of HBM per device.

```python
import jax
import jax.numpy as jnp
from jax import lax

D = 1024
HEADS = 16
HEAD_DIM = 64
FF = 4096
IMG_LEN = 1024
TEXT = 128
IMG_DEV = 4
IMAGES = 32
N_DP = 8


def draw_text_lengths(key, part):
    first_key = jax.random.fold_in(key, 11)
    second_key = jax.random.fold_in(key, 12)
    third_key = jax.random.fold_in(key, 13)
    lengths = jax.random.randint(first_key, (IMAGES,), 8, TEXT + 1, dtype=jnp.int32)
    longest = jax.random.randint(second_key, (), 0, IMAGES, dtype=jnp.int32)
    shortest = (longest + 1 + jax.random.randint(third_key, (), 0, IMAGES - 1, dtype=jnp.int32)) % IMAGES
    positions = jnp.arange(IMAGES, dtype=jnp.int32)
    lengths = jnp.where(positions == longest, TEXT, lengths)
    lengths = jnp.where(positions == shortest, 8, lengths)
    return lengths.astype(jnp.int32)


def level_of(stream_key, shape, shards, smallest, top_value):
    factor_of = 1.0
    for position, blocks in shards:
        heights = jax.random.uniform(jax.random.fold_in(jax.random.fold_in(stream_key, 6), position), (blocks,), jnp.float32, smallest / len(shards), top_value / len(shards))
        factor_of = factor_of * jnp.repeat(jnp.exp(heights), shape[position] // blocks).reshape((-1,) + (1,) * (len(shape) - 1 - position))
    return factor_of


def centred(stream_key, shape, scale, bound, pieces=(), held_as=jnp.bfloat16):
    values = scale * jax.random.normal(stream_key, shape, jnp.float32)
    if pieces:
        values = values * level_of(stream_key, shape, pieces, -0.22, 0.18)
    return jnp.clip(values, -bound, bound).astype(held_as)


def setup_inputs(seed: int = 0) -> dict:
    splits = jax.random.split(jax.random.key(seed), 24)
    image_tokens = centred(splits[0], (IMAGES, IMG_LEN, D), 1.0, 6.0, ((0, 8), (1, 4)))
    text_states = centred(splits[1], (IMAGES, TEXT, D), 1.0, 6.0, ((0, 8), (1, 4)))
    text_lengths = draw_text_lengths(jax.random.fold_in(splits[23], 71), 0)
    out_grad = centred(splits[3], (IMAGES, IMG_LEN, D), 1.0, 6.0, ((0, 8), (1, 4)))
    norm1_gain = jnp.clip(1.0 + 0.1 * jax.random.normal(splits[4], (D,), jnp.float32), 0.5, 1.5).astype(jnp.bfloat16)
    norm1_bias = centred(splits[5], (D,), 0.3, 1.75, ((0, 32),))
    self_qkv = centred(splits[6], (D, 3 * D), D ** -0.5, 0.1875, ((0, 32),))
    self_bias_qv = centred(splits[7], (2 * D,), 0.3, 1.75, ((0, 32),))
    self_out = centred(splits[8], (D, D), (D // 16) ** -0.5, 0.75, ((0, 32),))
    self_out_bias = centred(splits[9], (D,), 0.3, 1.75, ((0, 32),))
    norm2_gain = jnp.clip(1.0 + 0.1 * jax.random.normal(splits[10], (D,), jnp.float32), 0.5, 1.5).astype(jnp.bfloat16)
    norm2_bias = centred(splits[11], (D,), 0.3, 1.75, ((0, 32),))
    cross_query = centred(splits[12], (D, D), D ** -0.5, 0.1875, ((0, 32),))
    cross_kv = centred(splits[13], (D, 2 * D), D ** -0.5, 0.1875, ((0, 32),))
    cross_bias_qv = centred(splits[14], (2 * D,), 0.3, 1.75, ((0, 32),))
    cross_out = centred(splits[15], (D, D), (D // 4) ** -0.5, 0.375, ((0, 32),))
    cross_out_bias = centred(splits[16], (D,), 0.3, 1.75, ((0, 32),))
    norm3_gain = jnp.clip(1.0 + 0.1 * jax.random.normal(splits[17], (D,), jnp.float32), 0.5, 1.5).astype(jnp.bfloat16)
    norm3_bias = centred(splits[18], (D,), 0.3, 1.75, ((0, 32),))
    mlp_in = centred(splits[19], (D, FF), D ** -0.5, 0.1875, ((0, 32),))
    mlp_in_bias = centred(splits[20], (FF,), 0.3, 1.75, ((0, 32),))
    mlp_out = centred(splits[21], (FF, D), FF ** -0.5, 0.09375, ((0, 32),))
    mlp_out_bias = centred(splits[22], (D,), 0.3, 1.75, ((0, 32),))
    return dict(image_tokens=image_tokens, text_states=text_states, text_lengths=text_lengths, out_grad=out_grad, norm1_gain=norm1_gain, norm1_bias=norm1_bias, self_qkv=self_qkv, self_bias_qv=self_bias_qv, self_out=self_out, self_out_bias=self_out_bias, norm2_gain=norm2_gain, norm2_bias=norm2_bias, cross_query=cross_query, cross_kv=cross_kv, cross_bias_qv=cross_bias_qv, cross_out=cross_out, cross_out_bias=cross_out_bias, norm3_gain=norm3_gain, norm3_bias=norm3_bias, mlp_in=mlp_in, mlp_in_bias=mlp_in_bias, mlp_out=mlp_out, mlp_out_bias=mlp_out_bias)


@jax.custom_vjp
def low(v):
    return lax.optimization_barrier(v.astype(jnp.bfloat16)).astype(jnp.float32)

@jax.custom_vjp
def low_back(v):
    return v

def low_keep(v):
    return (low(v), None)

def low_pass(kept, grad):
    return (grad,)

def back_keep(v):
    return (v, None)

def back_low(kept, grad):
    return (low(grad),)
low.defvjp(low_keep, low_pass)
low_back.defvjp(back_keep, back_low)
EPSILON = 1e-05
SCALING = 0.125
NEGATIVE = -1e+30

def layer_norm(values, gain, shift):
    center = values - lax.optimization_barrier(jnp.mean(values, axis=-1, keepdims=True))
    inverse = lax.rsqrt(lax.optimization_barrier(jnp.mean(center * center, axis=-1, keepdims=True)) + EPSILON)
    return center * inverse * gain + shift

def project(left, weight):
    return jnp.einsum('bld,de->ble', left, weight, precision=lax.Precision.HIGHEST)

def attention(query_rows, key_rows, value_rows, mask):
    batch_size, length = (query_rows.shape[0], query_rows.shape[1])
    key_count = key_rows.shape[1]
    query_heads = query_rows.reshape(batch_size, length, HEADS, HEAD_DIM)
    key_heads = key_rows.reshape(batch_size, key_count, HEADS, HEAD_DIM)
    value_heads = value_rows.reshape(batch_size, key_count, HEADS, HEAD_DIM)
    scores = low_back(jnp.einsum('bqhd,bkhd->bhqk', query_heads, key_heads, precision=lax.Precision.HIGHEST) * SCALING)
    scores = jnp.where(mask, scores, NEGATIVE)
    probs = low(jax.nn.softmax(scores, axis=-1))
    mixed = jnp.einsum('bhqk,bkhd->bqhd', probs, value_heads, precision=lax.Precision.HIGHEST)
    return mixed.reshape(batch_size, length, HEADS * HEAD_DIM)

def layer(params, tokens, texts, lengths):
    gain_one, shift_one, w_qkv, bias_qv, w_self, b_self, gain_two, shift_two, w_cquery, w_ckv, cross_bias, w_cross, b_cross, gain_three, shift_three, w_in, b_in, w_out, b_out = params
    hidden_one = low(layer_norm(tokens, gain_one, shift_one))
    mixed = project(hidden_one, w_qkv)
    query_one = low(low_back(mixed[..., :D] + bias_qv[:D]))
    key_one = low(low_back(mixed[..., D:2 * D]))
    value_one = low(low_back(mixed[..., 2 * D:] + bias_qv[D:]))
    positions = jnp.arange(IMG_LEN, dtype=jnp.int32)
    causal = (positions[None, :] <= positions[:, None])[None, None]
    attended = low(low_back(attention(query_one, key_one, value_one, causal)))
    after_self = tokens + low_back(project(attended, w_self) + b_self)
    hidden_two = low(layer_norm(after_self, gain_two, shift_two))
    query_two = low(low_back(project(hidden_two, w_cquery) + cross_bias[:D]))
    text_mixed = project(texts, w_ckv)
    key_two = low(low_back(text_mixed[..., :D]))
    value_two = low(low_back(text_mixed[..., D:] + cross_bias[D:]))
    text_pos = jnp.arange(TEXT, dtype=jnp.int32)
    padded = (text_pos[None, :] < lengths[:, None])[:, None, None, :]
    attended_two = low(low_back(attention(query_two, key_two, value_two, padded)))
    after_cross = after_self + low_back(project(attended_two, w_cross) + b_cross)
    hidden_three = low(layer_norm(after_cross, gain_three, shift_three))
    pre_act = low_back(project(hidden_three, w_in) + b_in)
    activated = low(jax.nn.gelu(pre_act, approximate=True))
    return after_cross + low_back(project(activated, w_out) + b_out)

def add_pair(first, second):
    return first + second

def reference(image_tokens, text_states, text_lengths, out_grad, norm1_gain, norm1_bias, self_qkv, self_bias_qv, self_out, self_out_bias, norm2_gain, norm2_bias, cross_query, cross_kv, cross_bias_qv, cross_out, cross_out_bias, norm3_gain, norm3_bias, mlp_in, mlp_in_bias, mlp_out, mlp_out_bias):
    params = tuple((weight.astype(jnp.float32) for weight in (norm1_gain, norm1_bias, self_qkv, self_bias_qv, self_out, self_out_bias, norm2_gain, norm2_bias, cross_query, cross_kv, cross_bias_qv, cross_out, cross_out_bias, norm3_gain, norm3_bias, mlp_in, mlp_in_bias, mlp_out, mlp_out_bias)))

    def regroup(array):
        return array.astype(jnp.float32).reshape((N_DP, IMG_DEV) + array.shape[1:])
    token_groups = regroup(image_tokens)
    text_groups = regroup(text_states)
    grad_groups = regroup(out_grad)
    length_groups = text_lengths.astype(jnp.int32).reshape(N_DP, IMG_DEV)

    def group_step(totals, group_items):
        tokens, texts, lengths, grad_rows = group_items

        def forward(weights, token_rows, text_rows):
            return layer(weights, token_rows, text_rows, lengths)
        output, pull_back = jax.vjp(forward, params, tokens, texts)
        weight_grads, token_grads, text_grads = pull_back(grad_rows)
        return (jax.tree.map(add_pair, totals, weight_grads), (output, token_grads, text_grads))
    zeros = jax.tree.map(jnp.zeros_like, params)
    totals, (outputs, token_grads, text_grads) = lax.scan(group_step, zeros, (token_groups, text_groups, length_groups, grad_groups))
    block_output = outputs.reshape(IMAGES, IMG_LEN, D).astype(jnp.bfloat16)
    image_grad = token_grads.reshape(IMAGES, IMG_LEN, D)
    text_grad = text_grads.reshape(IMAGES, TEXT, D)
    return (block_output, image_grad, text_grad, totals[0], totals[1], totals[2], totals[3], totals[4], totals[5], totals[6], totals[7], totals[8], totals[9], totals[10], totals[11], totals[12], totals[13], totals[14], totals[15], totals[16], totals[17], totals[18])
```

```python
import functools

import jax
import jax.numpy as jnp
from jax import lax
from jax.experimental import pallas as pl
from jax.experimental.pallas import tpu as pltpu
from jax.sharding import PartitionSpec as P

D = 1024
HEADS = 16
HEAD_DIM = 64


EPSILON = 1e-05
SCALING = 0.125
NEGATIVE = -1e30
VMEM = 48 * 1024 * 1024


def layer_norm(values, gain, shift):
    center = values - jnp.mean(values, axis=-1, keepdims=True)
    inverse = lax.rsqrt(jnp.mean(center * center, axis=-1, keepdims=True) + EPSILON)
    normed = center * inverse
    return (normed * gain + shift, normed, inverse)


def norm_back(grad_rows, normed, inverse, gain):
    scaled = grad_rows * gain
    back = inverse * (
        scaled
        - jnp.mean(scaled, axis=-1, keepdims=True)
        - normed * jnp.mean(scaled * normed, axis=-1, keepdims=True)
    )
    return (back, jnp.sum(grad_rows * normed, axis=(0, 1)), jnp.sum(grad_rows, axis=(0, 1)))


def project(left, weight):
    return jnp.einsum("bld,de->ble", left, weight, preferred_element_type=jnp.float32)


def project_back(grad_rows, weight):
    return jnp.einsum("ble,de->bld", grad_rows, weight, preferred_element_type=jnp.float32)


def weight_grad(left, grad_rows):
    return jnp.einsum("bld,ble->de", left, grad_rows, preferred_element_type=jnp.float32)


def column_sums(grad_rows):
    return jnp.sum(grad_rows.astype(jnp.float32), axis=(0, 1))


def split_heads(rows):
    return rows.reshape(rows.shape[0], rows.shape[1], HEADS, HEAD_DIM)


def gelu_tanh(values):
    return jax.nn.gelu(values, approximate=True)


def block_scores(queries, key_rows, start, width, mask_at):
    key_block = split_heads(lax.dynamic_slice_in_dim(key_rows, start, width, 1))
    scores = (
        jnp.einsum("bqhd,bkhd->bhqk", queries, key_block, preferred_element_type=jnp.float32)
        * SCALING
    )
    return (jnp.where(mask_at(start, width), scores, NEGATIVE), key_block)


def attend(query_rows, key_rows, value_rows, mask_at, width):
    queries = split_heads(query_rows)
    batch_size, length = (query_rows.shape[0], query_rows.shape[1])
    blocks = key_rows.shape[1] // width

    def stats(block_index, carry):
        running_max, running_sum = carry
        scores, key_block = block_scores(queries, key_rows, block_index * width, width, mask_at)
        new_max = jnp.maximum(running_max, jnp.max(scores, axis=-1))
        running_sum = running_sum * jnp.exp(running_max - new_max) + jnp.sum(
            jnp.exp(scores - new_max[..., None]), axis=-1
        )
        return (new_max, running_sum)

    start_max = jnp.full((batch_size, HEADS, length), NEGATIVE, jnp.float32)
    final_max, final_sum = lax.fori_loop(0, blocks, stats, (start_max, jnp.zeros_like(start_max)))
    log_total = final_max + jnp.log(final_sum)

    def accumulate(block_index, total):
        start = block_index * width
        scores, key_block = block_scores(queries, key_rows, start, width, mask_at)
        weights = jnp.exp(scores - log_total[..., None]).astype(jnp.bfloat16)
        value_block = split_heads(lax.dynamic_slice_in_dim(value_rows, start, width, 1))
        return total + jnp.einsum(
            "bhqk,bkhd->bqhd", weights, value_block, preferred_element_type=jnp.float32
        )

    total = lax.fori_loop(
        0, blocks, accumulate, jnp.zeros((batch_size, length, HEADS, HEAD_DIM), jnp.float32)
    )
    return (total.reshape(batch_size, length, HEADS * HEAD_DIM).astype(jnp.bfloat16), log_total)


def attend_back(query_rows, key_rows, value_rows, grad_rows, log_total, mask_at, width):
    queries = split_heads(query_rows)
    grad_heads = split_heads(grad_rows)
    batch_size, length = (query_rows.shape[0], query_rows.shape[1])
    blocks = key_rows.shape[1] // width

    def weights_at(start):
        scores, key_block = block_scores(queries, key_rows, start, width, mask_at)
        value_block = split_heads(lax.dynamic_slice_in_dim(value_rows, start, width, 1))
        probs = jnp.exp(scores - log_total[..., None])
        grad_probs = jnp.einsum(
            "bqhd,bkhd->bhqk", grad_heads, value_block, preferred_element_type=jnp.float32
        )
        return (probs, grad_probs, key_block)

    def inner(block_index, delta):
        probs, grad_probs, key_block = weights_at(block_index * width)
        return delta + jnp.sum(probs * grad_probs, axis=-1)

    delta = lax.fori_loop(0, blocks, inner, jnp.zeros((batch_size, HEADS, length), jnp.float32))
    start_grad = jnp.zeros((batch_size, length, HEADS, HEAD_DIM), jnp.float32)

    def step(grad_queries, block_index):
        probs, grad_probs, key_block = weights_at(block_index * width)
        grad_scores = (probs * (grad_probs - delta[..., None])).astype(jnp.bfloat16)
        grad_queries = grad_queries + jnp.einsum(
            "bhqk,bkhd->bqhd", grad_scores, key_block, preferred_element_type=jnp.float32
        )
        grad_keys = jnp.einsum(
            "bhqk,bqhd->bkhd", grad_scores, queries, preferred_element_type=jnp.float32
        )
        grad_values = jnp.einsum(
            "bhqk,bqhd->bkhd",
            probs.astype(jnp.bfloat16),
            grad_heads,
            preferred_element_type=jnp.float32,
        )
        return (grad_queries, (grad_keys, grad_values))

    grad_queries, (key_parts, value_parts) = lax.scan(
        step, start_grad, jnp.arange(blocks, dtype=jnp.int32)
    )

    def merge_blocks(parts):
        return jnp.moveaxis(parts, 0, 1).reshape(batch_size, blocks * width, HEADS * HEAD_DIM)

    return (
        (grad_queries * SCALING).reshape(batch_size, length, HEADS * HEAD_DIM),
        merge_blocks(key_parts) * SCALING,
        merge_blocks(value_parts),
        delta,
    )


def gather_self(gain, shift, weight_qkv, bias_qv, weight_out, bias_out):
    return (
        lax.all_gather(gain, ("dp", "seq"), axis=0, tiled=True),
        lax.all_gather(shift, ("dp", "seq"), axis=0, tiled=True),
        lax.all_gather(weight_qkv, ("dp", "seq"), axis=0, tiled=True),
        lax.all_gather(bias_qv, ("dp", "seq"), axis=0, tiled=True),
        lax.all_gather(weight_out, ("dp", "seq"), axis=0, tiled=True),
        lax.all_gather(bias_out, ("dp", "seq"), axis=0, tiled=True),
    )


def gather_cross(gain, shift, weight_query, weight_kv, bias_qv, weight_out, bias_out):
    return (
        lax.all_gather(gain, ("dp", "seq"), axis=0, tiled=True),
        lax.all_gather(shift, ("dp", "seq"), axis=0, tiled=True),
        lax.all_gather(weight_query, ("dp", "seq"), axis=0, tiled=True),
        lax.all_gather(weight_kv, ("dp", "seq"), axis=0, tiled=True),
        lax.all_gather(bias_qv, ("dp", "seq"), axis=0, tiled=True),
        lax.all_gather(weight_out, ("dp", "seq"), axis=0, tiled=True),
        lax.all_gather(bias_out, ("dp", "seq"), axis=0, tiled=True),
    )


def gather_mlp(gain, shift, weight_in, bias_in, weight_out, bias_out):
    return (
        lax.all_gather(gain, ("dp", "seq"), axis=0, tiled=True),
        lax.all_gather(shift, ("dp", "seq"), axis=0, tiled=True),
        lax.all_gather(weight_in, ("dp", "seq"), axis=0, tiled=True),
        lax.all_gather(bias_in, ("dp", "seq"), axis=0, tiled=True),
        lax.all_gather(weight_out, ("dp", "seq"), axis=0, tiled=True),
        lax.all_gather(bias_out, ("dp", "seq"), axis=0, tiled=True),
    )


def per_device(
    image_tokens,
    text_states,
    text_lengths,
    out_grad,
    norm1_gain,
    norm1_bias,
    self_qkv,
    self_bias_qv,
    self_out,
    self_out_bias,
    norm2_gain,
    norm2_bias,
    cross_query,
    cross_kv,
    cross_bias_qv,
    cross_out,
    cross_out_bias,
    norm3_gain,
    norm3_bias,
    mlp_in,
    mlp_in_bias,
    mlp_out,
    mlp_out_bias,
):
    length = image_tokens.shape[1]
    own_start = lax.axis_index("seq") * length
    query_pos = own_start + jnp.arange(length, dtype=jnp.int32)

    def causal_at(start, width):
        key_pos = start + jnp.arange(width, dtype=jnp.int32)
        return (key_pos[None, :] <= query_pos[:, None])[None, None]

    def padded_at(start, width):
        key_pos = start + jnp.arange(width, dtype=jnp.int32)
        return (key_pos[None, :] < text_lengths[:, None])[:, None, None, :]

    self_full = gather_self(norm1_gain, norm1_bias, self_qkv, self_bias_qv, self_out, self_out_bias)
    residual = image_tokens.astype(jnp.float32)
    normed_in, normed_one, inverse_one = layer_norm(
        residual, self_full[0].astype(jnp.float32), self_full[1].astype(jnp.float32)
    )
    hidden_one = normed_in.astype(jnp.bfloat16)
    mixed = project(hidden_one, self_full[2])
    bias_self = self_full[3].astype(jnp.float32)
    query_one = (mixed[..., :D] + bias_self[:D]).astype(jnp.bfloat16)
    key_one = mixed[..., D : 2 * D].astype(jnp.bfloat16)
    value_one = (mixed[..., 2 * D :] + bias_self[D:]).astype(jnp.bfloat16)
    key_all, value_all = (
        lax.all_gather(key_one, "seq", axis=1, tiled=True),
        lax.all_gather(value_one, "seq", axis=1, tiled=True),
    )
    self_width = min(128, key_all.shape[1])
    attended, log_one = attend(query_one, key_all, value_all, causal_at, self_width)
    after_self = residual + project(attended, self_full[4]) + self_full[5].astype(jnp.float32)
    cross_full = gather_cross(
        norm2_gain, norm2_bias, cross_query, cross_kv, cross_bias_qv, cross_out, cross_out_bias
    )
    normed_mid, normed_two, inverse_two = layer_norm(
        after_self, cross_full[0].astype(jnp.float32), cross_full[1].astype(jnp.float32)
    )
    hidden_two = normed_mid.astype(jnp.bfloat16)
    bias_cross = cross_full[4].astype(jnp.float32)
    query_two = (project(hidden_two, cross_full[2]) + bias_cross[:D]).astype(jnp.bfloat16)
    text_mixed = project(text_states, cross_full[3])
    text_key = text_mixed[..., :D].astype(jnp.bfloat16)
    text_value = (text_mixed[..., D:] + bias_cross[D:]).astype(jnp.bfloat16)
    key_two, value_two = (
        lax.all_gather(text_key, "seq", axis=1, tiled=True),
        lax.all_gather(text_value, "seq", axis=1, tiled=True),
    )
    text_width = key_two.shape[1]
    attended_two, log_two = attend(query_two, key_two, value_two, padded_at, text_width)
    after_cross = (
        after_self + project(attended_two, cross_full[5]) + cross_full[6].astype(jnp.float32)
    )
    mlp_full = gather_mlp(norm3_gain, norm3_bias, mlp_in, mlp_in_bias, mlp_out, mlp_out_bias)
    normed_last, normed_three, inverse_three = layer_norm(
        after_cross, mlp_full[0].astype(jnp.float32), mlp_full[1].astype(jnp.float32)
    )
    hidden_three = normed_last.astype(jnp.bfloat16)
    pre_act = project(hidden_three, mlp_full[2]) + mlp_full[3].astype(jnp.float32)
    activated, gelu_back = jax.vjp(gelu_tanh, pre_act)
    act_low = activated.astype(jnp.bfloat16)
    block_output = (
        after_cross + project(act_low, mlp_full[4]) + mlp_full[5].astype(jnp.float32)
    ).astype(jnp.bfloat16)
    mlp_back = gather_mlp(norm3_gain, norm3_bias, mlp_in, mlp_in_bias, mlp_out, mlp_out_bias)
    grad_top = out_grad.astype(jnp.float32)
    w_out_grad = weight_grad(act_low, out_grad)
    b_out_grad = column_sums(out_grad)
    grad_act = project_back(out_grad, mlp_back[4])
    grad_pre = gelu_back(grad_act)[0].astype(jnp.bfloat16)
    w_in_grad = weight_grad(hidden_three, grad_pre)
    b_in_grad = column_sums(grad_pre)
    back_three, gain_three_grad, shift_three_grad = norm_back(
        project_back(grad_pre, mlp_back[2]),
        normed_three,
        inverse_three,
        mlp_back[0].astype(jnp.float32),
    )
    grad_two = grad_top + back_three
    mlp_grads = (
        lax.psum_scatter(gain_three_grad, ("dp", "seq"), scatter_dimension=0, tiled=True),
        lax.psum_scatter(shift_three_grad, ("dp", "seq"), scatter_dimension=0, tiled=True),
        lax.psum_scatter(w_in_grad, ("dp", "seq"), scatter_dimension=0, tiled=True),
        lax.psum_scatter(b_in_grad, ("dp", "seq"), scatter_dimension=0, tiled=True),
        lax.psum_scatter(w_out_grad, ("dp", "seq"), scatter_dimension=0, tiled=True),
        lax.psum_scatter(b_out_grad, ("dp", "seq"), scatter_dimension=0, tiled=True),
    )
    cross_back = gather_cross(
        norm2_gain, norm2_bias, cross_query, cross_kv, cross_bias_qv, cross_out, cross_out_bias
    )
    grad_cross = grad_two.astype(jnp.bfloat16)
    cross_out_term = weight_grad(attended_two, grad_cross)
    cross_bias_term = column_sums(grad_cross)
    grad_att_two = project_back(grad_cross, cross_back[5]).astype(jnp.bfloat16)
    grad_query_two, grad_key_two, grad_value_two, delta_two = attend_back(
        query_two, key_two, value_two, grad_att_two, log_two, padded_at, text_width
    )
    query_two_low = grad_query_two.astype(jnp.bfloat16)
    text_key_grad, text_value_grad = (
        lax.psum_scatter(
            grad_key_two.astype(jnp.bfloat16), "seq", scatter_dimension=1, tiled=True
        ).astype(jnp.float32),
        lax.psum_scatter(
            grad_value_two.astype(jnp.bfloat16), "seq", scatter_dimension=1, tiled=True
        ).astype(jnp.float32),
    )
    text_value_low = text_value_grad.astype(jnp.bfloat16)
    text_kv_grad = jnp.concatenate([text_key_grad.astype(jnp.bfloat16), text_value_low], axis=-1)
    cross_query_term = weight_grad(hidden_two, query_two_low)
    cross_kv_term = weight_grad(text_states, text_kv_grad)
    cross_qv_term = jnp.concatenate([column_sums(query_two_low), column_sums(text_value_low)])
    text_grad = project_back(text_kv_grad, cross_back[3])
    back_two, gain_two_grad, shift_two_grad = norm_back(
        project_back(query_two_low, cross_back[2]),
        normed_two,
        inverse_two,
        cross_back[0].astype(jnp.float32),
    )
    grad_one = grad_two + back_two
    cross_grads = (
        lax.psum_scatter(gain_two_grad, ("dp", "seq"), scatter_dimension=0, tiled=True),
        lax.psum_scatter(shift_two_grad, ("dp", "seq"), scatter_dimension=0, tiled=True),
        lax.psum_scatter(cross_query_term, ("dp", "seq"), scatter_dimension=0, tiled=True),
        lax.psum_scatter(cross_kv_term, ("dp", "seq"), scatter_dimension=0, tiled=True),
        lax.psum_scatter(cross_qv_term, ("dp", "seq"), scatter_dimension=0, tiled=True),
        lax.psum_scatter(cross_out_term, ("dp", "seq"), scatter_dimension=0, tiled=True),
        lax.psum_scatter(cross_bias_term, ("dp", "seq"), scatter_dimension=0, tiled=True),
    )
    self_back = gather_self(norm1_gain, norm1_bias, self_qkv, self_bias_qv, self_out, self_out_bias)
    grad_self = grad_one.astype(jnp.bfloat16)
    self_out_term = weight_grad(attended, grad_self)
    self_bias_term = column_sums(grad_self)
    grad_att_one = project_back(grad_self, self_back[4]).astype(jnp.bfloat16)
    grad_query_one, grad_key_all, grad_value_all, delta_one = attend_back(
        query_one, key_all, value_all, grad_att_one, log_one, causal_at, self_width
    )
    grad_key_one, grad_value_one = (
        lax.psum_scatter(
            grad_key_all.astype(jnp.bfloat16), "seq", scatter_dimension=1, tiled=True
        ).astype(jnp.float32),
        lax.psum_scatter(
            grad_value_all.astype(jnp.bfloat16), "seq", scatter_dimension=1, tiled=True
        ).astype(jnp.float32),
    )
    query_one_low = grad_query_one.astype(jnp.bfloat16)
    value_one_low = grad_value_one.astype(jnp.bfloat16)
    grad_qkv = jnp.concatenate(
        [query_one_low, grad_key_one.astype(jnp.bfloat16), value_one_low], axis=-1
    )
    self_qkv_term = weight_grad(hidden_one, grad_qkv)
    self_qv_term = jnp.concatenate([column_sums(query_one_low), column_sums(value_one_low)])
    back_one, gain_one_grad, shift_one_grad = norm_back(
        project_back(grad_qkv, self_back[2]),
        normed_one,
        inverse_one,
        self_back[0].astype(jnp.float32),
    )
    image_grad = grad_one + back_one
    self_grads = (
        lax.psum_scatter(gain_one_grad, ("dp", "seq"), scatter_dimension=0, tiled=True),
        lax.psum_scatter(shift_one_grad, ("dp", "seq"), scatter_dimension=0, tiled=True),
        lax.psum_scatter(self_qkv_term, ("dp", "seq"), scatter_dimension=0, tiled=True),
        lax.psum_scatter(self_qv_term, ("dp", "seq"), scatter_dimension=0, tiled=True),
        lax.psum_scatter(self_out_term, ("dp", "seq"), scatter_dimension=0, tiled=True),
        lax.psum_scatter(self_bias_term, ("dp", "seq"), scatter_dimension=0, tiled=True),
    )
    return (
        block_output,
        image_grad,
        text_grad,
        self_grads[0],
        self_grads[1],
        self_grads[2],
        self_grads[3],
        self_grads[4],
        self_grads[5],
        cross_grads[0],
        cross_grads[1],
        cross_grads[2],
        cross_grads[3],
        cross_grads[4],
        cross_grads[5],
        cross_grads[6],
        mlp_grads[0],
        mlp_grads[1],
        mlp_grads[2],
        mlp_grads[3],
        mlp_grads[4],
        mlp_grads[5],
    )


LOG2E = 1.4426950408889634
LN2 = 0.6931471805599453
QB = 256
PAIR = 2 * HEAD_DIM
NT = (((1,), (1,)), ((), ()))
NN = (((1,), (0,)), ((), ()))
TN = (((0,), (0,)), ((), ()))


def mm(left, right, dims=NN):
    return lax.dot_general(left, right, dims, preferred_element_type=jnp.float32)


def head_lanes(rows, head):
    lane = lax.broadcasted_iota(jnp.int32, rows.shape, 1)
    keep = (lane < HEAD_DIM) if head == 0 else (lane >= HEAD_DIM)
    return jnp.where(keep, rows, jnp.zeros_like(rows))


def attend_kernel(causal, len_ref, q_ref, k_ref, v_ref, o_ref, lse_ref, vx_ref):
    keys = k_ref.shape[0]
    length = q_ref.shape[0]
    block = min(QB, length)
    vx_ref[:, :PAIR] = v_ref[...]
    vx_ref[:, PAIR:] = jnp.ones((keys, PAIR), jnp.bfloat16)
    for start in range(0, length, block):
        limit = start + block if causal else keys
        rows = q_ref[start : start + block, :]
        both = []
        for head in range(2):
            scores = mm(head_lanes(rows, head), k_ref[:limit, :], NT)
            col = lax.broadcasted_iota(jnp.int32, scores.shape, 1)
            if causal:
                row = lax.broadcasted_iota(jnp.int32, scores.shape, 0) + start
                scores = jnp.where(col <= row, scores, NEGATIVE)
            else:
                scores = jnp.where(col < len_ref[0], scores, NEGATIVE)
            top = jnp.max(scores, axis=1, keepdims=True)
            weights = jnp.exp2(scores - top).astype(jnp.bfloat16)
            total = mm(weights, vx_ref[:limit, :])
            both.append(total[:, :PAIR] / total[:, PAIR:])
            stat = (top + jnp.log2(total[:, PAIR:])).T
            lse_ref[0, head : head + 1, start : start + block] = stat[:1, :]
        lane = lax.broadcasted_iota(jnp.int32, both[0].shape, 1)
        merged = jnp.where(lane < HEAD_DIM, both[0], both[1])
        o_ref[start : start + block, :] = merged.astype(jnp.bfloat16)


def attend_back_kernel(
    causal, len_ref, q_ref, k_ref, v_ref, o_ref, do_ref, lse_ref, dq_ref, dk_ref, dv_ref, acc_ref
):
    keys = k_ref.shape[0]
    length = q_ref.shape[0]
    block = min(QB, keys)
    product = (do_ref[...].astype(jnp.float32) * o_ref[...].astype(jnp.float32)).T
    acc_ref[...] = jnp.zeros_like(acc_ref)
    delta = [
        jnp.sum(product[head * HEAD_DIM : (head + 1) * HEAD_DIM, :], axis=0, keepdims=True)
        for head in range(2)
    ]
    for start in range(0, keys, block):
        first = start if causal else 0
        key_rows = k_ref[start : start + block, :]
        value_rows = v_ref[start : start + block, :]
        grad_keys = grad_values = None
        for head in range(2):
            queries = head_lanes(q_ref[first:, :], head)
            grads = head_lanes(do_ref[first:, :], head)
            scores = mm(key_rows, queries, NT)
            probs = jnp.exp2(scores - lse_ref[0, head : head + 1, first:])
            row = lax.broadcasted_iota(jnp.int32, scores.shape, 0)
            if causal:
                col = lax.broadcasted_iota(jnp.int32, scores.shape, 1)
                probs = jnp.where(row <= col, probs, 0.0)
            else:
                probs = jnp.where(row + start < len_ref[0], probs, 0.0)
            back = mm(value_rows, grads, NT)
            scored = (probs * (back - delta[head][:, first:])).astype(jnp.bfloat16)
            term_v = mm(probs.astype(jnp.bfloat16), grads)
            term_k = mm(scored, queries)
            grad_values = term_v if grad_values is None else grad_values + term_v
            grad_keys = term_k if grad_keys is None else grad_keys + term_k
            acc_ref[first:, :] += mm(scored, head_lanes(key_rows, head), TN)
        dk_ref[start : start + block, :] = (grad_keys * LN2).astype(jnp.bfloat16)
        dv_ref[start : start + block, :] = grad_values.astype(jnp.bfloat16)
    dq_ref[...] = (acc_ref[...] * SCALING).astype(jnp.bfloat16)


def flash(lengths, query, keys, values, offsets, causal):
    length, count = (query.shape[0], keys.shape[0])
    pairs = HEADS // 2

    def columns(rows, offset):
        return pl.BlockSpec((rows, PAIR), lambda i, *_: (0, i + offset))

    area = length * count * HEADS // (2 if causal else 1)
    return pl.pallas_call(
        functools.partial(attend_kernel, causal),
        grid_spec=pltpu.PrefetchScalarGridSpec(
            num_scalar_prefetch=1,
            grid=(pairs,),
            in_specs=[
                columns(length, offsets[0]),
                columns(count, offsets[1]),
                columns(count, offsets[2]),
            ],
            out_specs=[
                columns(length, 0),
                pl.BlockSpec((1, 2, length), lambda i, *_: (i, 0, 0)),
            ],
            scratch_shapes=[pltpu.VMEM((count, 2 * PAIR), jnp.bfloat16)],
        ),
        out_shape=[
            jax.ShapeDtypeStruct((length, D), jnp.bfloat16),
            jax.ShapeDtypeStruct((pairs, 2, length), jnp.float32),
        ],
        compiler_params=pltpu.CompilerParams(vmem_limit_bytes=VMEM),
        cost_estimate=pl.CostEstimate(
            flops=area * 1024, bytes_accessed=8 * length * D, transcendentals=area
        ),
        name="attend",
    )(lengths, query, keys, values)


def flash_back(lengths, query, keys, values, offsets, out, grad, lse, causal):
    length, count = (query.shape[0], keys.shape[0])
    pairs = HEADS // 2

    def columns(rows, offset):
        return pl.BlockSpec((rows, PAIR), lambda i, *_: (0, i + offset))

    area = length * count * HEADS // (2 if causal else 1)
    return pl.pallas_call(
        functools.partial(attend_back_kernel, causal),
        grid_spec=pltpu.PrefetchScalarGridSpec(
            num_scalar_prefetch=1,
            grid=(pairs,),
            in_specs=[
                columns(length, offsets[0]),
                columns(count, offsets[1]),
                columns(count, offsets[2]),
                columns(length, 0),
                columns(length, 0),
                pl.BlockSpec((1, 2, length), lambda i, *_: (i, 0, 0)),
            ],
            out_specs=[columns(length, 0), columns(count, 0), columns(count, 0)],
            scratch_shapes=[pltpu.VMEM((length, PAIR), jnp.float32)],
        ),
        out_shape=[
            jax.ShapeDtypeStruct((length, D), jnp.bfloat16),
            jax.ShapeDtypeStruct((count, D), jnp.bfloat16),
            jax.ShapeDtypeStruct((count, D), jnp.bfloat16),
        ],
        compiler_params=pltpu.CompilerParams(vmem_limit_bytes=VMEM),
        cost_estimate=pl.CostEstimate(
            flops=area * 2560, bytes_accessed=14 * length * D, transcendentals=area
        ),
        name="attend_back",
    )(lengths, query, keys, values, out, grad, lse)


def gelu_pair(values):
    root = 0.7978845608028654
    square = values * values
    bend = jnp.tanh(root * values * (1.0 + 0.044715 * square))
    half = 0.5 * (1.0 + bend)
    slope = half + 0.5 * values * (1.0 - bend * bend) * root * (1.0 + 0.134145 * square)
    return (values * half, slope)


def norm_rows(rows, gain, shift):
    center = rows - jnp.mean(rows, axis=-1, keepdims=True)
    inverse = lax.rsqrt(jnp.mean(center * center, axis=-1, keepdims=True) + EPSILON)
    normed = center * inverse
    return ((normed * gain + shift).astype(jnp.bfloat16), normed, inverse)


def norm_rows_back(grad_rows, normed, inverse, gain):
    scaled = grad_rows * gain
    back = inverse * (
        scaled
        - jnp.mean(scaled, axis=-1, keepdims=True)
        - normed * jnp.mean(scaled * normed, axis=-1, keepdims=True)
    )
    return (back, jnp.sum(grad_rows * normed, axis=0), jnp.sum(grad_rows, axis=0))


def total_of(*terms):
    total = terms[0].astype(jnp.float32)
    for term in terms[1:]:
        total = total + term.astype(jnp.float32)
    return total


def pick(array, index, axis):
    return lax.dynamic_index_in_dim(array, index, axis, keepdims=False)


class Ring:
    def __init__(self, n_dp, n_seq):
        dp, seq = (lax.axis_index("dp"), lax.axis_index("seq"))
        self.count = n_dp * n_seq
        self.seq = seq
        self.index = dp * n_seq + seq
        self.x, self.y, self.c, self.z = (seq % 2, seq // 2, dp % 2, dp // 2)

    def swap(self, array, bits):
        return lax.ppermute(array, ("dp", "seq"), [(i, i ^ bits) for i in range(self.count)])

    def spread_sum(self, grads):
        widths = [grad.shape[-1] for grad in grads]
        per = grads[0].shape[0] // self.count
        views = [grad.reshape(4, 2, 2, 2, per, grad.shape[-1]) for grad in grads]

        def joined(parts):
            return parts[0] if len(parts) == 1 else jnp.concatenate(parts, axis=-1)

        sent = joined([pick(view, 1 - self.c, 1).astype(jnp.bfloat16) for view in views])
        kept = joined([pick(view, self.c, 1).astype(jnp.bfloat16) for view in views])
        got = self.swap(sent, 4)
        half = sum(widths) // 2
        halves = []
        for side, (axis, bit, other_bit) in enumerate(((1, 2, 1), (2, 1, 2))):
            cut = slice(side * half, (side + 1) * half)
            here, there = (self.y, self.x) if side == 0 else (self.x, self.y)
            mine, came = (kept[..., cut], got[..., cut])
            out = total_of(pick(mine, 1 - here, axis), pick(came, 1 - here, axis))
            back = self.swap(out.astype(jnp.bfloat16), bit)
            mine, came = (pick(mine, here, axis), pick(came, here, axis))
            out = total_of(*(pick(part, 1 - there, 1) for part in (mine, came, back)))
            last = self.swap(out.astype(jnp.bfloat16), other_bit)
            halves.append(
                [*(pick(part, there, 1) for part in (mine, came, back)), last]
            )
        result = [total_of(*(pick(part, self.z, 0) for part in parts)) for parts in halves]
        result = jnp.concatenate(result, axis=-1)
        for step in (1, 2, 3):
            out = jnp.concatenate(
                [total_of(*(pick(p, self.z ^ step, 0) for p in parts)).astype(jnp.bfloat16) for parts in halves],
                axis=-1,
            )
            result = result + self.swap(out, 8 * step).astype(jnp.float32)
        ends = [sum(widths[: i + 1]) for i in range(len(widths))]
        return [result[:, end - width : end] for end, width in zip(ends, widths)]


def whole_images(n_dp, n_seq, *args):
    (
        image_tokens,
        text_states,
        text_lengths,
        out_grad,
        norm1_gain,
        norm1_bias,
        self_qkv,
        self_bias_qv,
        self_out,
        self_out_bias,
        norm2_gain,
        norm2_bias,
        cross_query,
        cross_kv,
        cross_bias_qv,
        cross_out,
        cross_out_bias,
        norm3_gain,
        norm3_bias,
        mlp_in,
        mlp_in_bias,
        mlp_out,
        mlp_out_bias,
    ) = args
    f32, bf16 = (jnp.float32, jnp.bfloat16)
    axes = ("dp", "seq")
    ring = Ring(n_dp, n_seq)
    images, part, _ = image_tokens.shape
    text_part = text_states.shape[1]
    rows = norm1_gain.shape[0]
    length, prompt = (part * n_seq, text_part * n_seq)

    def gather(shard):
        return lax.all_gather(shard, axes, axis=0, tiled=True)

    vectors = [
        norm1_gain, norm1_bias, self_out_bias, norm2_gain, norm2_bias, cross_out_bias,
        norm3_gain, norm3_bias, mlp_out_bias, self_bias_qv, cross_bias_qv, mlp_in_bias,
    ]
    strip = jnp.concatenate([v.reshape(-1, rows) for v in vectors], axis=0).T
    strip = jnp.pad(strip, ((0, 0), (0, 128 - strip.shape[1])))
    moved = lax.all_to_all(
        jnp.concatenate([image_tokens, text_states], axis=1), "seq", 0, 0, tiled=True
    )
    first = gather(jnp.concatenate([self_qkv, strip], axis=1))
    second = gather(jnp.concatenate([self_out, cross_query, cross_kv, cross_out], axis=1))
    w_in, w_out = (gather(mlp_in), gather(mlp_out))
    grad_rows = lax.all_to_all(out_grad, "seq", 0, 0, tiled=True).reshape(length, D)

    table = first[:, 3 * D :].T.astype(f32)
    full, at = ([], 0)
    for v in vectors:
        wide = v.shape[0] // rows
        full.append(
            table[at : at + wide].reshape(wide, -1, rows).transpose(1, 0, 2).reshape(-1)
        )
        at += wide
    (g1, b1, bias_out, g2, b2, bias_cross, g3, b3, bias_last, bias_qv, bias_qv2, bias_in) = full
    w_qkv = first[:, : 3 * D]
    w_self, w_query, w_kv, w_cross = (
        second[:, :D],
        second[:, D : 2 * D],
        second[:, 2 * D : 4 * D],
        second[:, 4 * D :],
    )

    tokens = moved[:, :part].reshape(length, D)
    texts = moved[:, part:].reshape(prompt, D)
    prompt_length = lax.dynamic_slice_in_dim(text_lengths, ring.seq, 1, 0)

    residual = tokens.astype(f32)
    h1, n1, r1 = norm_rows(residual, g1, b1)
    scale = jnp.concatenate([jnp.full((D,), SCALING * LOG2E, f32), jnp.ones((2 * D,), f32)])
    shift = jnp.concatenate([bias_qv[:D], jnp.zeros((D,), f32), bias_qv[D:]])
    qkv = ((mm(h1, w_qkv) + shift) * scale).astype(bf16)
    o1, lse1 = flash(prompt_length, qkv, qkv, qkv, (0, 8, 16), True)
    x1 = residual + mm(o1, w_self) + bias_out
    h2, n2, r2 = norm_rows(x1, g2, b2)
    q2 = ((mm(h2, w_query) + bias_qv2[:D]) * (SCALING * LOG2E)).astype(bf16)
    shift2 = jnp.concatenate([jnp.zeros((D,), f32), bias_qv2[D:]])
    kv2 = (mm(texts, w_kv) + shift2).astype(bf16)
    o2, lse2 = flash(prompt_length, q2, kv2, kv2, (0, 0, 8), False)
    x2 = x1 + mm(o2, w_cross) + bias_cross
    h3, n3, r3 = norm_rows(x2, g3, b3)
    act, slope = gelu_pair(mm(h3, w_in) + bias_in)
    act, slope = (act.astype(bf16), slope.astype(bf16))
    out = (x2 + mm(act, w_out) + bias_last).astype(bf16)
    block_output = lax.all_to_all(out.reshape(n_seq, part, D), "seq", 0, 0, tiled=True)

    w_out_grad = mm(act, grad_rows, TN)
    du = (mm(grad_rows, w_out, NT) * slope.astype(f32)).astype(bf16)
    (mlp_out_grad,) = ring.spread_sum([w_out_grad])
    (mlp_in_grad,) = ring.spread_sum([mm(h3, du, TN)])
    top = grad_rows.astype(f32)
    back3, g3_grad, b3_grad = norm_rows_back(mm(du, w_in, NT), n3, r3, g3)
    dx2 = top + back3
    dc = dx2.astype(bf16)
    do2 = mm(dc, w_cross, NT).astype(bf16)
    dq2, dk2, dv2 = flash_back(prompt_length, q2, kv2, kv2, (0, 0, 8), o2, do2, lse2, False)
    dkv2 = jnp.concatenate([dk2, dv2], axis=1)
    text_grad = mm(dkv2, w_kv, NT)
    back2, g2_grad, b2_grad = norm_rows_back(mm(dq2, w_query, NT), n2, r2, g2)
    dx1 = dx2 + back2
    da = dx1.astype(bf16)
    do1 = mm(da, w_self, NT).astype(bf16)
    cross_out_grad, cross_query_grad, cross_kv_grad, self_out_grad = ring.spread_sum(
        [mm(o2, dc, TN), mm(h2, dq2, TN), mm(texts, dkv2, TN), mm(o1, da, TN)]
    )
    dq1, dk1, dv1 = flash_back(prompt_length, qkv, qkv, qkv, (0, 8, 16), o1, do1, lse1, True)
    dqkv = jnp.concatenate([dq1, dk1, dv1], axis=1)
    (self_qkv_grad,) = ring.spread_sum([mm(h1, dqkv, TN)])
    back1, g1_grad, b1_grad = norm_rows_back(mm(dqkv, w_qkv, NT), n1, r1, g1)
    image_grad = (dx1 + back1).astype(bf16)
    leaving = jnp.concatenate(
        [image_grad.reshape(n_seq, part, D), text_grad.astype(bf16).reshape(n_seq, text_part, D)],
        axis=1,
    )
    leaving = lax.all_to_all(leaving, "seq", 0, 0, tiled=True).astype(f32)

    def columns(array):
        return jnp.sum(array.astype(f32), axis=0)

    small = [
        g1_grad, b1_grad, columns(da), g2_grad, b2_grad, columns(dc), g3_grad, b3_grad,
        columns(grad_rows), jnp.concatenate([columns(dq1), columns(dv1)]),
        jnp.concatenate([columns(dq2), columns(dv2)]), columns(du),
    ]
    sums = lax.psum(jnp.concatenate(small), axes)
    mine, at = ([], 0)
    for v in small:
        wide = v.shape[0] // ring.count
        mine.append(lax.dynamic_slice_in_dim(sums, at + ring.index * wide, wide, 0))
        at += v.shape[0]
    return (
        block_output,
        leaving[:, :part],
        leaving[:, part:],
        mine[0],
        mine[1],
        self_qkv_grad,
        mine[9],
        self_out_grad,
        mine[2],
        mine[3],
        mine[4],
        cross_query_grad,
        cross_kv_grad,
        mine[10],
        cross_out_grad,
        mine[5],
        mine[6],
        mine[7],
        mlp_in_grad,
        mine[11],
        mlp_out_grad,
        mine[8],
    )


def plan_of(mesh):
    n_dp, n_seq = (mesh.shape["dp"], mesh.shape["seq"])

    def layer(*args):
        images = args[0].shape[0]
        if images == n_seq and (n_dp, n_seq) == (8, 4):
            return whole_images(n_dp, n_seq, *args)
        return per_device(*args)

    return layer


def solution(mesh):
    placed = (
        P("dp", "seq", None),
        P("dp", "seq", None),
        P("dp"),
        P("dp", "seq", None),
        P(("dp", "seq")),
        P(("dp", "seq")),
        P(("dp", "seq"), None),
        P(("dp", "seq")),
        P(("dp", "seq"), None),
        P(("dp", "seq")),
        P(("dp", "seq")),
        P(("dp", "seq")),
        P(("dp", "seq"), None),
        P(("dp", "seq"), None),
        P(("dp", "seq")),
        P(("dp", "seq"), None),
        P(("dp", "seq")),
        P(("dp", "seq")),
        P(("dp", "seq")),
        P(("dp", "seq"), None),
        P(("dp", "seq")),
        P(("dp", "seq"), None),
        P(("dp", "seq")),
    )
    return jax.shard_map(
        plan_of(mesh),
        mesh=mesh,
        in_specs=placed,
        out_specs=(
            P("dp", "seq", None),
            P("dp", "seq", None),
            P("dp", "seq", None),
            P(("dp", "seq")),
            P(("dp", "seq")),
            P(("dp", "seq"), None),
            P(("dp", "seq")),
            P(("dp", "seq"), None),
            P(("dp", "seq")),
            P(("dp", "seq")),
            P(("dp", "seq")),
            P(("dp", "seq"), None),
            P(("dp", "seq"), None),
            P(("dp", "seq")),
            P(("dp", "seq"), None),
            P(("dp", "seq")),
            P(("dp", "seq")),
            P(("dp", "seq")),
            P(("dp", "seq"), None),
            P(("dp", "seq")),
            P(("dp", "seq"), None),
            P(("dp", "seq")),
        ),
        check_vma=False,
    )
```

```python
import functools
import itertools

import jax
import jax.numpy as jnp
from jax import lax
from jax.experimental import pallas as pl
from jax.experimental.pallas import tpu as pltpu
from jax.sharding import Mesh
from jax.sharding import PartitionSpec as P

D = 1024
HEADS = 16
HEAD_DIM = 64


EPSILON = 1e-05
SCALING = 0.125
NEGATIVE = -1e30
VMEM = 56 * 1024 * 1024


def layer_norm(values, gain, shift):
    center = values - jnp.mean(values, axis=-1, keepdims=True)
    inverse = lax.rsqrt(jnp.mean(center * center, axis=-1, keepdims=True) + EPSILON)
    normed = center * inverse
    return (normed * gain + shift, normed, inverse)


def norm_back(grad_rows, normed, inverse, gain):
    scaled = grad_rows * gain
    back = inverse * (
        scaled
        - jnp.mean(scaled, axis=-1, keepdims=True)
        - normed * jnp.mean(scaled * normed, axis=-1, keepdims=True)
    )
    return (back, jnp.sum(grad_rows * normed, axis=(0, 1)), jnp.sum(grad_rows, axis=(0, 1)))


def project(left, weight):
    return jnp.einsum("bld,de->ble", left, weight, preferred_element_type=jnp.float32)


def project_back(grad_rows, weight):
    return jnp.einsum("ble,de->bld", grad_rows, weight, preferred_element_type=jnp.float32)


def weight_grad(left, grad_rows):
    return jnp.einsum("bld,ble->de", left, grad_rows, preferred_element_type=jnp.float32)


def column_sums(grad_rows):
    return jnp.sum(grad_rows.astype(jnp.float32), axis=(0, 1))


def split_heads(rows):
    return rows.reshape(rows.shape[0], rows.shape[1], HEADS, HEAD_DIM)


def gelu_tanh(values):
    return jax.nn.gelu(values, approximate=True)


def block_scores(queries, key_rows, start, width, mask_at):
    key_block = split_heads(lax.dynamic_slice_in_dim(key_rows, start, width, 1))
    scores = (
        jnp.einsum("bqhd,bkhd->bhqk", queries, key_block, preferred_element_type=jnp.float32)
        * SCALING
    )
    return (jnp.where(mask_at(start, width), scores, NEGATIVE), key_block)


def spread_attend(query_rows, key_rows, value_rows, mask_at, width):
    queries = split_heads(query_rows)
    batch_size, length = (query_rows.shape[0], query_rows.shape[1])
    blocks = key_rows.shape[1] // width

    def stats(block_index, carry):
        running_max, running_sum = carry
        scores, key_block = block_scores(queries, key_rows, block_index * width, width, mask_at)
        new_max = jnp.maximum(running_max, jnp.max(scores, axis=-1))
        running_sum = running_sum * jnp.exp(running_max - new_max) + jnp.sum(
            jnp.exp(scores - new_max[..., None]), axis=-1
        )
        return (new_max, running_sum)

    start_max = jnp.full((batch_size, HEADS, length), NEGATIVE, jnp.float32)
    final_max, final_sum = lax.fori_loop(0, blocks, stats, (start_max, jnp.zeros_like(start_max)))
    log_total = final_max + jnp.log(final_sum)

    def accumulate(block_index, total):
        start = block_index * width
        scores, key_block = block_scores(queries, key_rows, start, width, mask_at)
        weights = jnp.exp(scores - log_total[..., None]).astype(jnp.bfloat16)
        value_block = split_heads(lax.dynamic_slice_in_dim(value_rows, start, width, 1))
        return total + jnp.einsum(
            "bhqk,bkhd->bqhd", weights, value_block, preferred_element_type=jnp.float32
        )

    total = lax.fori_loop(
        0, blocks, accumulate, jnp.zeros((batch_size, length, HEADS, HEAD_DIM), jnp.float32)
    )
    return (total.reshape(batch_size, length, HEADS * HEAD_DIM).astype(jnp.bfloat16), log_total)


def spread_attend_back(query_rows, key_rows, value_rows, grad_rows, log_total, mask_at, width):
    queries = split_heads(query_rows)
    grad_heads = split_heads(grad_rows)
    batch_size, length = (query_rows.shape[0], query_rows.shape[1])
    blocks = key_rows.shape[1] // width

    def weights_at(start):
        scores, key_block = block_scores(queries, key_rows, start, width, mask_at)
        value_block = split_heads(lax.dynamic_slice_in_dim(value_rows, start, width, 1))
        probs = jnp.exp(scores - log_total[..., None])
        grad_probs = jnp.einsum(
            "bqhd,bkhd->bhqk", grad_heads, value_block, preferred_element_type=jnp.float32
        )
        return (probs, grad_probs, key_block)

    def inner(block_index, delta):
        probs, grad_probs, key_block = weights_at(block_index * width)
        return delta + jnp.sum(probs * grad_probs, axis=-1)

    delta = lax.fori_loop(0, blocks, inner, jnp.zeros((batch_size, HEADS, length), jnp.float32))
    start_grad = jnp.zeros((batch_size, length, HEADS, HEAD_DIM), jnp.float32)

    def step(grad_queries, block_index):
        probs, grad_probs, key_block = weights_at(block_index * width)
        grad_scores = (probs * (grad_probs - delta[..., None])).astype(jnp.bfloat16)
        grad_queries = grad_queries + jnp.einsum(
            "bhqk,bkhd->bqhd", grad_scores, key_block, preferred_element_type=jnp.float32
        )
        grad_keys = jnp.einsum(
            "bhqk,bqhd->bkhd", grad_scores, queries, preferred_element_type=jnp.float32
        )
        grad_values = jnp.einsum(
            "bhqk,bqhd->bkhd",
            probs.astype(jnp.bfloat16),
            grad_heads,
            preferred_element_type=jnp.float32,
        )
        return (grad_queries, (grad_keys, grad_values))

    grad_queries, (key_parts, value_parts) = lax.scan(
        step, start_grad, jnp.arange(blocks, dtype=jnp.int32)
    )

    def merge_blocks(parts):
        return jnp.moveaxis(parts, 0, 1).reshape(batch_size, blocks * width, HEADS * HEAD_DIM)

    return (
        (grad_queries * SCALING).reshape(batch_size, length, HEADS * HEAD_DIM),
        merge_blocks(key_parts) * SCALING,
        merge_blocks(value_parts),
        delta,
    )


def gather_self(gain, shift, weight_qkv, bias_qv, weight_out, bias_out):
    return (
        lax.all_gather(gain, ("dp", "seq"), axis=0, tiled=True),
        lax.all_gather(shift, ("dp", "seq"), axis=0, tiled=True),
        lax.all_gather(weight_qkv, ("dp", "seq"), axis=0, tiled=True),
        lax.all_gather(bias_qv, ("dp", "seq"), axis=0, tiled=True),
        lax.all_gather(weight_out, ("dp", "seq"), axis=0, tiled=True),
        lax.all_gather(bias_out, ("dp", "seq"), axis=0, tiled=True),
    )


def gather_cross(gain, shift, weight_query, weight_kv, bias_qv, weight_out, bias_out):
    return (
        lax.all_gather(gain, ("dp", "seq"), axis=0, tiled=True),
        lax.all_gather(shift, ("dp", "seq"), axis=0, tiled=True),
        lax.all_gather(weight_query, ("dp", "seq"), axis=0, tiled=True),
        lax.all_gather(weight_kv, ("dp", "seq"), axis=0, tiled=True),
        lax.all_gather(bias_qv, ("dp", "seq"), axis=0, tiled=True),
        lax.all_gather(weight_out, ("dp", "seq"), axis=0, tiled=True),
        lax.all_gather(bias_out, ("dp", "seq"), axis=0, tiled=True),
    )


def gather_mlp(gain, shift, weight_in, bias_in, weight_out, bias_out):
    return (
        lax.all_gather(gain, ("dp", "seq"), axis=0, tiled=True),
        lax.all_gather(shift, ("dp", "seq"), axis=0, tiled=True),
        lax.all_gather(weight_in, ("dp", "seq"), axis=0, tiled=True),
        lax.all_gather(bias_in, ("dp", "seq"), axis=0, tiled=True),
        lax.all_gather(weight_out, ("dp", "seq"), axis=0, tiled=True),
        lax.all_gather(bias_out, ("dp", "seq"), axis=0, tiled=True),
    )


def per_device(
    image_tokens,
    text_states,
    text_lengths,
    out_grad,
    norm1_gain,
    norm1_bias,
    self_qkv,
    self_bias_qv,
    self_out,
    self_out_bias,
    norm2_gain,
    norm2_bias,
    cross_query,
    cross_kv,
    cross_bias_qv,
    cross_out,
    cross_out_bias,
    norm3_gain,
    norm3_bias,
    mlp_in,
    mlp_in_bias,
    mlp_out,
    mlp_out_bias,
):
    length = image_tokens.shape[1]
    own_start = lax.axis_index("seq") * length
    query_pos = own_start + jnp.arange(length, dtype=jnp.int32)

    def causal_at(start, width):
        key_pos = start + jnp.arange(width, dtype=jnp.int32)
        return (key_pos[None, :] <= query_pos[:, None])[None, None]

    def padded_at(start, width):
        key_pos = start + jnp.arange(width, dtype=jnp.int32)
        return (key_pos[None, :] < text_lengths[:, None])[:, None, None, :]

    self_full = gather_self(norm1_gain, norm1_bias, self_qkv, self_bias_qv, self_out, self_out_bias)
    residual = image_tokens.astype(jnp.float32)
    normed_in, normed_one, inverse_one = layer_norm(
        residual, self_full[0].astype(jnp.float32), self_full[1].astype(jnp.float32)
    )
    hidden_one = normed_in.astype(jnp.bfloat16)
    mixed = project(hidden_one, self_full[2])
    bias_self = self_full[3].astype(jnp.float32)
    query_one = (mixed[..., :D] + bias_self[:D]).astype(jnp.bfloat16)
    key_one = mixed[..., D : 2 * D].astype(jnp.bfloat16)
    value_one = (mixed[..., 2 * D :] + bias_self[D:]).astype(jnp.bfloat16)
    key_all, value_all = (
        lax.all_gather(key_one, "seq", axis=1, tiled=True),
        lax.all_gather(value_one, "seq", axis=1, tiled=True),
    )
    self_width = min(128, key_all.shape[1])
    attended, log_one = spread_attend(query_one, key_all, value_all, causal_at, self_width)
    after_self = residual + project(attended, self_full[4]) + self_full[5].astype(jnp.float32)
    cross_full = gather_cross(
        norm2_gain, norm2_bias, cross_query, cross_kv, cross_bias_qv, cross_out, cross_out_bias
    )
    normed_mid, normed_two, inverse_two = layer_norm(
        after_self, cross_full[0].astype(jnp.float32), cross_full[1].astype(jnp.float32)
    )
    hidden_two = normed_mid.astype(jnp.bfloat16)
    bias_cross = cross_full[4].astype(jnp.float32)
    query_two = (project(hidden_two, cross_full[2]) + bias_cross[:D]).astype(jnp.bfloat16)
    text_mixed = project(text_states, cross_full[3])
    text_key = text_mixed[..., :D].astype(jnp.bfloat16)
    text_value = (text_mixed[..., D:] + bias_cross[D:]).astype(jnp.bfloat16)
    key_two, value_two = (
        lax.all_gather(text_key, "seq", axis=1, tiled=True),
        lax.all_gather(text_value, "seq", axis=1, tiled=True),
    )
    text_width = key_two.shape[1]
    attended_two, log_two = spread_attend(query_two, key_two, value_two, padded_at, text_width)
    after_cross = (
        after_self + project(attended_two, cross_full[5]) + cross_full[6].astype(jnp.float32)
    )
    mlp_full = gather_mlp(norm3_gain, norm3_bias, mlp_in, mlp_in_bias, mlp_out, mlp_out_bias)
    normed_last, normed_three, inverse_three = layer_norm(
        after_cross, mlp_full[0].astype(jnp.float32), mlp_full[1].astype(jnp.float32)
    )
    hidden_three = normed_last.astype(jnp.bfloat16)
    pre_act = project(hidden_three, mlp_full[2]) + mlp_full[3].astype(jnp.float32)
    activated, gelu_back = jax.vjp(gelu_tanh, pre_act)
    act_low = activated.astype(jnp.bfloat16)
    block_output = (
        after_cross + project(act_low, mlp_full[4]) + mlp_full[5].astype(jnp.float32)
    ).astype(jnp.bfloat16)
    mlp_back = gather_mlp(norm3_gain, norm3_bias, mlp_in, mlp_in_bias, mlp_out, mlp_out_bias)
    grad_top = out_grad.astype(jnp.float32)
    w_out_grad = weight_grad(act_low, out_grad)
    b_out_grad = column_sums(out_grad)
    grad_act = project_back(out_grad, mlp_back[4])
    grad_pre = gelu_back(grad_act)[0].astype(jnp.bfloat16)
    w_in_grad = weight_grad(hidden_three, grad_pre)
    b_in_grad = column_sums(grad_pre)
    back_three, gain_three_grad, shift_three_grad = norm_back(
        project_back(grad_pre, mlp_back[2]),
        normed_three,
        inverse_three,
        mlp_back[0].astype(jnp.float32),
    )
    grad_two = grad_top + back_three
    mlp_grads = (
        lax.psum_scatter(gain_three_grad, ("dp", "seq"), scatter_dimension=0, tiled=True),
        lax.psum_scatter(shift_three_grad, ("dp", "seq"), scatter_dimension=0, tiled=True),
        lax.psum_scatter(w_in_grad, ("dp", "seq"), scatter_dimension=0, tiled=True),
        lax.psum_scatter(b_in_grad, ("dp", "seq"), scatter_dimension=0, tiled=True),
        lax.psum_scatter(w_out_grad, ("dp", "seq"), scatter_dimension=0, tiled=True),
        lax.psum_scatter(b_out_grad, ("dp", "seq"), scatter_dimension=0, tiled=True),
    )
    cross_back = gather_cross(
        norm2_gain, norm2_bias, cross_query, cross_kv, cross_bias_qv, cross_out, cross_out_bias
    )
    grad_cross = grad_two.astype(jnp.bfloat16)
    cross_out_term = weight_grad(attended_two, grad_cross)
    cross_bias_term = column_sums(grad_cross)
    grad_att_two = project_back(grad_cross, cross_back[5]).astype(jnp.bfloat16)
    grad_query_two, grad_key_two, grad_value_two, delta_two = spread_attend_back(
        query_two, key_two, value_two, grad_att_two, log_two, padded_at, text_width
    )
    query_two_low = grad_query_two.astype(jnp.bfloat16)
    text_key_grad, text_value_grad = (
        lax.psum_scatter(
            grad_key_two.astype(jnp.bfloat16), "seq", scatter_dimension=1, tiled=True
        ).astype(jnp.float32),
        lax.psum_scatter(
            grad_value_two.astype(jnp.bfloat16), "seq", scatter_dimension=1, tiled=True
        ).astype(jnp.float32),
    )
    text_value_low = text_value_grad.astype(jnp.bfloat16)
    text_kv_grad = jnp.concatenate([text_key_grad.astype(jnp.bfloat16), text_value_low], axis=-1)
    cross_query_term = weight_grad(hidden_two, query_two_low)
    cross_kv_term = weight_grad(text_states, text_kv_grad)
    cross_qv_term = jnp.concatenate([column_sums(query_two_low), column_sums(text_value_low)])
    text_grad = project_back(text_kv_grad, cross_back[3])
    back_two, gain_two_grad, shift_two_grad = norm_back(
        project_back(query_two_low, cross_back[2]),
        normed_two,
        inverse_two,
        cross_back[0].astype(jnp.float32),
    )
    grad_one = grad_two + back_two
    cross_grads = (
        lax.psum_scatter(gain_two_grad, ("dp", "seq"), scatter_dimension=0, tiled=True),
        lax.psum_scatter(shift_two_grad, ("dp", "seq"), scatter_dimension=0, tiled=True),
        lax.psum_scatter(cross_query_term, ("dp", "seq"), scatter_dimension=0, tiled=True),
        lax.psum_scatter(cross_kv_term, ("dp", "seq"), scatter_dimension=0, tiled=True),
        lax.psum_scatter(cross_qv_term, ("dp", "seq"), scatter_dimension=0, tiled=True),
        lax.psum_scatter(cross_out_term, ("dp", "seq"), scatter_dimension=0, tiled=True),
        lax.psum_scatter(cross_bias_term, ("dp", "seq"), scatter_dimension=0, tiled=True),
    )
    self_back = gather_self(norm1_gain, norm1_bias, self_qkv, self_bias_qv, self_out, self_out_bias)
    grad_self = grad_one.astype(jnp.bfloat16)
    self_out_term = weight_grad(attended, grad_self)
    self_bias_term = column_sums(grad_self)
    grad_att_one = project_back(grad_self, self_back[4]).astype(jnp.bfloat16)
    grad_query_one, grad_key_all, grad_value_all, delta_one = spread_attend_back(
        query_one, key_all, value_all, grad_att_one, log_one, causal_at, self_width
    )
    grad_key_one, grad_value_one = (
        lax.psum_scatter(
            grad_key_all.astype(jnp.bfloat16), "seq", scatter_dimension=1, tiled=True
        ).astype(jnp.float32),
        lax.psum_scatter(
            grad_value_all.astype(jnp.bfloat16), "seq", scatter_dimension=1, tiled=True
        ).astype(jnp.float32),
    )
    query_one_low = grad_query_one.astype(jnp.bfloat16)
    value_one_low = grad_value_one.astype(jnp.bfloat16)
    grad_qkv = jnp.concatenate(
        [query_one_low, grad_key_one.astype(jnp.bfloat16), value_one_low], axis=-1
    )
    self_qkv_term = weight_grad(hidden_one, grad_qkv)
    self_qv_term = jnp.concatenate([column_sums(query_one_low), column_sums(value_one_low)])
    back_one, gain_one_grad, shift_one_grad = norm_back(
        project_back(grad_qkv, self_back[2]),
        normed_one,
        inverse_one,
        self_back[0].astype(jnp.float32),
    )
    image_grad = grad_one + back_one
    self_grads = (
        lax.psum_scatter(gain_one_grad, ("dp", "seq"), scatter_dimension=0, tiled=True),
        lax.psum_scatter(shift_one_grad, ("dp", "seq"), scatter_dimension=0, tiled=True),
        lax.psum_scatter(self_qkv_term, ("dp", "seq"), scatter_dimension=0, tiled=True),
        lax.psum_scatter(self_qv_term, ("dp", "seq"), scatter_dimension=0, tiled=True),
        lax.psum_scatter(self_out_term, ("dp", "seq"), scatter_dimension=0, tiled=True),
        lax.psum_scatter(self_bias_term, ("dp", "seq"), scatter_dimension=0, tiled=True),
    )
    return (
        block_output,
        image_grad,
        text_grad,
        self_grads[0],
        self_grads[1],
        self_grads[2],
        self_grads[3],
        self_grads[4],
        self_grads[5],
        cross_grads[0],
        cross_grads[1],
        cross_grads[2],
        cross_grads[3],
        cross_grads[4],
        cross_grads[5],
        cross_grads[6],
        mlp_grads[0],
        mlp_grads[1],
        mlp_grads[2],
        mlp_grads[3],
        mlp_grads[4],
        mlp_grads[5],
    )


LOG2E = 1.4426950408889634
LN2 = 0.6931471805599453
QB = 256
PAIR = 2 * HEAD_DIM
NT = (((1,), (1,)), ((), ()))
NN = (((1,), (0,)), ((), ()))
TN = (((0,), (0,)), ((), ()))
BF16 = jnp.bfloat16
F32 = jnp.float32


def mm(left, right, dims=NN):
    return lax.dot_general(left, right, dims, preferred_element_type=F32)


def head_lanes(rows, head):
    lane = lax.broadcasted_iota(jnp.int32, rows.shape, 1)
    keep = (lane < HEAD_DIM) if head == 0 else (lane >= HEAD_DIM)
    return jnp.where(keep, rows, jnp.zeros_like(rows))


def whole(shape, index=None, single=True):
    where = index or (0,) * len(shape)
    mode = {"pipeline_mode": pl.Buffered(1)} if single else {}
    return pl.BlockSpec(shape, lambda *_: where, **mode)


def kernel_call(body, name, grid, ins, outs, shapes, args, scratch=(), flops=0, prefetch=0, moved=0, exps=0):
    return pl.pallas_call(
        body,
        grid_spec=pltpu.PrefetchScalarGridSpec(
            num_scalar_prefetch=prefetch,
            grid=grid,
            in_specs=ins,
            out_specs=outs,
            scratch_shapes=list(scratch),
        ),
        out_shape=[jax.ShapeDtypeStruct(s, d) for s, d in shapes],
        compiler_params=pltpu.CompilerParams(vmem_limit_bytes=VMEM),
        cost_estimate=pl.CostEstimate(flops=flops // 32, bytes_accessed=moved // 32, transcendentals=exps // 32),
        name=name,
    )(*args)


def attend_kernel(q_ref, k_ref, v_ref, o_ref, lse_ref, vx_ref):
    keys = k_ref.shape[0]
    length = q_ref.shape[0]
    block = min(QB, length)
    vx_ref[:, :PAIR] = v_ref[...]
    vx_ref[:, PAIR:] = jnp.ones((keys, PAIR), BF16)
    for start in range(0, length, block):
        limit = start + block
        rows = q_ref[start:limit, :]
        both = []
        for head in range(2):
            scores = mm(head_lanes(rows, head), k_ref[:limit, :], NT)
            last = scores[:, start:]
            col = lax.broadcasted_iota(jnp.int32, last.shape, 1)
            row = lax.broadcasted_iota(jnp.int32, last.shape, 0)
            last = jnp.where(col <= row, last, NEGATIVE)
            if start:
                scores = jnp.concatenate([scores[:, :start], last], axis=1)
            else:
                scores = last
            top = jnp.max(scores, axis=1, keepdims=True)
            weights = jnp.exp2(scores - top).astype(BF16)
            total = mm(weights, vx_ref[:limit, :])
            both.append(total[:, :PAIR] / total[:, PAIR:])
            stat = (top + jnp.log2(total[:, PAIR:])).T
            lse_ref[0, head : head + 1, start:limit] = stat[:1, :]
        lane = lax.broadcasted_iota(jnp.int32, both[0].shape, 1)
        o_ref[start:limit, :] = jnp.where(lane < HEAD_DIM, both[0], both[1]).astype(BF16)


def attend_back_kernel(
    q_ref, k_ref, v_ref, o_ref, do_ref, lse_ref, dq_ref, dk_ref, dv_ref, acc_ref
):
    keys = k_ref.shape[0]
    block = min(QB, keys)
    product = (do_ref[...].astype(F32) * o_ref[...].astype(F32)).T
    acc_ref[...] = jnp.zeros_like(acc_ref)
    delta = [
        jnp.sum(product[head * HEAD_DIM : (head + 1) * HEAD_DIM, :], axis=0, keepdims=True)
        for head in range(2)
    ]
    for start in range(0, keys, block):
        key_rows = k_ref[start : start + block, :]
        value_rows = v_ref[start : start + block, :]
        grad_keys = grad_values = None
        for head in range(2):
            queries = head_lanes(q_ref[start:, :], head)
            grads = head_lanes(do_ref[start:, :], head)
            scores = mm(key_rows, queries, NT)
            probs = jnp.exp2(scores - lse_ref[0, head : head + 1, start:])
            edge = probs[:, :block]
            row = lax.broadcasted_iota(jnp.int32, edge.shape, 0)
            col = lax.broadcasted_iota(jnp.int32, edge.shape, 1)
            edge = jnp.where(row <= col, edge, 0.0)
            if start + block < keys:
                probs = jnp.concatenate([edge, probs[:, block:]], axis=1)
            else:
                probs = edge
            back = mm(value_rows, grads, NT)
            scored = (probs * (back - delta[head][:, start:])).astype(BF16)
            term_v = mm(probs.astype(BF16), grads)
            term_k = mm(scored, queries)
            grad_values = term_v if grad_values is None else grad_values + term_v
            grad_keys = term_k if grad_keys is None else grad_keys + term_k
            acc_ref[start:, :] += mm(scored, head_lanes(key_rows, head), TN)
        dk_ref[start : start + block, :] = (grad_keys * LN2).astype(BF16)
        dv_ref[start : start + block, :] = grad_values.astype(BF16)
    dq_ref[...] = (acc_ref[...] * SCALING).astype(BF16)


def column_pair(rows, offset):
    return pl.BlockSpec((rows, PAIR), lambda i, *_: (0, i + offset))


def attend(qkv):
    length = qkv.shape[0]
    pairs = HEADS // 2
    return kernel_call(
        attend_kernel,
        "attend",
        (pairs,),
        [column_pair(length, pairs * i) for i in range(3)],
        [column_pair(length, 0), pl.BlockSpec((1, 2, length), lambda i, *_: (i, 0, 0))],
        [((length, D), BF16), ((pairs, 2, length), F32)],
        (qkv, qkv, qkv),
        scratch=[pltpu.VMEM((length, 2 * PAIR), BF16)],
        flops=length * length * HEADS * 512,
        moved=8 * length * D,
        exps=length * length * HEADS // 2,
    )


def attend_back(qkv, out, grad, lse, first, count):
    length = qkv.shape[0]
    pairs = HEADS // 2
    return kernel_call(
        attend_back_kernel,
        "attend_back",
        (count,),
        [column_pair(length, pairs * i + first) for i in range(3)]
        + [column_pair(length, first)] * 2
        + [pl.BlockSpec((1, 2, length), lambda i, *_: (i + first, 0, 0))],
        [column_pair(length, 0)] * 3,
        [((length, count * PAIR), BF16)] * 3,
        (qkv, qkv, qkv, out, grad, lse),
        scratch=[pltpu.VMEM((length, PAIR), F32)],
        flops=length * length * count * 2560,
        moved=2 * 8 * length * count * PAIR,
        exps=length * length * count,
    )


def normed_of(rows):
    center = rows - jnp.mean(rows, axis=1, keepdims=True)
    inverse = lax.rsqrt(jnp.mean(center * center, axis=1, keepdims=True) + EPSILON)
    return (center * inverse, inverse)


def norm_input_grad(grads, normed, inverse, gain):
    scaled = grads * gain
    return inverse * (
        scaled
        - jnp.mean(scaled, axis=1, keepdims=True)
        - normed * jnp.mean(scaled * normed, axis=1, keepdims=True)
    )


def sums(rows):
    return jnp.sum(rows, axis=0, keepdims=True)


def add_row(ref, at, value, first):
    @pl.when(first)
    def _():
        ref[at : at + 1, :] = value

    @pl.when(jnp.logical_not(first))
    def _():
        ref[at : at + 1, :] += value


def gelu_pair(values):
    root = 0.7978845608028654
    square = values * values
    bend = jnp.tanh(values * (root + (0.044715 * root) * square))
    half = 0.5 + 0.5 * bend
    slope = half + values * (0.5 - 0.5 * bend * bend) * (root + (0.134145 * root) * square)
    return (values * half, slope)


def qkv_kernel(x_ref, w_ref, vec_ref, h_ref, qkv_ref):
    normed, _ = normed_of(x_ref[...].astype(F32))
    low = (normed * vec_ref[0:1, :] + vec_ref[1:2, :]).astype(BF16)
    h_ref[...] = low
    for part in range(3):
        mixed = mm(low, w_ref[:, part * D : (part + 1) * D]) + vec_ref[2 + part : 3 + part, :]
        if part == 0:
            mixed = mixed * (SCALING * LOG2E)
        qkv_ref[:, part * D : (part + 1) * D] = mixed.astype(BF16)


def pair_keys(kv_ref, at, keys):
    block = kv_ref[:, at : at + PAIR]
    return jnp.concatenate([head_lanes(block, 0), head_lanes(block, 1)], axis=0)


def cross_kernel(
    len_ref, x_ref, o_ref, ws_ref, wq_ref, wc_ref, kv_ref, vec_ref,
    x1_ref, h2_ref, q2_ref, o2_ref, x2_ref, h3_ref, lse_ref,
):
    keys = kv_ref.shape[0]
    after = x_ref[...].astype(F32) + mm(o_ref[...], ws_ref[...]) + vec_ref[0:1, :]
    x1_ref[...] = after
    normed, _ = normed_of(after)
    low = (normed * vec_ref[1:2, :] + vec_ref[2:3, :]).astype(BF16)
    h2_ref[...] = low
    q2_ref[...] = ((mm(low, wq_ref[...]) + vec_ref[3:4, :]) * (SCALING * LOG2E)).astype(BF16)
    ones = jnp.ones((keys, PAIR), BF16)
    for pair in range(HEADS // 2):
        at = pair * PAIR
        scores = mm(q2_ref[:, at : at + PAIR], pair_keys(kv_ref, at, keys), NT)
        col = lax.broadcasted_iota(jnp.int32, (scores.shape[0], keys), 1)
        inside = col < len_ref[0]
        halves, tops = ([], [])
        for head in range(2):
            part = jnp.where(inside, scores[:, head * keys : (head + 1) * keys], NEGATIVE)
            top = jnp.max(part, axis=1, keepdims=True)
            halves.append(jnp.exp2(part - top).astype(BF16))
            tops.append(top)
        values = kv_ref[:, D + at : D + at + PAIR]
        right = jnp.concatenate(
            [
                jnp.concatenate([head_lanes(values, h), head_lanes(ones, h)], axis=1)
                for h in range(2)
            ],
            axis=0,
        )
        total = mm(jnp.concatenate(halves, axis=1), right)
        o2_ref[:, at : at + PAIR] = (total[:, :PAIR] / total[:, PAIR:]).astype(BF16)
        lane = lax.broadcasted_iota(jnp.int32, (scores.shape[0], PAIR), 1)
        stat = (jnp.where(lane < HEAD_DIM, tops[0], tops[1]) + jnp.log2(total[:, PAIR:])).T
        lse_ref[2 * pair : 2 * pair + 1, :] = stat[:1, :]
        lse_ref[2 * pair + 1 : 2 * pair + 2, :] = stat[HEAD_DIM : HEAD_DIM + 1, :]
    after = after + mm(o2_ref[...], wc_ref[...]) + vec_ref[4:5, :]
    x2_ref[...] = after
    normed, _ = normed_of(after)
    h3_ref[...] = (normed * vec_ref[5:6, :] + vec_ref[6:7, :]).astype(BF16)


def mlp_kernel(h_ref, wi_ref, wo_ref, bias_ref, x2_ref, last_ref, act_ref, slope_ref, out_ref, acc_ref):
    step = pl.program_id(0)
    length = h_ref.shape[0]
    for start in range(0, length, QB):
        rows = slice(start, start + QB)
        act, slope = gelu_pair(mm(h_ref[rows, :], wi_ref[...]) + bias_ref[0])
        act = act.astype(BF16)
        act_ref[rows, :] = act
        slope_ref[rows, :] = slope.astype(BF16)
        term = mm(act, wo_ref[...])

        @pl.when(step == 0)
        def _():
            acc_ref[rows, :] = x2_ref[rows, :] + last_ref[...] + term

        @pl.when(step > 0)
        def _():
            acc_ref[rows, :] += term

        @pl.when(step == pl.num_programs(0) - 1)
        def _():
            out_ref[rows, :] = acc_ref[rows, :].astype(BF16)


def du_kernel(g_ref, wo_ref, slope_ref, du_ref, sum_ref):
    length = g_ref.shape[0]
    total = None
    for start in range(0, length, QB):
        rows = slice(start, start + QB)
        grad = mm(g_ref[rows, :], wo_ref[...], NT) * slope_ref[rows, :].astype(F32)
        low = grad.astype(BF16)
        du_ref[rows, :] = low
        part = sums(low.astype(F32))
        total = part if total is None else total + part
    sum_ref[0] = total


def norm3_kernel(du_ref, wi_ref, g_ref, x2_ref, gain_ref, wc_ref, dx_ref, dc_ref, do_ref, vec_ref):
    first = pl.program_id(0) == 0
    grads = None
    for step in range(wi_ref.shape[1] // D):
        cols = slice(step * D, (step + 1) * D)
        term = mm(du_ref[:, cols], wi_ref[:, cols], NT)
        grads = term if grads is None else grads + term
    normed, inverse = normed_of(x2_ref[...])
    out = g_ref[...].astype(F32) + norm_input_grad(grads, normed, inverse, gain_ref[...])
    dx_ref[...] = out
    low = out.astype(BF16)
    dc_ref[...] = low
    do_ref[...] = mm(low, wc_ref[...], NT).astype(BF16)
    add_row(vec_ref, 0, sums(grads * normed), first)
    add_row(vec_ref, 1, sums(grads), first)
    add_row(vec_ref, 2, sums(low.astype(F32)), first)
    add_row(vec_ref, 3, sums(g_ref[...].astype(F32)), first)


def cross_back_kernel(
    len_ref, q_ref, kv_ref, o_ref, do_ref, lse_ref, wq_ref, ws_ref, x1_ref, dx2_ref, gain_ref,
    dq_ref, dkv_ref, dx_ref, da_ref, do1_ref, vec_ref, acc_ref,
):
    step = pl.program_id(0)
    first = step == 0
    keys = kv_ref.shape[0]

    @pl.when(first)
    def _():
        acc_ref[...] = jnp.zeros_like(acc_ref)

    lane = lax.broadcasted_iota(jnp.int32, (keys, PAIR), 1)
    for pair in range(HEADS // 2):
        at = pair * PAIR
        queries = q_ref[:, at : at + PAIR]
        grads = do_ref[:, at : at + PAIR]
        product = (grads.astype(F32) * o_ref[:, at : at + PAIR].astype(F32)).T
        both_keys = pair_keys(kv_ref, at, keys)
        scores = mm(both_keys, queries, NT)
        back = mm(pair_keys(kv_ref, D + at, keys), grads, NT)
        row = lax.broadcasted_iota(jnp.int32, (keys, scores.shape[1]), 0)
        inside = row < len_ref[0]
        probs, scored = ([], [])
        for head in range(2):
            span = slice(head * keys, (head + 1) * keys)
            at_head = 2 * pair + head
            prob = jnp.exp2(scores[span, :] - lse_ref[at_head : at_head + 1, :])
            prob = jnp.where(inside, prob, 0.0)
            delta = sums(product[head * HEAD_DIM : (head + 1) * HEAD_DIM, :])
            probs.append(prob.astype(BF16))
            scored.append((prob * (back[span, :] - delta)).astype(BF16))
        probs, scored = (jnp.concatenate(probs, axis=0), jnp.concatenate(scored, axis=0))
        for base, left, right in ((0, scored, queries), (D, probs, grads)):
            both = mm(left, right)
            acc_ref[:, base + at : base + at + PAIR] += jnp.where(
                lane < HEAD_DIM, both[:keys, :], both[keys:, :]
            )
        dq_ref[:, at : at + PAIR] = (mm(scored, both_keys, TN) * SCALING).astype(BF16)

    @pl.when(step == pl.num_programs(0) - 1)
    def _():
        dkv_ref[:, :D] = (acc_ref[:, :D] * LN2).astype(BF16)
        dkv_ref[:, D:] = acc_ref[:, D:].astype(BF16)

    grads = mm(dq_ref[...], wq_ref[...], NT)
    normed, inverse = normed_of(x1_ref[...])
    out = dx2_ref[...] + norm_input_grad(grads, normed, inverse, gain_ref[...])
    dx_ref[...] = out
    low = out.astype(BF16)
    da_ref[...] = low
    do1_ref[...] = mm(low, ws_ref[...], NT).astype(BF16)
    add_row(vec_ref, 0, sums(grads * normed), first)
    add_row(vec_ref, 1, sums(grads), first)
    add_row(vec_ref, 2, sums(low.astype(F32)), first)
    add_row(vec_ref, 3, sums(dq_ref[...].astype(F32)), first)


def norm1_kernel(*refs):
    *grad_refs, w_ref, x_ref, dx1_ref, gain_ref, out_ref, vec_ref = refs
    first = pl.program_id(0) == 0
    grads, at = (None, 0)
    groups = len(grad_refs) // 3
    rows_q, rows_v = ([], [])
    for group in range(groups):
        for part in range(3):
            ref = grad_refs[3 * group + part]
            wide = ref.shape[1]
            base = part * D + group * wide
            term = mm(ref[...], w_ref[:, base : base + wide], NT)
            grads = term if grads is None else grads + term
        rows_q.append(sums(grad_refs[3 * group][...].astype(F32)))
        rows_v.append(sums(grad_refs[3 * group + 2][...].astype(F32)))
    normed, inverse = normed_of(x_ref[...].astype(F32))
    back = norm_input_grad(grads, normed, inverse, gain_ref[...])
    out_ref[...] = (dx1_ref[...] + back).astype(BF16)
    add_row(vec_ref, 0, sums(grads * normed), first)
    add_row(vec_ref, 1, sums(grads), first)
    add_row(vec_ref, 2, jnp.concatenate(rows_q, axis=1), first)
    add_row(vec_ref, 3, jnp.concatenate(rows_v, axis=1), first)


def weight_grad_kernel(units, count, scattered, place_ref, *refs):
    operands, (sent_ref, kept_ref, acc_ref) = (refs[:count], refs[count:])
    step = pl.program_id(0)
    block = acc_ref.shape[0] // 32
    known = sorted(set(units))
    for left, right in known:
        steps = [t for t, unit in enumerate(units) if unit == (left, right)]
        hit = step == steps[0]
        for t in steps[1:]:
            hit = jnp.logical_or(hit, step == t)

        @pl.when(hit)
        def _():
            acc_ref[...] = mm(operands[left][...], operands[right][...], TN)

    halves = ((sent_ref, 1 - place_ref[1]), (kept_ref, place_ref[1]))
    if not scattered:
        wide = 4 * block
        for z, (ref, core) in itertools.product(range(4), halves):
            row = pl.multiple_of((2 * z + core) * wide, wide)
            ref[z * wide : (z + 1) * wide, :] = acc_ref[pl.ds(row, wide), :].astype(BF16)
        return
    for order, far, near, low in itertools.product(range(2), repeat=4):
        z = place_ref[0] ^ (2 * order + low)
        y, x = (near, far) if order else (far, near)
        inner = (place_ref[2] ^ y) * 2 + (place_ref[3] ^ x)
        at = (((order * 2 + far) * 2 + near) * 2 + low) * block
        for ref, core in halves:
            row = pl.multiple_of(((z * 2 + core) * 4 + inner) * block, block)
            ref[at : at + block, :] = acc_ref[pl.ds(row, block), :].astype(BF16)


def weight_grads(places, operands, specs, units, width, name, scattered=True):
    steps = len(units)
    tokens = operands[0].shape[0]
    return kernel_call(
        functools.partial(weight_grad_kernel, tuple(units), len(operands), scattered),
        name,
        (steps,),
        specs,
        [pl.BlockSpec((D // 2, width), lambda t, *_: (0, t))] * 2,
        [((D // 2, steps * width), BF16)] * 2,
        (places, *operands),
        scratch=[pltpu.VMEM((D, width), F32)],
        flops=2 * tokens * D * width * steps,
        moved=2 * D * width * steps + 2 * tokens * D,
        prefetch=1,
    )


def place_kernel(per, place_ref, *refs):
    pieces, out_ref = (refs[:8], refs[8])
    for index, piece in enumerate(pieces):
        far_core, far_side, second = (index // 4, index % 2, (index // 2) % 2)
        for near in range(2):
            for low in range(2):
                z = 2 * second + low
                y, x = (near, far_side) if second else (far_side, near)
                row = (place_ref[0] ^ z) * 2 + (place_ref[1] ^ far_core)
                row = (row * 2 + (place_ref[2] ^ y)) * 2 + (place_ref[3] ^ x)
                row = pl.multiple_of(row * per, per)
                out_ref[pl.ds(row, per), :] = piece[near, low]


def put_in_order(places, pieces):
    near, low, per, width = pieces[0].shape
    wide = width // 5
    (out,) = kernel_call(
        functools.partial(place_kernel, per),
        "put_in_order",
        (5,),
        [pl.BlockSpec((near, low, per, wide), lambda t, *_: (0, 0, 0, t))] * 8,
        [pl.BlockSpec((per * 32, wide), lambda t, *_: (0, t))],
        [((per * 32, width), BF16)],
        (places, *pieces),
        moved=4 * per * 32 * width,
        prefetch=1,
    )
    return out


def total_of(*terms):
    total = terms[0].astype(F32)
    for term in terms[1:]:
        total = total + term.astype(F32)
    return total


AXES = ("z", "core", "seq")


class Ring:
    def __init__(self, mesh):
        self.count = mesh.size
        self.seq, self.z, self.c = (lax.axis_index(a) for a in ("seq", "z", "core"))
        self.x, self.y = (self.seq % 2, self.seq // 2)

    def swap(self, array, bits):
        return lax.ppermute(array, AXES, [(i, i ^ bits) for i in range(self.count)])


class Gather:
    def __init__(self, ring, shard):
        self.ring = ring
        self.hold = [shard] * 3
        self.own = shard
        self.bits = (8, 16, 24)

    def launch(self):
        self.hold = [self.ring.swap(array, bits) for array, bits in zip(self.hold, self.bits)]

    def near(self):
        self.pair = [jnp.stack([self.own, self.hold[0]]), jnp.stack(self.hold[1:])]
        self.hold, self.bits = (list(self.pair), (1, 2))

    def far(self):
        self.pair = [jnp.stack([mine, came]) for mine, came in zip(self.pair, self.hold)]
        self.hold, self.bits = (list(self.pair), (2, 1))

    def core(self):
        self.quad = [self.pair[0], self.hold[0], self.pair[1], self.hold[1]]
        self.hold, self.bits = (list(self.quad), (4,) * 4)

    def done(self, places):
        return put_in_order(places, self.quad + self.hold)


class Steps:
    def __init__(self, ring, halves):
        self.ring = ring
        shape = (2, 2, 2, 2, halves[0].shape[0] // 16, halves[0].shape[1])
        sent, self.kept = (half.reshape(shape) for half in halves)
        self.hold, self.bits = ([sent], (4,))

    def launch(self):
        self.hold = [self.ring.swap(array, bits) for array, bits in zip(self.hold, self.bits)]

    def near(self):
        (self.got,) = self.hold
        self.bits = (2, 1)
        self.hold = [total_of(self.kept[i, 1], self.got[i, 1]).astype(BF16) for i in range(2)]

    def far(self):
        parts = [(self.kept[i, 0], self.got[i, 0], self.hold[i]) for i in range(2)]
        self.bits = (1, 2)
        self.hold = [total_of(*(p[1] for p in parts[i])).astype(BF16) for i in range(2)]
        self.parts = [total_of(*(p[0] for p in parts[i])).astype(BF16) for i in range(2)]

    def deep(self):
        parts = [(self.parts[i], self.hold[i]) for i in range(2)]
        self.result = total_of(*(p[0] for p in parts[0]))
        self.bits = (8, 16, 24)
        self.hold = [
            total_of(*(p[step % 2] for p in parts[step // 2])).astype(BF16) for step in (1, 2, 3)
        ]

    def scatter(self):
        parts = [total_of(self.parts[i], self.hold[i]).astype(BF16) for i in range(2)]
        self.hold = [jnp.concatenate(parts).reshape(-1, self.kept.shape[-1])]

    def launch_scatter(self):
        self.result = lax.psum_scatter(self.hold[0], "z", scatter_dimension=0, tiled=True)
        self.hold = []

    def done(self):
        return total_of(self.result, *self.hold)


def at_once(*groups):
    arrays = [group if isinstance(group, list) else group.hold for group in groups]
    arrays = lax.optimization_barrier(arrays)
    for group, values in zip(groups, arrays):
        if isinstance(group, list):
            group[:] = values
        else:
            group.hold = list(values)


def whole_images(mesh, *args):
    (
        image_tokens, text_states, text_lengths, out_grad, norm1_gain, norm1_bias, self_qkv,
        self_bias_qv, self_out, self_out_bias, norm2_gain, norm2_bias, cross_query, cross_kv,
        cross_bias_qv, cross_out, cross_out_bias, norm3_gain, norm3_bias, mlp_in, mlp_in_bias,
        mlp_out, mlp_out_bias,
    ) = args
    n_seq = mesh.shape["seq"]
    ring = Ring(mesh)
    part, text_part = (image_tokens.shape[1], text_states.shape[1])
    rows = norm1_gain.shape[0]
    fours = mlp_out.shape[0] // rows
    length, prompt = (part * n_seq, text_part * n_seq)
    places = jnp.stack([ring.z, ring.c, ring.y, ring.x]).astype(jnp.int32)
    flat_places = places * jnp.array([0, 1, 1, 1], jnp.int32)

    def gather(shard):
        return lax.all_gather(shard, AXES, axis=0, tiled=True)

    def across(vectors):
        return jnp.concatenate([v.reshape(ring.count, -1) for v in vectors], axis=1)

    def line(*vectors):
        table = jnp.stack(vectors)
        return jnp.pad(table, ((0, -len(vectors) % 8), (0, 0)))

    in_shard = mlp_in.reshape(rows, ring.count, fours, rows).transpose(0, 2, 1, 3).reshape(rows, -1)
    out_shard = mlp_out.reshape(fours, rows, D).transpose(1, 0, 2).reshape(rows, -1)
    mlp = gather(jnp.concatenate([in_shard, out_shard], axis=1))
    vectors = [
        norm1_gain, norm1_bias, self_out_bias, norm2_gain, norm2_bias, cross_out_bias,
        norm3_gain, norm3_bias, mlp_out_bias, self_bias_qv, cross_bias_qv, mlp_in_bias,
    ]
    strip = jnp.concatenate(vectors).reshape(-1, rows)
    strip = jnp.pad(strip, ((0, 128 - strip.shape[0]), (0, 0))).T
    w_first = Gather(ring, jnp.concatenate([self_qkv, strip], axis=1))
    w_second = Gather(
        ring, jnp.concatenate([self_out, cross_query, cross_kv, cross_out], axis=1)
    )
    w_first.launch()
    now = [
        lax.all_to_all(
            jnp.concatenate([image_tokens, text_states], axis=1), "seq", 0, 0, tiled=True
        )
    ]
    at_once(now, w_first)
    (moved,) = now
    w_first.near()
    at_once(w_first, w_second)
    w_first.launch()
    w_second.launch()
    at_once(w_first)
    w_first.far()
    w_first.launch()
    at_once(w_first, w_second)
    w_first.core()
    w_second.near()
    at_once(w_first, w_second)
    w_first.launch()
    w_second.launch()
    at_once(w_first)
    first = w_first.done(places)

    tokens = moved[:, :part].reshape(length, D)
    texts = moved[:, part:].reshape(prompt, D)
    prompt_length = lax.dynamic_slice_in_dim(text_lengths, ring.seq, 1, 0)

    table = lax.optimization_barrier(first[:, 3 * D :]).T.astype(F32)
    full, at = ([], 0)
    for v in vectors[:-1]:
        wide = v.shape[0] // rows
        full.append(table[at : at + wide].reshape(wide, -1, rows).transpose(1, 0, 2).reshape(-1))
        at += wide
    bias_in = table[at : at + fours].reshape(fours, 1, D)
    (g1, b1, bias_out, g2, b2, bias_cross, g3, b3, bias_last, bias_qv, bias_qv2) = full
    zero = jnp.zeros((D,), F32)

    tile = min(QB, length)
    grid = (length // tile,)
    row_tile = pl.BlockSpec((tile, D), lambda i, *_: (i, 0))
    vec8, vec1 = (whole((8, D)), whole((1, D)))
    sum8 = pl.BlockSpec((8, D), lambda *_: (0, 0))
    square = (D, D)
    flat = (length, D)

    def weight_block(index):
        return whole(square, (0, index))

    def streamed(offset):
        return pl.BlockSpec(square, lambda t, *_: (0, t + offset))

    def columns(width):
        return pl.BlockSpec((tile, width), lambda i, *_: (i, 0))

    stat_tile = pl.BlockSpec((HEADS, tile), lambda i, *_: (0, i))
    unit = 2 * length * D * D

    h1, qkv = kernel_call(
        qkv_kernel, "qkv", grid,
        [row_tile, whole((D, 3 * D)), vec8],
        [row_tile, columns(3 * D)],
        [(flat, BF16), ((length, 3 * D), BF16)],
        (tokens, first, line(g1, b1, bias_qv[:D], zero, bias_qv[D:])),
        flops=3 * unit, moved=16 * length * D,
    )
    now = [qkv, h1]
    at_once(now, w_second)
    w_second.far()
    at_once(now, w_second)
    qkv, h1 = now
    w_second.launch()
    o1, lse1 = attend(qkv)
    now = [o1]
    at_once(now, w_second)
    w_second.core()
    w_second.launch()
    at_once(now, w_second)
    (o1,) = now
    second = w_second.done(places)
    kv2 = (mm(texts, second[:, 2 * D : 4 * D]) + jnp.concatenate([zero, bias_qv2[D:]])).astype(BF16)
    x1, h2, q2, o2, x2, h3, lse2 = kernel_call(
        cross_kernel, "cross", grid,
        [row_tile, row_tile, weight_block(0), weight_block(1), weight_block(4),
         whole((prompt, 2 * D)), vec8],
        [row_tile] * 6 + [stat_tile],
        [(flat, F32), (flat, BF16), (flat, BF16), (flat, BF16), (flat, F32), (flat, BF16),
         ((HEADS, length), F32)],
        (prompt_length, tokens, o1, second, second, second, kv2,
         line(bias_out, g2, b2, bias_qv2[:D], bias_cross, g3, b3)),
        flops=5 * unit, moved=30 * length * D, prefetch=1,
    )
    out_grad, h3 = lax.optimization_barrier((out_grad, h3))
    grad_rows = lax.all_to_all(out_grad, "seq", 0, 0, tiled=True).reshape(flat)
    hidden = (length, fours * D)
    by_unit = pl.BlockSpec((length, D), lambda t, *_: (0, t))
    act, slope, out = kernel_call(
        mlp_kernel, "mlp", (fours,),
        [whole(flat), streamed(0), streamed(fours),
         pl.BlockSpec((1, 1, D), lambda t, *_: (t, 0, 0)), whole(flat), vec1],
        [by_unit, by_unit, whole(flat, single=False)],
        [(hidden, BF16), (hidden, BF16), (flat, BF16)],
        (h3, mlp, mlp, bias_in, x2, bias_last.reshape(1, D)),
        scratch=[pltpu.VMEM(flat, F32)],
        flops=2 * fours * unit, moved=40 * length * D,
    )

    now = [out, act, slope, grad_rows]
    at_once(now)
    out, act, slope, grad_rows = now
    leaving_out = [lax.all_to_all(out.reshape(n_seq, part, D), "seq", 0, 0, tiled=True)]
    full_flat = whole(flat)
    du, du_sum = kernel_call(
        du_kernel, "du", (fours,),
        [full_flat, streamed(fours), by_unit],
        [by_unit, pl.BlockSpec((1, 1, D), lambda t, *_: (t, 0, 0))],
        [(hidden, BF16), ((fours, 1, D), F32)],
        (grad_rows, mlp, slope),
        flops=fours * unit, moved=26 * length * D,
    )
    last = fours - 1
    r_mlp = Steps(
        ring,
        weight_grads(
            flat_places,
            (act, grad_rows, h3, du),
            [
                pl.BlockSpec((length, D), lambda t, *_: (0, jnp.minimum(t, last))),
                full_flat,
                full_flat,
                pl.BlockSpec((length, D), lambda t, *_: (0, jnp.maximum(t - fours, 0))),
            ],
            [(0, 1)] * fours + [(2, 3)] * fours,
            D,
            "d_mlp",
        ),
    )
    now = [du]
    at_once(now, leaving_out, r_mlp)
    (du,) = now
    (block_output,) = leaving_out
    r_mlp.launch()
    dx2, dc, do2, sums3 = kernel_call(
        norm3_kernel, "norm3_back", grid,
        [columns(fours * D), whole((D, fours * D)), row_tile, row_tile, vec1, weight_block(4)],
        [row_tile] * 3 + [sum8],
        [(flat, F32), (flat, BF16), (flat, BF16), ((8, D), F32)],
        (du, mlp, grad_rows, x2, g3.reshape(1, D), second),
        flops=(fours + 1) * unit, moved=32 * length * D,
    )
    now = [dx2, dc, do2]
    at_once(now, r_mlp)
    r_mlp.near()
    at_once(now, r_mlp)
    r_mlp.launch()
    dx2, dc, do2 = now
    dq2, dkv2, dx1, da, do1, sums2 = kernel_call(
        cross_back_kernel, "cross_back", grid,
        [row_tile, whole((prompt, 2 * D)), row_tile, row_tile, stat_tile,
         weight_block(1), weight_block(0), row_tile, row_tile, vec1],
        [row_tile, whole((prompt, 2 * D), single=False), row_tile, row_tile, row_tile, sum8],
        [(flat, BF16), ((prompt, 2 * D), BF16), (flat, F32), (flat, BF16), (flat, BF16), ((8, D), F32)],
        (prompt_length, q2, kv2, o2, do2, lse2, second, second, x1, dx2, g2.reshape(1, D)),
        scratch=[pltpu.VMEM((prompt, 2 * D), F32)],
        flops=5 * unit, moved=34 * length * D, prefetch=1,
    )
    text_block = [whole((prompt, D), (0, i)) for i in range(2)]
    r_mid = Steps(
        ring,
        weight_grads(
            flat_places,
            (o1, da, o2, dc, h2, dq2, texts, dkv2, dkv2),
            [full_flat] * 6 + [whole((prompt, D))] + text_block,
            [(0, 1), (2, 3), (4, 5), (6, 7), (6, 8)],
            D,
            "d_mid",
        ),
    )
    now = [do1, dx1, dkv2]
    at_once(now, r_mid, r_mlp)
    r_mlp.far()
    at_once(now, r_mid, r_mlp)
    do1, dx1, dkv2 = now
    r_mid.launch()
    r_mlp.launch()
    count = HEADS // 4
    back_a = list(attend_back(qkv, o1, do1, lse1, 0, count))
    now = [do1]
    at_once(now, back_a, r_mid, r_mlp)
    r_mid.near()
    r_mlp.scatter()
    at_once(now, back_a, r_mid, r_mlp)
    (do1,) = now
    r_mid.launch()
    r_mlp.launch_scatter()
    narrow = [full_flat] + [whole((length, count * PAIR))] * 3
    units = [(0, 1), (0, 2), (0, 3)]
    r_a = Steps(ring, weight_grads(places, (h1, *back_a), narrow, units, count * PAIR, "d_qkv_a"))
    now = [do1]
    at_once(now, r_a)
    r_a.launch()
    back_b = list(attend_back(qkv, o1, now[0], lse1, count, count))
    at_once(back_b, r_a, r_mid)
    r_mid.far()
    r_a.near()
    at_once(back_b, r_a, r_mid)
    r_mid.launch()
    r_a.launch()
    r_b = Steps(ring, weight_grads(places, (h1, *back_b), narrow, units, count * PAIR, "d_qkv_b"))
    at_once(back_b, r_a, r_b, r_mid)
    r_mid.scatter()
    r_a.far()
    dv2_sum = jnp.sum(dkv2[:, D:].astype(F32), axis=0)
    early = [
        sums2[2], sums2[0], sums2[1], sums3[2], sums3[0], sums3[1], sums3[3],
        jnp.concatenate([sums2[3], dv2_sum]),
        du_sum.reshape(fours, ring.count, rows).transpose(1, 0, 2).reshape(-1),
    ]
    early = [across(early)]
    text_grad = mm(dkv2, second[:, 2 * D : 4 * D], NT).astype(BF16)
    at_once(back_b, r_a, r_b, r_mid, early)
    r_b.launch()
    r_a.launch()
    r_mid.launch_scatter()
    early = [lax.all_to_all(early[0], AXES, 0, 0, tiled=True)]
    image_grad, sums1 = kernel_call(
        norm1_kernel, "norm1_back", grid,
        [columns(count * PAIR)] * 6 + [whole((D, 3 * D)), row_tile, row_tile, vec1],
        [row_tile, sum8],
        [(flat, BF16), ((8, D), F32)],
        (*back_a, *back_b, first, tokens, dx1, g1.reshape(1, D)),
        flops=3 * unit, moved=18 * length * D,
    )
    now = [image_grad, text_grad, sums1]
    at_once(now, r_a, r_b, early)
    image_grad, text_grad, sums1 = now
    r_b.near()
    leaving = jnp.concatenate(
        [image_grad.reshape(n_seq, part, D), text_grad.reshape(n_seq, text_part, D)], axis=1
    )
    now = [leaving]
    at_once(now, r_b)
    r_b.launch()
    (leaving,) = now
    leaving = [lax.all_to_all(leaving, "seq", 0, 0, tiled=True)]
    at_once(r_b, r_a)
    r_a.deep()
    r_b.far()
    late = [across([sums1[0], sums1[1], jnp.concatenate([sums1[2], sums1[3]])])]
    at_once(r_a, r_b, late)
    r_b.launch()
    r_a.launch()
    at_once(r_b, leaving, late)
    late = lax.all_to_all(late[0], AXES, 0, 0, tiled=True)
    r_b.deep()
    r_b.launch()
    leaving = leaving[0].astype(F32)
    mlp_grad = r_mlp.done()
    mlp_out_grad = mlp_grad[:, : fours * D].reshape(rows, fours, D).transpose(1, 0, 2).reshape(-1, D)
    mlp_in_grad = mlp_grad[:, fours * D :].reshape(rows, fours, ring.count, rows)
    mlp_in_grad = mlp_in_grad.transpose(0, 2, 1, 3).reshape(rows, -1)
    mid, last_a, last_b = (r_mid.done(), r_a.done(), r_b.done())
    wide = count * PAIR
    self_qkv_grad = jnp.concatenate(
        [half[:, i * wide : (i + 1) * wide] for i in range(3) for half in (last_a, last_b)], axis=1
    )

    small = jnp.concatenate([jnp.sum(early[0], axis=0), jnp.sum(late, axis=0)])

    def mine(total, at, wide):
        return total[at * rows : at * rows + wide]

    two = 2 * rows
    return (
        block_output,
        leaving[:, :part],
        leaving[:, part:],
        mine(small, 9 + fours, rows),
        mine(small, 10 + fours, rows),
        self_qkv_grad,
        mine(small, 11 + fours, two),
        mid[:, :D],
        mine(small, 0, rows),
        mine(small, 1, rows),
        mine(small, 2, rows),
        mid[:, 2 * D : 3 * D],
        mid[:, 3 * D :],
        mine(small, 7, two),
        mid[:, D : 2 * D],
        mine(small, 3, rows),
        mine(small, 4, rows),
        mine(small, 5, rows),
        mlp_in_grad,
        mine(small, 9, fours * rows),
        mlp_out_grad,
        mine(small, 6, rows),
    )


def places_of(images, rows):
    ins = (
        P(images, "seq", None),
        P(images, "seq", None),
        P(images),
        P(images, "seq", None),
        P(rows),
        P(rows),
        P(rows, None),
        P(rows),
        P(rows, None),
        P(rows),
        P(rows),
        P(rows),
        P(rows, None),
        P(rows, None),
        P(rows),
        P(rows, None),
        P(rows),
        P(rows),
        P(rows),
        P(rows, None),
        P(rows),
        P(rows, None),
        P(rows),
    )
    outs = (
            P(images, "seq", None),
            P(images, "seq", None),
            P(images, "seq", None),
            P(rows),
            P(rows),
            P(rows, None),
            P(rows),
            P(rows, None),
            P(rows),
            P(rows),
            P(rows),
            P(rows, None),
            P(rows, None),
            P(rows),
            P(rows, None),
            P(rows),
            P(rows),
            P(rows),
            P(rows, None),
            P(rows),
            P(rows, None),
            P(rows),
        )
    return (ins, outs)


def solution(mesh):
    n_dp, n_seq = (mesh.shape["dp"], mesh.shape["seq"])
    spread = places_of("dp", ("dp", "seq"))
    single = places_of(("z", "core"), AXES)

    def layer(*args):
        images = args[0].shape[0] // n_dp
        if images == n_seq and (n_dp, n_seq) == (8, 4):
            fine = Mesh(mesh.devices.reshape(n_dp // 2, 2, n_seq), AXES)
            plan, place, grid = (functools.partial(whole_images, fine), single, fine)
        else:
            plan, place, grid = (per_device, spread, mesh)
        return jax.shard_map(
            plan, mesh=grid, in_specs=place[0], out_specs=place[1], check_vma=False
        )(*args)

    return layer
```

```python
import functools
import itertools

import jax
import jax.numpy as jnp
from jax import lax
from jax.experimental import pallas as pl
from jax.experimental.pallas import tpu as pltpu
from jax.sharding import Mesh
from jax.sharding import PartitionSpec as P

D = 1024
HEADS = 16
HEAD_DIM = 64


EPSILON = 1e-05
SCALING = 0.125
NEGATIVE = -1e30
VMEM = 56 * 1024 * 1024


def layer_norm(values, gain, shift):
    center = values - jnp.mean(values, axis=-1, keepdims=True)
    inverse = lax.rsqrt(jnp.mean(center * center, axis=-1, keepdims=True) + EPSILON)
    normed = center * inverse
    return (normed * gain + shift, normed, inverse)


def norm_back(grad_rows, normed, inverse, gain):
    scaled = grad_rows * gain
    back = inverse * (
        scaled
        - jnp.mean(scaled, axis=-1, keepdims=True)
        - normed * jnp.mean(scaled * normed, axis=-1, keepdims=True)
    )
    return (back, jnp.sum(grad_rows * normed, axis=(0, 1)), jnp.sum(grad_rows, axis=(0, 1)))


def project(left, weight):
    return jnp.einsum("bld,de->ble", left, weight, preferred_element_type=jnp.float32)


def project_back(grad_rows, weight):
    return jnp.einsum("ble,de->bld", grad_rows, weight, preferred_element_type=jnp.float32)


def weight_grad(left, grad_rows):
    return jnp.einsum("bld,ble->de", left, grad_rows, preferred_element_type=jnp.float32)


def column_sums(grad_rows):
    return jnp.sum(grad_rows.astype(jnp.float32), axis=(0, 1))


def split_heads(rows):
    return rows.reshape(rows.shape[0], rows.shape[1], HEADS, HEAD_DIM)


def gelu_tanh(values):
    return jax.nn.gelu(values, approximate=True)


def block_scores(queries, key_rows, start, width, mask_at):
    key_block = split_heads(lax.dynamic_slice_in_dim(key_rows, start, width, 1))
    scores = (
        jnp.einsum("bqhd,bkhd->bhqk", queries, key_block, preferred_element_type=jnp.float32)
        * SCALING
    )
    return (jnp.where(mask_at(start, width), scores, NEGATIVE), key_block)


def spread_attend(query_rows, key_rows, value_rows, mask_at, width):
    queries = split_heads(query_rows)
    batch_size, length = (query_rows.shape[0], query_rows.shape[1])
    blocks = key_rows.shape[1] // width

    def stats(block_index, carry):
        running_max, running_sum = carry
        scores, key_block = block_scores(queries, key_rows, block_index * width, width, mask_at)
        new_max = jnp.maximum(running_max, jnp.max(scores, axis=-1))
        running_sum = running_sum * jnp.exp(running_max - new_max) + jnp.sum(
            jnp.exp(scores - new_max[..., None]), axis=-1
        )
        return (new_max, running_sum)

    start_max = jnp.full((batch_size, HEADS, length), NEGATIVE, jnp.float32)
    final_max, final_sum = lax.fori_loop(0, blocks, stats, (start_max, jnp.zeros_like(start_max)))
    log_total = final_max + jnp.log(final_sum)

    def accumulate(block_index, total):
        start = block_index * width
        scores, key_block = block_scores(queries, key_rows, start, width, mask_at)
        weights = jnp.exp(scores - log_total[..., None]).astype(jnp.bfloat16)
        value_block = split_heads(lax.dynamic_slice_in_dim(value_rows, start, width, 1))
        return total + jnp.einsum(
            "bhqk,bkhd->bqhd", weights, value_block, preferred_element_type=jnp.float32
        )

    total = lax.fori_loop(
        0, blocks, accumulate, jnp.zeros((batch_size, length, HEADS, HEAD_DIM), jnp.float32)
    )
    return (total.reshape(batch_size, length, HEADS * HEAD_DIM).astype(jnp.bfloat16), log_total)


def spread_attend_back(query_rows, key_rows, value_rows, grad_rows, log_total, mask_at, width):
    queries = split_heads(query_rows)
    grad_heads = split_heads(grad_rows)
    batch_size, length = (query_rows.shape[0], query_rows.shape[1])
    blocks = key_rows.shape[1] // width

    def weights_at(start):
        scores, key_block = block_scores(queries, key_rows, start, width, mask_at)
        value_block = split_heads(lax.dynamic_slice_in_dim(value_rows, start, width, 1))
        probs = jnp.exp(scores - log_total[..., None])
        grad_probs = jnp.einsum(
            "bqhd,bkhd->bhqk", grad_heads, value_block, preferred_element_type=jnp.float32
        )
        return (probs, grad_probs, key_block)

    def inner(block_index, delta):
        probs, grad_probs, key_block = weights_at(block_index * width)
        return delta + jnp.sum(probs * grad_probs, axis=-1)

    delta = lax.fori_loop(0, blocks, inner, jnp.zeros((batch_size, HEADS, length), jnp.float32))
    start_grad = jnp.zeros((batch_size, length, HEADS, HEAD_DIM), jnp.float32)

    def step(grad_queries, block_index):
        probs, grad_probs, key_block = weights_at(block_index * width)
        grad_scores = (probs * (grad_probs - delta[..., None])).astype(jnp.bfloat16)
        grad_queries = grad_queries + jnp.einsum(
            "bhqk,bkhd->bqhd", grad_scores, key_block, preferred_element_type=jnp.float32
        )
        grad_keys = jnp.einsum(
            "bhqk,bqhd->bkhd", grad_scores, queries, preferred_element_type=jnp.float32
        )
        grad_values = jnp.einsum(
            "bhqk,bqhd->bkhd",
            probs.astype(jnp.bfloat16),
            grad_heads,
            preferred_element_type=jnp.float32,
        )
        return (grad_queries, (grad_keys, grad_values))

    grad_queries, (key_parts, value_parts) = lax.scan(
        step, start_grad, jnp.arange(blocks, dtype=jnp.int32)
    )

    def merge_blocks(parts):
        return jnp.moveaxis(parts, 0, 1).reshape(batch_size, blocks * width, HEADS * HEAD_DIM)

    return (
        (grad_queries * SCALING).reshape(batch_size, length, HEADS * HEAD_DIM),
        merge_blocks(key_parts) * SCALING,
        merge_blocks(value_parts),
        delta,
    )


def gather_self(gain, shift, weight_qkv, bias_qv, weight_out, bias_out):
    return (
        lax.all_gather(gain, ("dp", "seq"), axis=0, tiled=True),
        lax.all_gather(shift, ("dp", "seq"), axis=0, tiled=True),
        lax.all_gather(weight_qkv, ("dp", "seq"), axis=0, tiled=True),
        lax.all_gather(bias_qv, ("dp", "seq"), axis=0, tiled=True),
        lax.all_gather(weight_out, ("dp", "seq"), axis=0, tiled=True),
        lax.all_gather(bias_out, ("dp", "seq"), axis=0, tiled=True),
    )


def gather_cross(gain, shift, weight_query, weight_kv, bias_qv, weight_out, bias_out):
    return (
        lax.all_gather(gain, ("dp", "seq"), axis=0, tiled=True),
        lax.all_gather(shift, ("dp", "seq"), axis=0, tiled=True),
        lax.all_gather(weight_query, ("dp", "seq"), axis=0, tiled=True),
        lax.all_gather(weight_kv, ("dp", "seq"), axis=0, tiled=True),
        lax.all_gather(bias_qv, ("dp", "seq"), axis=0, tiled=True),
        lax.all_gather(weight_out, ("dp", "seq"), axis=0, tiled=True),
        lax.all_gather(bias_out, ("dp", "seq"), axis=0, tiled=True),
    )


def gather_mlp(gain, shift, weight_in, bias_in, weight_out, bias_out):
    return (
        lax.all_gather(gain, ("dp", "seq"), axis=0, tiled=True),
        lax.all_gather(shift, ("dp", "seq"), axis=0, tiled=True),
        lax.all_gather(weight_in, ("dp", "seq"), axis=0, tiled=True),
        lax.all_gather(bias_in, ("dp", "seq"), axis=0, tiled=True),
        lax.all_gather(weight_out, ("dp", "seq"), axis=0, tiled=True),
        lax.all_gather(bias_out, ("dp", "seq"), axis=0, tiled=True),
    )


def per_device(
    image_tokens,
    text_states,
    text_lengths,
    out_grad,
    norm1_gain,
    norm1_bias,
    self_qkv,
    self_bias_qv,
    self_out,
    self_out_bias,
    norm2_gain,
    norm2_bias,
    cross_query,
    cross_kv,
    cross_bias_qv,
    cross_out,
    cross_out_bias,
    norm3_gain,
    norm3_bias,
    mlp_in,
    mlp_in_bias,
    mlp_out,
    mlp_out_bias,
):
    length = image_tokens.shape[1]
    own_start = lax.axis_index("seq") * length
    query_pos = own_start + jnp.arange(length, dtype=jnp.int32)

    def causal_at(start, width):
        key_pos = start + jnp.arange(width, dtype=jnp.int32)
        return (key_pos[None, :] <= query_pos[:, None])[None, None]

    def padded_at(start, width):
        key_pos = start + jnp.arange(width, dtype=jnp.int32)
        return (key_pos[None, :] < text_lengths[:, None])[:, None, None, :]

    self_full = gather_self(norm1_gain, norm1_bias, self_qkv, self_bias_qv, self_out, self_out_bias)
    residual = image_tokens.astype(jnp.float32)
    normed_in, normed_one, inverse_one = layer_norm(
        residual, self_full[0].astype(jnp.float32), self_full[1].astype(jnp.float32)
    )
    hidden_one = normed_in.astype(jnp.bfloat16)
    mixed = project(hidden_one, self_full[2])
    bias_self = self_full[3].astype(jnp.float32)
    query_one = (mixed[..., :D] + bias_self[:D]).astype(jnp.bfloat16)
    key_one = mixed[..., D : 2 * D].astype(jnp.bfloat16)
    value_one = (mixed[..., 2 * D :] + bias_self[D:]).astype(jnp.bfloat16)
    key_all, value_all = (
        lax.all_gather(key_one, "seq", axis=1, tiled=True),
        lax.all_gather(value_one, "seq", axis=1, tiled=True),
    )
    self_width = min(128, key_all.shape[1])
    attended, log_one = spread_attend(query_one, key_all, value_all, causal_at, self_width)
    after_self = residual + project(attended, self_full[4]) + self_full[5].astype(jnp.float32)
    cross_full = gather_cross(
        norm2_gain, norm2_bias, cross_query, cross_kv, cross_bias_qv, cross_out, cross_out_bias
    )
    normed_mid, normed_two, inverse_two = layer_norm(
        after_self, cross_full[0].astype(jnp.float32), cross_full[1].astype(jnp.float32)
    )
    hidden_two = normed_mid.astype(jnp.bfloat16)
    bias_cross = cross_full[4].astype(jnp.float32)
    query_two = (project(hidden_two, cross_full[2]) + bias_cross[:D]).astype(jnp.bfloat16)
    text_mixed = project(text_states, cross_full[3])
    text_key = text_mixed[..., :D].astype(jnp.bfloat16)
    text_value = (text_mixed[..., D:] + bias_cross[D:]).astype(jnp.bfloat16)
    key_two, value_two = (
        lax.all_gather(text_key, "seq", axis=1, tiled=True),
        lax.all_gather(text_value, "seq", axis=1, tiled=True),
    )
    text_width = key_two.shape[1]
    attended_two, log_two = spread_attend(query_two, key_two, value_two, padded_at, text_width)
    after_cross = (
        after_self + project(attended_two, cross_full[5]) + cross_full[6].astype(jnp.float32)
    )
    mlp_full = gather_mlp(norm3_gain, norm3_bias, mlp_in, mlp_in_bias, mlp_out, mlp_out_bias)
    normed_last, normed_three, inverse_three = layer_norm(
        after_cross, mlp_full[0].astype(jnp.float32), mlp_full[1].astype(jnp.float32)
    )
    hidden_three = normed_last.astype(jnp.bfloat16)
    pre_act = project(hidden_three, mlp_full[2]) + mlp_full[3].astype(jnp.float32)
    activated, gelu_back = jax.vjp(gelu_tanh, pre_act)
    act_low = activated.astype(jnp.bfloat16)
    block_output = (
        after_cross + project(act_low, mlp_full[4]) + mlp_full[5].astype(jnp.float32)
    ).astype(jnp.bfloat16)
    mlp_back = gather_mlp(norm3_gain, norm3_bias, mlp_in, mlp_in_bias, mlp_out, mlp_out_bias)
    grad_top = out_grad.astype(jnp.float32)
    w_out_grad = weight_grad(act_low, out_grad)
    b_out_grad = column_sums(out_grad)
    grad_act = project_back(out_grad, mlp_back[4])
    grad_pre = gelu_back(grad_act)[0].astype(jnp.bfloat16)
    w_in_grad = weight_grad(hidden_three, grad_pre)
    b_in_grad = column_sums(grad_pre)
    back_three, gain_three_grad, shift_three_grad = norm_back(
        project_back(grad_pre, mlp_back[2]),
        normed_three,
        inverse_three,
        mlp_back[0].astype(jnp.float32),
    )
    grad_two = grad_top + back_three
    mlp_grads = (
        lax.psum_scatter(gain_three_grad, ("dp", "seq"), scatter_dimension=0, tiled=True),
        lax.psum_scatter(shift_three_grad, ("dp", "seq"), scatter_dimension=0, tiled=True),
        lax.psum_scatter(w_in_grad, ("dp", "seq"), scatter_dimension=0, tiled=True),
        lax.psum_scatter(b_in_grad, ("dp", "seq"), scatter_dimension=0, tiled=True),
        lax.psum_scatter(w_out_grad, ("dp", "seq"), scatter_dimension=0, tiled=True),
        lax.psum_scatter(b_out_grad, ("dp", "seq"), scatter_dimension=0, tiled=True),
    )
    cross_back = gather_cross(
        norm2_gain, norm2_bias, cross_query, cross_kv, cross_bias_qv, cross_out, cross_out_bias
    )
    grad_cross = grad_two.astype(jnp.bfloat16)
    cross_out_term = weight_grad(attended_two, grad_cross)
    cross_bias_term = column_sums(grad_cross)
    grad_att_two = project_back(grad_cross, cross_back[5]).astype(jnp.bfloat16)
    grad_query_two, grad_key_two, grad_value_two, delta_two = spread_attend_back(
        query_two, key_two, value_two, grad_att_two, log_two, padded_at, text_width
    )
    query_two_low = grad_query_two.astype(jnp.bfloat16)
    text_key_grad, text_value_grad = (
        lax.psum_scatter(
            grad_key_two.astype(jnp.bfloat16), "seq", scatter_dimension=1, tiled=True
        ).astype(jnp.float32),
        lax.psum_scatter(
            grad_value_two.astype(jnp.bfloat16), "seq", scatter_dimension=1, tiled=True
        ).astype(jnp.float32),
    )
    text_value_low = text_value_grad.astype(jnp.bfloat16)
    text_kv_grad = jnp.concatenate([text_key_grad.astype(jnp.bfloat16), text_value_low], axis=-1)
    cross_query_term = weight_grad(hidden_two, query_two_low)
    cross_kv_term = weight_grad(text_states, text_kv_grad)
    cross_qv_term = jnp.concatenate([column_sums(query_two_low), column_sums(text_value_low)])
    text_grad = project_back(text_kv_grad, cross_back[3])
    back_two, gain_two_grad, shift_two_grad = norm_back(
        project_back(query_two_low, cross_back[2]),
        normed_two,
        inverse_two,
        cross_back[0].astype(jnp.float32),
    )
    grad_one = grad_two + back_two
    cross_grads = (
        lax.psum_scatter(gain_two_grad, ("dp", "seq"), scatter_dimension=0, tiled=True),
        lax.psum_scatter(shift_two_grad, ("dp", "seq"), scatter_dimension=0, tiled=True),
        lax.psum_scatter(cross_query_term, ("dp", "seq"), scatter_dimension=0, tiled=True),
        lax.psum_scatter(cross_kv_term, ("dp", "seq"), scatter_dimension=0, tiled=True),
        lax.psum_scatter(cross_qv_term, ("dp", "seq"), scatter_dimension=0, tiled=True),
        lax.psum_scatter(cross_out_term, ("dp", "seq"), scatter_dimension=0, tiled=True),
        lax.psum_scatter(cross_bias_term, ("dp", "seq"), scatter_dimension=0, tiled=True),
    )
    self_back = gather_self(norm1_gain, norm1_bias, self_qkv, self_bias_qv, self_out, self_out_bias)
    grad_self = grad_one.astype(jnp.bfloat16)
    self_out_term = weight_grad(attended, grad_self)
    self_bias_term = column_sums(grad_self)
    grad_att_one = project_back(grad_self, self_back[4]).astype(jnp.bfloat16)
    grad_query_one, grad_key_all, grad_value_all, delta_one = spread_attend_back(
        query_one, key_all, value_all, grad_att_one, log_one, causal_at, self_width
    )
    grad_key_one, grad_value_one = (
        lax.psum_scatter(
            grad_key_all.astype(jnp.bfloat16), "seq", scatter_dimension=1, tiled=True
        ).astype(jnp.float32),
        lax.psum_scatter(
            grad_value_all.astype(jnp.bfloat16), "seq", scatter_dimension=1, tiled=True
        ).astype(jnp.float32),
    )
    query_one_low = grad_query_one.astype(jnp.bfloat16)
    value_one_low = grad_value_one.astype(jnp.bfloat16)
    grad_qkv = jnp.concatenate(
        [query_one_low, grad_key_one.astype(jnp.bfloat16), value_one_low], axis=-1
    )
    self_qkv_term = weight_grad(hidden_one, grad_qkv)
    self_qv_term = jnp.concatenate([column_sums(query_one_low), column_sums(value_one_low)])
    back_one, gain_one_grad, shift_one_grad = norm_back(
        project_back(grad_qkv, self_back[2]),
        normed_one,
        inverse_one,
        self_back[0].astype(jnp.float32),
    )
    image_grad = grad_one + back_one
    self_grads = (
        lax.psum_scatter(gain_one_grad, ("dp", "seq"), scatter_dimension=0, tiled=True),
        lax.psum_scatter(shift_one_grad, ("dp", "seq"), scatter_dimension=0, tiled=True),
        lax.psum_scatter(self_qkv_term, ("dp", "seq"), scatter_dimension=0, tiled=True),
        lax.psum_scatter(self_qv_term, ("dp", "seq"), scatter_dimension=0, tiled=True),
        lax.psum_scatter(self_out_term, ("dp", "seq"), scatter_dimension=0, tiled=True),
        lax.psum_scatter(self_bias_term, ("dp", "seq"), scatter_dimension=0, tiled=True),
    )
    return (
        block_output,
        image_grad,
        text_grad,
        self_grads[0],
        self_grads[1],
        self_grads[2],
        self_grads[3],
        self_grads[4],
        self_grads[5],
        cross_grads[0],
        cross_grads[1],
        cross_grads[2],
        cross_grads[3],
        cross_grads[4],
        cross_grads[5],
        cross_grads[6],
        mlp_grads[0],
        mlp_grads[1],
        mlp_grads[2],
        mlp_grads[3],
        mlp_grads[4],
        mlp_grads[5],
    )


LOG2E = 1.4426950408889634
LN2 = 0.6931471805599453
QB = 256
PAIR = 2 * HEAD_DIM
NT = (((1,), (1,)), ((), ()))
NN = (((1,), (0,)), ((), ()))
TN = (((0,), (0,)), ((), ()))
BF16 = jnp.bfloat16
F32 = jnp.float32


def mm(left, right, dims=NN):
    return lax.dot_general(left, right, dims, preferred_element_type=F32)


def head_lanes(rows, head):
    lane = lax.broadcasted_iota(jnp.int32, rows.shape, 1)
    keep = (lane < HEAD_DIM) if head == 0 else (lane >= HEAD_DIM)
    return jnp.where(keep, rows, jnp.zeros_like(rows))


def ahead(items, start):
    later = start(items[0])
    for at, item in enumerate(items):
        value = later
        if at + 1 < len(items):
            later = start(items[at + 1])
        yield item, value


def whole(shape, index=None, single=True):
    where = index or (0,) * len(shape)
    mode = {"pipeline_mode": pl.Buffered(1)} if single else {}
    return pl.BlockSpec(shape, lambda *_: where, **mode)


def kernel_call(body, name, grid, ins, outs, shapes, args, scratch=(), flops=0, prefetch=0, moved=0, exps=0):
    return pl.pallas_call(
        body,
        grid_spec=pltpu.PrefetchScalarGridSpec(
            num_scalar_prefetch=prefetch,
            grid=grid,
            in_specs=ins,
            out_specs=outs,
            scratch_shapes=list(scratch),
        ),
        out_shape=[jax.ShapeDtypeStruct(s, d) for s, d in shapes],
        compiler_params=pltpu.CompilerParams(vmem_limit_bytes=VMEM),
        cost_estimate=pl.CostEstimate(flops=flops // 32, bytes_accessed=moved // 32, transcendentals=exps // 32),
        name=name,
    )(*args)


def attend_kernel(q_ref, k_ref, v_ref, o_ref, lse_ref, vx_ref):
    keys = k_ref.shape[0]
    length = q_ref.shape[0]
    block = min(QB, length)
    vx_ref[:, :PAIR] = v_ref[...]
    vx_ref[:, PAIR:] = jnp.ones((keys, PAIR), BF16)
    items = list(itertools.product(range(0, length, block), range(2)))

    def products(item):
        start, head = item
        rows = head_lanes(q_ref[start : start + block, :], head)
        return mm(rows, k_ref[: start + block, :], NT)

    for (start, head), scores in ahead(items, products):
        limit = start + block
        last = scores[:, start:]
        col = lax.broadcasted_iota(jnp.int32, last.shape, 1)
        row = lax.broadcasted_iota(jnp.int32, last.shape, 0)
        last = jnp.where(col <= row, last, NEGATIVE)
        scores = jnp.concatenate([scores[:, :start], last], axis=1) if start else last
        top = jnp.max(scores, axis=1, keepdims=True)
        weights = jnp.exp2(scores - top).astype(BF16)
        total = mm(weights, vx_ref[:limit, :])
        out = total[:, :PAIR] / total[:, PAIR:]
        stat = (top + jnp.log2(total[:, PAIR:])).T
        lse_ref[0, head : head + 1, start:limit] = stat[:1, :]
        if head == 0:
            kept = out
        else:
            lane = lax.broadcasted_iota(jnp.int32, out.shape, 1)
            o_ref[start:limit, :] = jnp.where(lane < HEAD_DIM, kept, out).astype(BF16)


def attend_back_kernel(
    q_ref, k_ref, v_ref, o_ref, do_ref, lse_ref, dq_ref, dk_ref, dv_ref, acc_ref
):
    keys = k_ref.shape[0]
    block = min(QB, keys)
    product = (do_ref[...].astype(F32) * o_ref[...].astype(F32)).T
    acc_ref[...] = jnp.zeros_like(acc_ref)
    delta = [
        jnp.sum(product[head * HEAD_DIM : (head + 1) * HEAD_DIM, :], axis=0, keepdims=True)
        for head in range(2)
    ]
    items = list(itertools.product(range(0, keys, block), range(2)))

    def products(item):
        start, head = item
        queries = head_lanes(q_ref[start:, :], head)
        grads = head_lanes(do_ref[start:, :], head)
        return (
            queries,
            grads,
            mm(k_ref[start : start + block, :], queries, NT),
            mm(v_ref[start : start + block, :], grads, NT),
        )

    for (start, head), (queries, grads, scores, back) in ahead(items, products):
        probs = jnp.exp2(scores - lse_ref[0, head : head + 1, start:])
        edge = probs[:, :block]
        row = lax.broadcasted_iota(jnp.int32, edge.shape, 0)
        col = lax.broadcasted_iota(jnp.int32, edge.shape, 1)
        edge = jnp.where(row <= col, edge, 0.0)
        if start + block < keys:
            probs = jnp.concatenate([edge, probs[:, block:]], axis=1)
        else:
            probs = edge
        scored = (probs * (back - delta[head][:, start:])).astype(BF16)
        term_v = mm(probs.astype(BF16), grads)
        term_k = mm(scored, queries)
        acc_ref[start:, :] += mm(scored, head_lanes(k_ref[start : start + block, :], head), TN)
        if head == 0:
            grad_keys, grad_values = (term_k, term_v)
        else:
            dk_ref[start : start + block, :] = ((grad_keys + term_k) * LN2).astype(BF16)
            dv_ref[start : start + block, :] = (grad_values + term_v).astype(BF16)
    dq_ref[...] = (acc_ref[...] * SCALING).astype(BF16)


def column_pair(rows, offset):
    return pl.BlockSpec((rows, PAIR), lambda i, *_: (0, i + offset))


def attend(qkv):
    length = qkv.shape[0]
    pairs = HEADS // 2
    return kernel_call(
        attend_kernel,
        "attend",
        (pairs,),
        [column_pair(length, pairs * i) for i in range(3)],
        [column_pair(length, 0), pl.BlockSpec((1, 2, length), lambda i, *_: (i, 0, 0))],
        [((length, D), BF16), ((pairs, 2, length), F32)],
        (qkv, qkv, qkv),
        scratch=[pltpu.VMEM((length, 2 * PAIR), BF16)],
        flops=length * length * HEADS * 512,
        moved=8 * length * D,
        exps=length * length * HEADS // 2,
    )


def attend_back(qkv, out, grad, lse, first, count):
    length = qkv.shape[0]
    pairs = HEADS // 2
    return kernel_call(
        attend_back_kernel,
        "attend_back",
        (count,),
        [column_pair(length, pairs * i + first) for i in range(3)]
        + [column_pair(length, first)] * 2
        + [pl.BlockSpec((1, 2, length), lambda i, *_: (i + first, 0, 0))],
        [column_pair(length, 0)] * 3,
        [((length, count * PAIR), BF16)] * 3,
        (qkv, qkv, qkv, out, grad, lse),
        scratch=[pltpu.VMEM((length, PAIR), F32)],
        flops=length * length * count * 2560,
        moved=2 * 8 * length * count * PAIR,
        exps=length * length * count,
    )


def normed_of(rows):
    center = rows - jnp.mean(rows, axis=1, keepdims=True)
    inverse = lax.rsqrt(jnp.mean(center * center, axis=1, keepdims=True) + EPSILON)
    return (center * inverse, inverse)


def norm_input_grad(grads, normed, inverse, gain):
    scaled = grads * gain
    return inverse * (
        scaled
        - jnp.mean(scaled, axis=1, keepdims=True)
        - normed * jnp.mean(scaled * normed, axis=1, keepdims=True)
    )


def sums(rows):
    return jnp.sum(rows, axis=0, keepdims=True)


def add_row(ref, at, value, first):
    @pl.when(first)
    def _():
        ref[at : at + 1, :] = value

    @pl.when(jnp.logical_not(first))
    def _():
        ref[at : at + 1, :] += value


def gelu_pair(values):
    root = 0.7978845608028654
    square = values * values
    part = 0.5 + 0.5 * jnp.tanh(values * (root + (0.044715 * root) * square))
    out = values * part
    slope = part + (out - out * part) * (2.0 * root + (0.26829 * root) * square)
    return (out, slope)


def qkv_kernel(x_ref, w_ref, vec_ref, h_ref, qkv_ref):
    normed, _ = normed_of(x_ref[0].astype(F32))
    low = (normed * vec_ref[0:1, :] + vec_ref[1:2, :]).astype(BF16)
    h_ref[...] = low
    for part in range(3):
        mixed = mm(low, w_ref[:, part * D : (part + 1) * D]) + vec_ref[2 + part : 3 + part, :]
        if part == 0:
            mixed = mixed * (SCALING * LOG2E)
        qkv_ref[:, part * D : (part + 1) * D] = mixed.astype(BF16)


def pair_keys(kv_ref, at, keys):
    block = kv_ref[:, at : at + PAIR]
    return jnp.concatenate([head_lanes(block, 0), head_lanes(block, 1)], axis=0)


def cross_kernel(
    len_ref, x_ref, o_ref, ws_ref, wq_ref, wc_ref, kv_ref, vec_ref,
    x1_ref, h2_ref, q2_ref, o2_ref, x2_ref, h3_ref, lse_ref,
):
    keys = kv_ref.shape[0]
    after = x_ref[0].astype(F32) + mm(o_ref[...], ws_ref[...]) + vec_ref[0:1, :]
    x1_ref[...] = after
    normed, _ = normed_of(after)
    low = (normed * vec_ref[1:2, :] + vec_ref[2:3, :]).astype(BF16)
    h2_ref[...] = low
    q2_ref[...] = ((mm(low, wq_ref[...]) + vec_ref[3:4, :]) * (SCALING * LOG2E)).astype(BF16)
    ones = jnp.ones((keys, PAIR), BF16)

    def products(at):
        return mm(q2_ref[:, at : at + PAIR], pair_keys(kv_ref, at, keys), NT)

    for at, scores in ahead(list(range(0, D, PAIR)), products):
        pair = at // PAIR
        col = lax.broadcasted_iota(jnp.int32, (scores.shape[0], keys), 1)
        inside = col < len_ref[0]
        halves, tops = ([], [])
        for head in range(2):
            part = jnp.where(inside, scores[:, head * keys : (head + 1) * keys], NEGATIVE)
            top = jnp.max(part, axis=1, keepdims=True)
            halves.append(jnp.exp2(part - top).astype(BF16))
            tops.append(top)
        values = kv_ref[:, D + at : D + at + PAIR]
        right = jnp.concatenate(
            [
                jnp.concatenate([head_lanes(values, h), head_lanes(ones, h)], axis=1)
                for h in range(2)
            ],
            axis=0,
        )
        total = mm(jnp.concatenate(halves, axis=1), right)
        o2_ref[:, at : at + PAIR] = (total[:, :PAIR] / total[:, PAIR:]).astype(BF16)
        lane = lax.broadcasted_iota(jnp.int32, (scores.shape[0], PAIR), 1)
        stat = (jnp.where(lane < HEAD_DIM, tops[0], tops[1]) + jnp.log2(total[:, PAIR:])).T
        lse_ref[2 * pair : 2 * pair + 1, :] = stat[:1, :]
        lse_ref[2 * pair + 1 : 2 * pair + 2, :] = stat[HEAD_DIM : HEAD_DIM + 1, :]
    after = after + mm(o2_ref[...], wc_ref[...]) + vec_ref[4:5, :]
    x2_ref[...] = after
    normed, _ = normed_of(after)
    h3_ref[...] = (normed * vec_ref[5:6, :] + vec_ref[6:7, :]).astype(BF16)


def mlp_kernel(h_ref, wi_ref, wo_ref, bias_ref, x2_ref, last_ref, act_ref, slope_ref, out_ref, acc_ref):
    step = pl.program_id(0)

    @pl.when(step == 0)
    def _():
        acc_ref[...] = x2_ref[...] + last_ref[...]

    tile = min(512, h_ref.shape[0])
    parts = [slice(at, at + tile) for at in range(0, h_ref.shape[0], tile)]
    for rows, mixed in ahead(parts, lambda rows: mm(h_ref[rows, :], wi_ref[...])):
        act, slope = gelu_pair(mixed + bias_ref[0])
        act = act.astype(BF16)
        act_ref[rows, :] = act
        slope_ref[rows, :] = slope.astype(BF16)
        acc_ref[rows, :] += mm(act, wo_ref[...])

    @pl.when(step == pl.num_programs(0) - 1)
    def _():
        out_ref[...] = acc_ref[...].astype(BF16)


def du_kernel(g_ref, wo_ref, slope_ref, du_ref, sum_ref):
    total = None
    parts = [slice(at, at + QB) for at in range(0, g_ref.shape[0], QB)]
    for rows, grad in ahead(parts, lambda rows: mm(g_ref[rows, :], wo_ref[...], NT)):
        low = (grad * slope_ref[rows, :].astype(F32)).astype(BF16)
        du_ref[rows, :] = low
        part = sums(low.astype(F32))
        total = part if total is None else total + part
    sum_ref[0] = total


def norm3_kernel(du_ref, wi_ref, g_ref, x2_ref, gain_ref, wc_ref, dx_ref, dc_ref, do_ref, vec_ref):
    first = pl.program_id(0) == 0
    grads = None
    for step in range(wi_ref.shape[1] // D):
        cols = slice(step * D, (step + 1) * D)
        term = mm(du_ref[:, cols], wi_ref[:, cols], NT)
        grads = term if grads is None else grads + term
    normed, inverse = normed_of(x2_ref[...])
    out = g_ref[...].astype(F32) + norm_input_grad(grads, normed, inverse, gain_ref[...])
    dx_ref[...] = out
    low = out.astype(BF16)
    dc_ref[...] = low
    do_ref[...] = mm(low, wc_ref[...], NT).astype(BF16)
    add_row(vec_ref, 0, sums(grads * normed), first)
    add_row(vec_ref, 1, sums(grads), first)
    add_row(vec_ref, 2, sums(low.astype(F32)), first)
    add_row(vec_ref, 3, sums(g_ref[...].astype(F32)), first)


def cross_back_kernel(
    len_ref, q_ref, kv_ref, o_ref, do_ref, lse_ref, wq_ref, ws_ref, x1_ref, dx2_ref, gain_ref,
    dq_ref, dkv_ref, dx_ref, da_ref, do1_ref, vec_ref, acc_ref,
):
    step = pl.program_id(0)
    first = step == 0
    keys = kv_ref.shape[0]

    @pl.when(first)
    def _():
        acc_ref[...] = jnp.zeros_like(acc_ref)

    lane = lax.broadcasted_iota(jnp.int32, (keys, PAIR), 1)

    def products(at):
        queries = q_ref[:, at : at + PAIR]
        grads = do_ref[:, at : at + PAIR]
        both_keys = pair_keys(kv_ref, at, keys)
        return (
            queries,
            grads,
            both_keys,
            mm(both_keys, queries, NT),
            mm(pair_keys(kv_ref, D + at, keys), grads, NT),
        )

    for at, (queries, grads, both_keys, scores, back) in ahead(list(range(0, D, PAIR)), products):
        pair = at // PAIR
        product = (grads.astype(F32) * o_ref[:, at : at + PAIR].astype(F32)).T
        row = lax.broadcasted_iota(jnp.int32, (keys, scores.shape[1]), 0)
        inside = row < len_ref[0]
        probs, scored = ([], [])
        for head in range(2):
            span = slice(head * keys, (head + 1) * keys)
            at_head = 2 * pair + head
            prob = jnp.exp2(scores[span, :] - lse_ref[at_head : at_head + 1, :])
            prob = jnp.where(inside, prob, 0.0)
            delta = sums(product[head * HEAD_DIM : (head + 1) * HEAD_DIM, :])
            probs.append(prob.astype(BF16))
            scored.append((prob * (back[span, :] - delta)).astype(BF16))
        probs, scored = (jnp.concatenate(probs, axis=0), jnp.concatenate(scored, axis=0))
        for base, left, right in ((0, scored, queries), (D, probs, grads)):
            both = mm(left, right)
            acc_ref[:, base + at : base + at + PAIR] += jnp.where(
                lane < HEAD_DIM, both[:keys, :], both[keys:, :]
            )
        dq_ref[:, at : at + PAIR] = (mm(scored, both_keys, TN) * SCALING).astype(BF16)

    @pl.when(step == pl.num_programs(0) - 1)
    def _():
        dkv_ref[:, :D] = (acc_ref[:, :D] * LN2).astype(BF16)
        dkv_ref[:, D:] = acc_ref[:, D:].astype(BF16)

    grads = mm(dq_ref[...], wq_ref[...], NT)
    normed, inverse = normed_of(x1_ref[...])
    out = dx2_ref[...] + norm_input_grad(grads, normed, inverse, gain_ref[...])
    dx_ref[...] = out
    low = out.astype(BF16)
    da_ref[...] = low
    do1_ref[...] = mm(low, ws_ref[...], NT).astype(BF16)
    add_row(vec_ref, 0, sums(grads * normed), first)
    add_row(vec_ref, 1, sums(grads), first)
    add_row(vec_ref, 2, sums(low.astype(F32)), first)
    add_row(vec_ref, 3, sums(dq_ref[...].astype(F32)), first)


def norm1_kernel(*refs):
    *grad_refs, w_ref, x_ref, dx1_ref, gain_ref, text_ref, out_ref, vec_ref = refs
    first = pl.program_id(0) == 0
    grads, at = (None, 0)
    groups = len(grad_refs) // 3
    rows_q, rows_v = ([], [])
    for group in range(groups):
        for part in range(3):
            ref = grad_refs[3 * group + part]
            wide = ref.shape[1]
            base = part * D + group * wide
            term = mm(ref[...], w_ref[:, base : base + wide], NT)
            grads = term if grads is None else grads + term
        rows_q.append(sums(grad_refs[3 * group][...].astype(F32)))
        rows_v.append(sums(grad_refs[3 * group + 2][...].astype(F32)))
    normed, inverse = normed_of(x_ref[0].astype(F32))
    back = norm_input_grad(grads, normed, inverse, gain_ref[...])
    tile = back.shape[0]
    out_ref[0, :tile, :] = (dx1_ref[...] + back).astype(BF16)
    out_ref[0, tile:, :] = text_ref[...]
    add_row(vec_ref, 0, sums(grads * normed), first)
    add_row(vec_ref, 1, sums(grads), first)
    add_row(vec_ref, 2, jnp.concatenate(rows_q, axis=1), first)
    add_row(vec_ref, 3, jnp.concatenate(rows_v, axis=1), first)


def weight_grad_kernel(units, count, scattered, place_ref, *refs):
    operands, (sent_ref, kept_ref, acc_ref) = (refs[:count], refs[count:])
    step = pl.program_id(0)
    block = acc_ref.shape[0] // 32
    known = sorted(set(units))
    for left, right in known:
        steps = [t for t, unit in enumerate(units) if unit == (left, right)]
        hit = step == steps[0]
        for t in steps[1:]:
            hit = jnp.logical_or(hit, step == t)

        @pl.when(hit)
        def _():
            acc_ref[...] = mm(operands[left][...], operands[right][...], TN)

    halves = ((sent_ref, 1 - place_ref[1]), (kept_ref, place_ref[1]))
    if not scattered:
        wide = 4 * block
        for z, (ref, core) in itertools.product(range(4), halves):
            row = pl.multiple_of((2 * z + core) * wide, wide)
            ref[z * wide : (z + 1) * wide, :] = acc_ref[pl.ds(row, wide), :].astype(BF16)
        return
    for order, far, near, low in itertools.product(range(2), repeat=4):
        z = place_ref[0] ^ (2 * order + low)
        y, x = (near, far) if order else (far, near)
        inner = (place_ref[2] ^ y) * 2 + (place_ref[3] ^ x)
        at = (((order * 2 + far) * 2 + near) * 2 + low) * block
        for ref, core in halves:
            row = pl.multiple_of(((z * 2 + core) * 4 + inner) * block, block)
            ref[at : at + block, :] = acc_ref[pl.ds(row, block), :].astype(BF16)


def weight_grads(places, operands, specs, units, width, name, scattered=True):
    steps = len(units)
    tokens = operands[0].shape[0]
    return kernel_call(
        functools.partial(weight_grad_kernel, tuple(units), len(operands), scattered),
        name,
        (steps,),
        specs,
        [pl.BlockSpec((D // 2, width), lambda t, *_: (0, t))] * 2,
        [((D // 2, steps * width), BF16)] * 2,
        (places, *operands),
        scratch=[pltpu.VMEM((D, width), F32)],
        flops=2 * tokens * D * width * steps,
        moved=2 * D * width * steps + 2 * tokens * D,
        prefetch=1,
    )


def place_kernel(per, place_ref, *refs):
    pieces, out_ref = (refs[:8], refs[8])
    for index, piece in enumerate(pieces):
        far_core, far_side, second = (index // 4, index % 2, (index // 2) % 2)
        for near in range(2):
            for low in range(2):
                z = 2 * second + low
                y, x = (near, far_side) if second else (far_side, near)
                row = (place_ref[0] ^ z) * 2 + (place_ref[1] ^ far_core)
                row = (row * 2 + (place_ref[2] ^ y)) * 2 + (place_ref[3] ^ x)
                row = pl.multiple_of(row * per, per)
                out_ref[pl.ds(row, per), :] = piece[near, low]


def put_in_order(places, pieces):
    near, low, per, width = pieces[0].shape
    wide = width // 5
    (out,) = kernel_call(
        functools.partial(place_kernel, per),
        "put_in_order",
        (5,),
        [pl.BlockSpec((near, low, per, wide), lambda t, *_: (0, 0, 0, t))] * 8,
        [pl.BlockSpec((per * 32, wide), lambda t, *_: (0, t))],
        [((per * 32, width), BF16)],
        (places, *pieces),
        moved=4 * per * 32 * width,
        prefetch=1,
    )
    return out


def total_of(*terms):
    total = terms[0].astype(F32)
    for term in terms[1:]:
        total = total + term.astype(F32)
    return total


AXES = ("z", "core", "seq")


class Ring:
    def __init__(self, mesh):
        self.count = mesh.size
        self.seq, self.z, self.c = (lax.axis_index(a) for a in ("seq", "z", "core"))
        self.x, self.y = (self.seq % 2, self.seq // 2)

    def swap(self, array, bits):
        return lax.ppermute(array, AXES, [(i, i ^ bits) for i in range(self.count)])


class Gather:
    def __init__(self, ring, shard):
        self.ring = ring
        self.hold = [shard] * 3
        self.own = shard
        self.bits = (8, 16, 24)

    def launch(self):
        self.hold = [self.ring.swap(array, bits) for array, bits in zip(self.hold, self.bits)]

    def near(self):
        self.pair = [jnp.stack([self.own, self.hold[0]]), jnp.stack(self.hold[1:])]
        self.hold, self.bits = (list(self.pair), (1, 2))

    def far(self):
        self.pair = [jnp.stack([mine, came]) for mine, came in zip(self.pair, self.hold)]
        self.hold, self.bits = (list(self.pair), (2, 1))

    def core(self):
        self.quad = [self.pair[0], self.hold[0], self.pair[1], self.hold[1]]
        self.hold, self.bits = (list(self.quad), (4,) * 4)

    def done(self, places):
        return put_in_order(places, self.quad + self.hold)


class Steps:
    def __init__(self, ring, halves):
        self.ring = ring
        shape = (2, 2, 2, 2, halves[0].shape[0] // 16, halves[0].shape[1])
        sent, self.kept = (half.reshape(shape) for half in halves)
        self.hold, self.bits = ([sent], (4,))

    def launch(self):
        self.hold = [self.ring.swap(array, bits) for array, bits in zip(self.hold, self.bits)]

    def near(self):
        (self.got,) = self.hold
        self.bits = (2, 1)
        self.hold = [total_of(self.kept[i, 1], self.got[i, 1]).astype(BF16) for i in range(2)]

    def far(self):
        parts = [(self.kept[i, 0], self.got[i, 0], self.hold[i]) for i in range(2)]
        self.bits = (1, 2)
        self.hold = [total_of(*(p[1] for p in parts[i])).astype(BF16) for i in range(2)]
        self.parts = [total_of(*(p[0] for p in parts[i])).astype(BF16) for i in range(2)]

    def deep(self):
        parts = [(self.parts[i], self.hold[i]) for i in range(2)]
        self.result = total_of(*(p[0] for p in parts[0]))
        self.bits = (8, 16, 24)
        self.hold = [
            total_of(*(p[step % 2] for p in parts[step // 2])).astype(BF16) for step in (1, 2, 3)
        ]

    def scatter(self):
        parts = [total_of(self.parts[i], self.hold[i]).astype(BF16) for i in range(2)]
        self.hold = [jnp.concatenate(parts).reshape(-1, self.kept.shape[-1])]

    def launch_scatter(self):
        self.result = lax.psum_scatter(self.hold[0], "z", scatter_dimension=0, tiled=True)
        self.hold = []

    def done(self):
        return total_of(self.result, *self.hold)


def at_once(*groups):
    arrays = [group if isinstance(group, list) else group.hold for group in groups]
    arrays = lax.optimization_barrier(arrays)
    for group, values in zip(groups, arrays):
        if isinstance(group, list):
            group[:] = values
        else:
            group.hold = list(values)


def whole_images(mesh, *args):
    (
        image_tokens, text_states, text_lengths, out_grad, norm1_gain, norm1_bias, self_qkv,
        self_bias_qv, self_out, self_out_bias, norm2_gain, norm2_bias, cross_query, cross_kv,
        cross_bias_qv, cross_out, cross_out_bias, norm3_gain, norm3_bias, mlp_in, mlp_in_bias,
        mlp_out, mlp_out_bias,
    ) = args
    n_seq = mesh.shape["seq"]
    ring = Ring(mesh)
    part, text_part = (image_tokens.shape[1], text_states.shape[1])
    rows = norm1_gain.shape[0]
    fours = mlp_out.shape[0] // rows
    length, prompt = (part * n_seq, text_part * n_seq)
    places = jnp.stack([ring.z, ring.c, ring.y, ring.x]).astype(jnp.int32)
    flat_places = places * jnp.array([0, 1, 1, 1], jnp.int32)

    def gather(shard):
        return lax.all_gather(shard, AXES, axis=0, tiled=True)

    def across(vectors):
        return jnp.concatenate([v.reshape(ring.count, -1) for v in vectors], axis=1)

    def line(*vectors):
        table = jnp.stack(vectors)
        return jnp.pad(table, ((0, -len(vectors) % 8), (0, 0)))

    in_shard = mlp_in.reshape(rows, ring.count, fours, rows).transpose(0, 2, 1, 3).reshape(rows, -1)
    out_shard = mlp_out.reshape(fours, rows, D).transpose(1, 0, 2).reshape(rows, -1)
    mlp = gather(jnp.concatenate([in_shard, out_shard], axis=1))
    vectors = [
        norm1_gain, norm1_bias, self_out_bias, norm2_gain, norm2_bias, cross_out_bias,
        norm3_gain, norm3_bias, mlp_out_bias, self_bias_qv, cross_bias_qv, mlp_in_bias,
    ]
    strip = jnp.concatenate(vectors).reshape(-1, rows)
    strip = jnp.pad(strip, ((0, 128 - strip.shape[0]), (0, 0))).T
    w_first = Gather(ring, jnp.concatenate([self_qkv, strip], axis=1))
    w_second = Gather(
        ring, jnp.concatenate([self_out, cross_query, cross_kv, cross_out], axis=1)
    )
    w_first.launch()
    now = [
        lax.all_to_all(
            jnp.concatenate([image_tokens, text_states], axis=1), "seq", 0, 0, tiled=True
        )
    ]
    at_once(now, w_first)
    (moved,) = now
    w_first.near()
    at_once(w_first, w_second)
    w_first.launch()
    w_second.launch()
    at_once(w_first)
    w_first.far()
    w_first.launch()
    at_once(w_first, w_second)
    w_first.core()
    w_second.near()
    at_once(w_first, w_second)
    w_first.launch()
    w_second.launch()
    at_once(w_first)
    first = w_first.done(places)

    texts = moved[:, part:].reshape(prompt, D)
    prompt_length = lax.dynamic_slice_in_dim(text_lengths, ring.seq, 1, 0)

    table = lax.optimization_barrier(first[:, 3 * D :]).T.astype(F32)
    full, at = ([], 0)
    for v in vectors[:-1]:
        wide = v.shape[0] // rows
        full.append(table[at : at + wide].reshape(wide, -1, rows).transpose(1, 0, 2).reshape(-1))
        at += wide
    bias_in = table[at : at + fours].reshape(fours, 1, D)
    (g1, b1, bias_out, g2, b2, bias_cross, g3, b3, bias_last, bias_qv, bias_qv2) = full
    zero = jnp.zeros((D,), F32)

    tile = part
    grid = (n_seq,)
    row_tile = pl.BlockSpec((tile, D), lambda i, *_: (i, 0))
    token_tile = pl.BlockSpec((1, tile, D), lambda i, *_: (i, 0, 0))
    vec8, vec1 = (whole((8, D)), whole((1, D)))
    sum8 = pl.BlockSpec((8, D), lambda *_: (0, 0))
    square = (D, D)
    flat = (length, D)

    def weight_block(index):
        return whole(square, (0, index))

    def streamed(offset):
        return pl.BlockSpec(square, lambda t, *_: (0, t + offset))

    def columns(width):
        return pl.BlockSpec((tile, width), lambda i, *_: (i, 0))

    stat_tile = pl.BlockSpec((HEADS, tile), lambda i, *_: (0, i))
    unit = 2 * length * D * D

    h1, qkv = kernel_call(
        qkv_kernel, "qkv", grid,
        [token_tile, whole((D, 3 * D)), vec8],
        [row_tile, columns(3 * D)],
        [(flat, BF16), ((length, 3 * D), BF16)],
        (moved, first, line(g1, b1, bias_qv[:D], zero, bias_qv[D:])),
        flops=3 * unit, moved=16 * length * D,
    )
    now = [qkv, h1]
    at_once(now, w_second)
    w_second.far()
    at_once(now, w_second)
    qkv, h1 = now
    w_second.launch()
    o1, lse1 = attend(qkv)
    now = [o1]
    at_once(now, w_second)
    w_second.core()
    w_second.launch()
    at_once(now, w_second)
    (o1,) = now
    second = w_second.done(places)
    kv2 = (mm(texts, second[:, 2 * D : 4 * D]) + jnp.concatenate([zero, bias_qv2[D:]])).astype(BF16)
    x1, h2, q2, o2, x2, h3, lse2 = kernel_call(
        cross_kernel, "cross", grid,
        [token_tile, row_tile, weight_block(0), weight_block(1), weight_block(4),
         whole((prompt, 2 * D)), vec8],
        [row_tile] * 6 + [stat_tile],
        [(flat, F32), (flat, BF16), (flat, BF16), (flat, BF16), (flat, F32), (flat, BF16),
         ((HEADS, length), F32)],
        (prompt_length, moved, o1, second, second, second, kv2,
         line(bias_out, g2, b2, bias_qv2[:D], bias_cross, g3, b3)),
        flops=5 * unit, moved=30 * length * D, prefetch=1,
    )
    out_grad, h3 = lax.optimization_barrier((out_grad, h3))
    grad_rows = lax.all_to_all(out_grad, "seq", 0, 0, tiled=True).reshape(flat)
    hidden = (length, fours * D)
    by_unit = pl.BlockSpec((length, D), lambda t, *_: (0, t))
    act, slope, out = kernel_call(
        mlp_kernel, "mlp", (fours,),
        [whole(flat), streamed(0), streamed(fours),
         pl.BlockSpec((1, 1, D), lambda t, *_: (t, 0, 0)), whole(flat), vec1],
        [by_unit, by_unit, whole(flat, single=False)],
        [(hidden, BF16), (hidden, BF16), (flat, BF16)],
        (h3, mlp, mlp, bias_in, x2, bias_last.reshape(1, D)),
        scratch=[pltpu.VMEM(flat, F32)],
        flops=2 * fours * unit, moved=40 * length * D,
    )

    full_flat = whole(flat)
    r_out = Steps(
        ring,
        weight_grads(
            flat_places, (act, grad_rows), [by_unit, full_flat], [(0, 1)] * fours, D, "d_mlp_out"
        ),
    )
    now = [out, slope, grad_rows]
    at_once(now, r_out)
    out, slope, grad_rows = now
    leaving_out = [lax.all_to_all(out.reshape(n_seq, part, D), "seq", 0, 0, tiled=True)]
    r_out.launch()
    du, du_sum = kernel_call(
        du_kernel, "du", (fours,),
        [full_flat, streamed(fours), by_unit],
        [by_unit, pl.BlockSpec((1, 1, D), lambda t, *_: (t, 0, 0))],
        [(hidden, BF16), ((fours, 1, D), F32)],
        (grad_rows, mlp, slope),
        flops=fours * unit, moved=26 * length * D,
    )
    now = [du, h3]
    at_once(now, r_out)
    r_out.near()
    at_once(now, r_out)
    r_out.launch()
    du, h3 = now
    r_in = Steps(
        ring,
        weight_grads(flat_places, (h3, du), [full_flat, by_unit], [(0, 1)] * fours, D, "d_mlp_in"),
    )
    now = [du]
    at_once(now, leaving_out, r_in)
    (du,) = now
    (block_output,) = leaving_out
    r_in.launch()
    dx2, dc, do2, sums3 = kernel_call(
        norm3_kernel, "norm3_back", grid,
        [columns(fours * D), whole((D, fours * D)), row_tile, row_tile, vec1, weight_block(4)],
        [row_tile] * 3 + [sum8],
        [(flat, F32), (flat, BF16), (flat, BF16), ((8, D), F32)],
        (du, mlp, grad_rows, x2, g3.reshape(1, D), second),
        flops=(fours + 1) * unit, moved=32 * length * D,
    )
    now = [dx2, dc, do2]
    at_once(now, r_in, r_out)
    r_out.far()
    r_in.near()
    at_once(now, r_in, r_out)
    r_out.launch()
    r_in.launch()
    dx2, dc, do2 = now
    dq2, dkv2, dx1, da, do1, sums2 = kernel_call(
        cross_back_kernel, "cross_back", grid,
        [row_tile, whole((prompt, 2 * D)), row_tile, row_tile, stat_tile,
         weight_block(1), weight_block(0), row_tile, row_tile, vec1],
        [row_tile, whole((prompt, 2 * D), single=False), row_tile, row_tile, row_tile, sum8],
        [(flat, BF16), ((prompt, 2 * D), BF16), (flat, F32), (flat, BF16), (flat, BF16), ((8, D), F32)],
        (prompt_length, q2, kv2, o2, do2, lse2, second, second, x1, dx2, g2.reshape(1, D)),
        scratch=[pltpu.VMEM((prompt, 2 * D), F32)],
        flops=5 * unit, moved=34 * length * D, prefetch=1,
    )
    text_block = [whole((prompt, D), (0, i)) for i in range(2)]
    r_mid = Steps(
        ring,
        weight_grads(
            places,
            (o1, da, o2, dc, h2, dq2, texts, dkv2, dkv2),
            [full_flat] * 6 + [whole((prompt, D))] + text_block,
            [(0, 1), (2, 3), (4, 5), (6, 7), (6, 8)],
            D,
            "d_mid",
        ),
    )
    now = [do1, dx1, dkv2]
    at_once(now, r_mid, r_in, r_out)
    r_in.far()
    r_out.scatter()
    at_once(now, r_mid, r_in, r_out)
    do1, dx1, dkv2 = now
    r_mid.launch()
    r_in.launch()
    r_out.launch_scatter()
    count = HEADS // 4
    back_a = list(attend_back(qkv, o1, do1, lse1, 0, count))
    now = [do1]
    at_once(now, back_a, r_mid, r_in)
    r_mid.near()
    r_in.scatter()
    at_once(now, back_a, r_mid, r_in)
    (do1,) = now
    r_mid.launch()
    r_in.launch_scatter()
    back_b = list(attend_back(qkv, o1, do1, lse1, count, count))
    narrow = [full_flat] + [whole((length, count * PAIR))] * 6
    r_qkv = Steps(
        ring,
        weight_grads(
            places, (h1, *back_a, *back_b), narrow, [(0, 1 + i) for i in range(6)],
            count * PAIR, "d_qkv",
        ),
    )
    at_once(back_b, r_qkv, r_mid)
    r_qkv.launch()
    r_mid.far()
    dv2_sum = jnp.sum(dkv2[:, D:].astype(F32), axis=0)
    early = [
        sums2[2], sums2[0], sums2[1], sums3[2], sums3[0], sums3[1], sums3[3],
        jnp.concatenate([sums2[3], dv2_sum]),
        du_sum.reshape(fours, ring.count, rows).transpose(1, 0, 2).reshape(-1),
    ]
    early = [across(early)]
    text_grad = mm(dkv2, second[:, 2 * D : 4 * D], NT).astype(BF16)
    now = [text_grad]
    at_once(back_b, r_qkv, r_mid, early, now)
    r_mid.launch()
    r_qkv.near()
    at_once(back_b, r_qkv, early, now)
    (text_grad,) = now
    r_qkv.launch()
    leaving, sums1 = kernel_call(
        norm1_kernel, "norm1_back", grid,
        [columns(count * PAIR)] * 6 + [whole((D, 3 * D)), token_tile, row_tile, vec1]
        + [pl.BlockSpec((text_part, D), lambda i, *_: (i, 0))],
        [pl.BlockSpec((1, part + text_part, D), lambda i, *_: (i, 0, 0)), sum8],
        [(moved.shape, BF16), ((8, D), F32)],
        (*back_a, *back_b, first, moved, dx1, g1.reshape(1, D), text_grad),
        flops=3 * unit, moved=18 * length * D,
    )
    leaving = [lax.all_to_all(leaving, "seq", 0, 0, tiled=True)]
    at_once(r_qkv, r_mid)
    r_qkv.far()
    r_mid.deep()
    at_once(r_qkv, r_mid)
    r_qkv.launch()
    r_mid.launch()
    late = [across([sums1[0], sums1[1], jnp.concatenate([sums1[2], sums1[3]])])]
    mlp_out_grad = r_out.done().reshape(rows, fours, D).transpose(1, 0, 2).reshape(-1, D)
    mlp_in_grad = r_in.done().reshape(rows, fours, ring.count, rows)
    mlp_in_grad = mlp_in_grad.transpose(0, 2, 1, 3).reshape(rows, -1)
    now = [mlp_out_grad, mlp_in_grad]
    at_once(r_qkv, r_mid, late, leaving, now)
    mlp_out_grad, mlp_in_grad = now
    r_qkv.deep()
    at_once(r_qkv, late, early)
    r_qkv.launch()
    small = jnp.concatenate([early[0], late[0]], axis=1)
    small = jnp.sum(lax.all_to_all(small, AXES, 0, 0, tiled=True), axis=0)
    leaving = leaving[0].astype(F32)
    mid, last = (r_mid.done(), r_qkv.done())
    wide = count * PAIR
    self_qkv_grad = jnp.concatenate(
        [last[:, (3 * j + i) * wide : (3 * j + i + 1) * wide] for i in range(3) for j in range(2)],
        axis=1,
    )

    def mine(total, at, wide):
        return total[at * rows : at * rows + wide]

    two = 2 * rows
    return (
        block_output,
        leaving[:, :part],
        leaving[:, part:],
        mine(small, 9 + fours, rows),
        mine(small, 10 + fours, rows),
        self_qkv_grad,
        mine(small, 11 + fours, two),
        mid[:, :D],
        mine(small, 0, rows),
        mine(small, 1, rows),
        mine(small, 2, rows),
        mid[:, 2 * D : 3 * D],
        mid[:, 3 * D :],
        mine(small, 7, two),
        mid[:, D : 2 * D],
        mine(small, 3, rows),
        mine(small, 4, rows),
        mine(small, 5, rows),
        mlp_in_grad,
        mine(small, 9, fours * rows),
        mlp_out_grad,
        mine(small, 6, rows),
    )


def places_of(images, rows):
    ins = (
        P(images, "seq", None),
        P(images, "seq", None),
        P(images),
        P(images, "seq", None),
        P(rows),
        P(rows),
        P(rows, None),
        P(rows),
        P(rows, None),
        P(rows),
        P(rows),
        P(rows),
        P(rows, None),
        P(rows, None),
        P(rows),
        P(rows, None),
        P(rows),
        P(rows),
        P(rows),
        P(rows, None),
        P(rows),
        P(rows, None),
        P(rows),
    )
    outs = (
            P(images, "seq", None),
            P(images, "seq", None),
            P(images, "seq", None),
            P(rows),
            P(rows),
            P(rows, None),
            P(rows),
            P(rows, None),
            P(rows),
            P(rows),
            P(rows),
            P(rows, None),
            P(rows, None),
            P(rows),
            P(rows, None),
            P(rows),
            P(rows),
            P(rows),
            P(rows, None),
            P(rows),
            P(rows, None),
            P(rows),
        )
    return (ins, outs)


def solution(mesh):
    n_dp, n_seq = (mesh.shape["dp"], mesh.shape["seq"])
    spread = places_of("dp", ("dp", "seq"))
    single = places_of(("z", "core"), AXES)

    def layer(*args):
        images = args[0].shape[0] // n_dp
        if images == n_seq and (n_dp, n_seq) == (8, 4):
            fine = Mesh(mesh.devices.reshape(n_dp // 2, 2, n_seq), AXES)
            plan, place, grid = (functools.partial(whole_images, fine), single, fine)
        else:
            plan, place, grid = (per_device, spread, mesh)
        return jax.shard_map(
            plan, mesh=grid, in_specs=place[0], out_specs=place[1], check_vma=False
        )(*args)

    return layer
```

```python
import functools
import itertools

import jax
import jax.numpy as jnp
from jax import lax
from jax.experimental import pallas as pl
from jax.experimental.pallas import tpu as pltpu
from jax.sharding import Mesh
from jax.sharding import PartitionSpec as P

D = 1024
HEADS = 16
HEAD_DIM = 64


EPSILON = 1e-05
SCALING = 0.125
NEGATIVE = -1e30
VMEM = 56 * 1024 * 1024


def layer_norm(values, gain, shift):
    center = values - jnp.mean(values, axis=-1, keepdims=True)
    inverse = lax.rsqrt(jnp.mean(center * center, axis=-1, keepdims=True) + EPSILON)
    normed = center * inverse
    return (normed * gain + shift, normed, inverse)


def norm_back(grad_rows, normed, inverse, gain):
    scaled = grad_rows * gain
    back = inverse * (
        scaled
        - jnp.mean(scaled, axis=-1, keepdims=True)
        - normed * jnp.mean(scaled * normed, axis=-1, keepdims=True)
    )
    return (back, jnp.sum(grad_rows * normed, axis=(0, 1)), jnp.sum(grad_rows, axis=(0, 1)))


def project(left, weight):
    return jnp.einsum("bld,de->ble", left, weight, preferred_element_type=jnp.float32)


def project_back(grad_rows, weight):
    return jnp.einsum("ble,de->bld", grad_rows, weight, preferred_element_type=jnp.float32)


def weight_grad(left, grad_rows):
    return jnp.einsum("bld,ble->de", left, grad_rows, preferred_element_type=jnp.float32)


def column_sums(grad_rows):
    return jnp.sum(grad_rows.astype(jnp.float32), axis=(0, 1))


def split_heads(rows):
    return rows.reshape(rows.shape[0], rows.shape[1], HEADS, HEAD_DIM)


def gelu_tanh(values):
    return jax.nn.gelu(values, approximate=True)


def block_scores(queries, key_rows, start, width, mask_at):
    key_block = split_heads(lax.dynamic_slice_in_dim(key_rows, start, width, 1))
    scores = (
        jnp.einsum("bqhd,bkhd->bhqk", queries, key_block, preferred_element_type=jnp.float32)
        * SCALING
    )
    return (jnp.where(mask_at(start, width), scores, NEGATIVE), key_block)


def spread_attend(query_rows, key_rows, value_rows, mask_at, width):
    queries = split_heads(query_rows)
    batch_size, length = (query_rows.shape[0], query_rows.shape[1])
    blocks = key_rows.shape[1] // width

    def stats(block_index, carry):
        running_max, running_sum = carry
        scores, key_block = block_scores(queries, key_rows, block_index * width, width, mask_at)
        new_max = jnp.maximum(running_max, jnp.max(scores, axis=-1))
        running_sum = running_sum * jnp.exp(running_max - new_max) + jnp.sum(
            jnp.exp(scores - new_max[..., None]), axis=-1
        )
        return (new_max, running_sum)

    start_max = jnp.full((batch_size, HEADS, length), NEGATIVE, jnp.float32)
    final_max, final_sum = lax.fori_loop(0, blocks, stats, (start_max, jnp.zeros_like(start_max)))
    log_total = final_max + jnp.log(final_sum)

    def accumulate(block_index, total):
        start = block_index * width
        scores, key_block = block_scores(queries, key_rows, start, width, mask_at)
        weights = jnp.exp(scores - log_total[..., None]).astype(jnp.bfloat16)
        value_block = split_heads(lax.dynamic_slice_in_dim(value_rows, start, width, 1))
        return total + jnp.einsum(
            "bhqk,bkhd->bqhd", weights, value_block, preferred_element_type=jnp.float32
        )

    total = lax.fori_loop(
        0, blocks, accumulate, jnp.zeros((batch_size, length, HEADS, HEAD_DIM), jnp.float32)
    )
    return (total.reshape(batch_size, length, HEADS * HEAD_DIM).astype(jnp.bfloat16), log_total)


def spread_attend_back(query_rows, key_rows, value_rows, grad_rows, log_total, mask_at, width):
    queries = split_heads(query_rows)
    grad_heads = split_heads(grad_rows)
    batch_size, length = (query_rows.shape[0], query_rows.shape[1])
    blocks = key_rows.shape[1] // width

    def weights_at(start):
        scores, key_block = block_scores(queries, key_rows, start, width, mask_at)
        value_block = split_heads(lax.dynamic_slice_in_dim(value_rows, start, width, 1))
        probs = jnp.exp(scores - log_total[..., None])
        grad_probs = jnp.einsum(
            "bqhd,bkhd->bhqk", grad_heads, value_block, preferred_element_type=jnp.float32
        )
        return (probs, grad_probs, key_block)

    def inner(block_index, delta):
        probs, grad_probs, key_block = weights_at(block_index * width)
        return delta + jnp.sum(probs * grad_probs, axis=-1)

    delta = lax.fori_loop(0, blocks, inner, jnp.zeros((batch_size, HEADS, length), jnp.float32))
    start_grad = jnp.zeros((batch_size, length, HEADS, HEAD_DIM), jnp.float32)

    def step(grad_queries, block_index):
        probs, grad_probs, key_block = weights_at(block_index * width)
        grad_scores = (probs * (grad_probs - delta[..., None])).astype(jnp.bfloat16)
        grad_queries = grad_queries + jnp.einsum(
            "bhqk,bkhd->bqhd", grad_scores, key_block, preferred_element_type=jnp.float32
        )
        grad_keys = jnp.einsum(
            "bhqk,bqhd->bkhd", grad_scores, queries, preferred_element_type=jnp.float32
        )
        grad_values = jnp.einsum(
            "bhqk,bqhd->bkhd",
            probs.astype(jnp.bfloat16),
            grad_heads,
            preferred_element_type=jnp.float32,
        )
        return (grad_queries, (grad_keys, grad_values))

    grad_queries, (key_parts, value_parts) = lax.scan(
        step, start_grad, jnp.arange(blocks, dtype=jnp.int32)
    )

    def merge_blocks(parts):
        return jnp.moveaxis(parts, 0, 1).reshape(batch_size, blocks * width, HEADS * HEAD_DIM)

    return (
        (grad_queries * SCALING).reshape(batch_size, length, HEADS * HEAD_DIM),
        merge_blocks(key_parts) * SCALING,
        merge_blocks(value_parts),
        delta,
    )


def gather_self(gain, shift, weight_qkv, bias_qv, weight_out, bias_out):
    return (
        lax.all_gather(gain, ("dp", "seq"), axis=0, tiled=True),
        lax.all_gather(shift, ("dp", "seq"), axis=0, tiled=True),
        lax.all_gather(weight_qkv, ("dp", "seq"), axis=0, tiled=True),
        lax.all_gather(bias_qv, ("dp", "seq"), axis=0, tiled=True),
        lax.all_gather(weight_out, ("dp", "seq"), axis=0, tiled=True),
        lax.all_gather(bias_out, ("dp", "seq"), axis=0, tiled=True),
    )


def gather_cross(gain, shift, weight_query, weight_kv, bias_qv, weight_out, bias_out):
    return (
        lax.all_gather(gain, ("dp", "seq"), axis=0, tiled=True),
        lax.all_gather(shift, ("dp", "seq"), axis=0, tiled=True),
        lax.all_gather(weight_query, ("dp", "seq"), axis=0, tiled=True),
        lax.all_gather(weight_kv, ("dp", "seq"), axis=0, tiled=True),
        lax.all_gather(bias_qv, ("dp", "seq"), axis=0, tiled=True),
        lax.all_gather(weight_out, ("dp", "seq"), axis=0, tiled=True),
        lax.all_gather(bias_out, ("dp", "seq"), axis=0, tiled=True),
    )


def gather_mlp(gain, shift, weight_in, bias_in, weight_out, bias_out):
    return (
        lax.all_gather(gain, ("dp", "seq"), axis=0, tiled=True),
        lax.all_gather(shift, ("dp", "seq"), axis=0, tiled=True),
        lax.all_gather(weight_in, ("dp", "seq"), axis=0, tiled=True),
        lax.all_gather(bias_in, ("dp", "seq"), axis=0, tiled=True),
        lax.all_gather(weight_out, ("dp", "seq"), axis=0, tiled=True),
        lax.all_gather(bias_out, ("dp", "seq"), axis=0, tiled=True),
    )


def per_device(
    image_tokens,
    text_states,
    text_lengths,
    out_grad,
    norm1_gain,
    norm1_bias,
    self_qkv,
    self_bias_qv,
    self_out,
    self_out_bias,
    norm2_gain,
    norm2_bias,
    cross_query,
    cross_kv,
    cross_bias_qv,
    cross_out,
    cross_out_bias,
    norm3_gain,
    norm3_bias,
    mlp_in,
    mlp_in_bias,
    mlp_out,
    mlp_out_bias,
):
    length = image_tokens.shape[1]
    own_start = lax.axis_index("seq") * length
    query_pos = own_start + jnp.arange(length, dtype=jnp.int32)

    def causal_at(start, width):
        key_pos = start + jnp.arange(width, dtype=jnp.int32)
        return (key_pos[None, :] <= query_pos[:, None])[None, None]

    def padded_at(start, width):
        key_pos = start + jnp.arange(width, dtype=jnp.int32)
        return (key_pos[None, :] < text_lengths[:, None])[:, None, None, :]

    self_full = gather_self(norm1_gain, norm1_bias, self_qkv, self_bias_qv, self_out, self_out_bias)
    residual = image_tokens.astype(jnp.float32)
    normed_in, normed_one, inverse_one = layer_norm(
        residual, self_full[0].astype(jnp.float32), self_full[1].astype(jnp.float32)
    )
    hidden_one = normed_in.astype(jnp.bfloat16)
    mixed = project(hidden_one, self_full[2])
    bias_self = self_full[3].astype(jnp.float32)
    query_one = (mixed[..., :D] + bias_self[:D]).astype(jnp.bfloat16)
    key_one = mixed[..., D : 2 * D].astype(jnp.bfloat16)
    value_one = (mixed[..., 2 * D :] + bias_self[D:]).astype(jnp.bfloat16)
    key_all, value_all = (
        lax.all_gather(key_one, "seq", axis=1, tiled=True),
        lax.all_gather(value_one, "seq", axis=1, tiled=True),
    )
    self_width = min(128, key_all.shape[1])
    attended, log_one = spread_attend(query_one, key_all, value_all, causal_at, self_width)
    after_self = residual + project(attended, self_full[4]) + self_full[5].astype(jnp.float32)
    cross_full = gather_cross(
        norm2_gain, norm2_bias, cross_query, cross_kv, cross_bias_qv, cross_out, cross_out_bias
    )
    normed_mid, normed_two, inverse_two = layer_norm(
        after_self, cross_full[0].astype(jnp.float32), cross_full[1].astype(jnp.float32)
    )
    hidden_two = normed_mid.astype(jnp.bfloat16)
    bias_cross = cross_full[4].astype(jnp.float32)
    query_two = (project(hidden_two, cross_full[2]) + bias_cross[:D]).astype(jnp.bfloat16)
    text_mixed = project(text_states, cross_full[3])
    text_key = text_mixed[..., :D].astype(jnp.bfloat16)
    text_value = (text_mixed[..., D:] + bias_cross[D:]).astype(jnp.bfloat16)
    key_two, value_two = (
        lax.all_gather(text_key, "seq", axis=1, tiled=True),
        lax.all_gather(text_value, "seq", axis=1, tiled=True),
    )
    text_width = key_two.shape[1]
    attended_two, log_two = spread_attend(query_two, key_two, value_two, padded_at, text_width)
    after_cross = (
        after_self + project(attended_two, cross_full[5]) + cross_full[6].astype(jnp.float32)
    )
    mlp_full = gather_mlp(norm3_gain, norm3_bias, mlp_in, mlp_in_bias, mlp_out, mlp_out_bias)
    normed_last, normed_three, inverse_three = layer_norm(
        after_cross, mlp_full[0].astype(jnp.float32), mlp_full[1].astype(jnp.float32)
    )
    hidden_three = normed_last.astype(jnp.bfloat16)
    pre_act = project(hidden_three, mlp_full[2]) + mlp_full[3].astype(jnp.float32)
    activated, gelu_back = jax.vjp(gelu_tanh, pre_act)
    act_low = activated.astype(jnp.bfloat16)
    block_output = (
        after_cross + project(act_low, mlp_full[4]) + mlp_full[5].astype(jnp.float32)
    ).astype(jnp.bfloat16)
    mlp_back = gather_mlp(norm3_gain, norm3_bias, mlp_in, mlp_in_bias, mlp_out, mlp_out_bias)
    grad_top = out_grad.astype(jnp.float32)
    w_out_grad = weight_grad(act_low, out_grad)
    b_out_grad = column_sums(out_grad)
    grad_act = project_back(out_grad, mlp_back[4])
    grad_pre = gelu_back(grad_act)[0].astype(jnp.bfloat16)
    w_in_grad = weight_grad(hidden_three, grad_pre)
    b_in_grad = column_sums(grad_pre)
    back_three, gain_three_grad, shift_three_grad = norm_back(
        project_back(grad_pre, mlp_back[2]),
        normed_three,
        inverse_three,
        mlp_back[0].astype(jnp.float32),
    )
    grad_two = grad_top + back_three
    mlp_grads = (
        lax.psum_scatter(gain_three_grad, ("dp", "seq"), scatter_dimension=0, tiled=True),
        lax.psum_scatter(shift_three_grad, ("dp", "seq"), scatter_dimension=0, tiled=True),
        lax.psum_scatter(w_in_grad, ("dp", "seq"), scatter_dimension=0, tiled=True),
        lax.psum_scatter(b_in_grad, ("dp", "seq"), scatter_dimension=0, tiled=True),
        lax.psum_scatter(w_out_grad, ("dp", "seq"), scatter_dimension=0, tiled=True),
        lax.psum_scatter(b_out_grad, ("dp", "seq"), scatter_dimension=0, tiled=True),
    )
    cross_back = gather_cross(
        norm2_gain, norm2_bias, cross_query, cross_kv, cross_bias_qv, cross_out, cross_out_bias
    )
    grad_cross = grad_two.astype(jnp.bfloat16)
    cross_out_term = weight_grad(attended_two, grad_cross)
    cross_bias_term = column_sums(grad_cross)
    grad_att_two = project_back(grad_cross, cross_back[5]).astype(jnp.bfloat16)
    grad_query_two, grad_key_two, grad_value_two, delta_two = spread_attend_back(
        query_two, key_two, value_two, grad_att_two, log_two, padded_at, text_width
    )
    query_two_low = grad_query_two.astype(jnp.bfloat16)
    text_key_grad, text_value_grad = (
        lax.psum_scatter(
            grad_key_two.astype(jnp.bfloat16), "seq", scatter_dimension=1, tiled=True
        ).astype(jnp.float32),
        lax.psum_scatter(
            grad_value_two.astype(jnp.bfloat16), "seq", scatter_dimension=1, tiled=True
        ).astype(jnp.float32),
    )
    text_value_low = text_value_grad.astype(jnp.bfloat16)
    text_kv_grad = jnp.concatenate([text_key_grad.astype(jnp.bfloat16), text_value_low], axis=-1)
    cross_query_term = weight_grad(hidden_two, query_two_low)
    cross_kv_term = weight_grad(text_states, text_kv_grad)
    cross_qv_term = jnp.concatenate([column_sums(query_two_low), column_sums(text_value_low)])
    text_grad = project_back(text_kv_grad, cross_back[3])
    back_two, gain_two_grad, shift_two_grad = norm_back(
        project_back(query_two_low, cross_back[2]),
        normed_two,
        inverse_two,
        cross_back[0].astype(jnp.float32),
    )
    grad_one = grad_two + back_two
    cross_grads = (
        lax.psum_scatter(gain_two_grad, ("dp", "seq"), scatter_dimension=0, tiled=True),
        lax.psum_scatter(shift_two_grad, ("dp", "seq"), scatter_dimension=0, tiled=True),
        lax.psum_scatter(cross_query_term, ("dp", "seq"), scatter_dimension=0, tiled=True),
        lax.psum_scatter(cross_kv_term, ("dp", "seq"), scatter_dimension=0, tiled=True),
        lax.psum_scatter(cross_qv_term, ("dp", "seq"), scatter_dimension=0, tiled=True),
        lax.psum_scatter(cross_out_term, ("dp", "seq"), scatter_dimension=0, tiled=True),
        lax.psum_scatter(cross_bias_term, ("dp", "seq"), scatter_dimension=0, tiled=True),
    )
    self_back = gather_self(norm1_gain, norm1_bias, self_qkv, self_bias_qv, self_out, self_out_bias)
    grad_self = grad_one.astype(jnp.bfloat16)
    self_out_term = weight_grad(attended, grad_self)
    self_bias_term = column_sums(grad_self)
    grad_att_one = project_back(grad_self, self_back[4]).astype(jnp.bfloat16)
    grad_query_one, grad_key_all, grad_value_all, delta_one = spread_attend_back(
        query_one, key_all, value_all, grad_att_one, log_one, causal_at, self_width
    )
    grad_key_one, grad_value_one = (
        lax.psum_scatter(
            grad_key_all.astype(jnp.bfloat16), "seq", scatter_dimension=1, tiled=True
        ).astype(jnp.float32),
        lax.psum_scatter(
            grad_value_all.astype(jnp.bfloat16), "seq", scatter_dimension=1, tiled=True
        ).astype(jnp.float32),
    )
    query_one_low = grad_query_one.astype(jnp.bfloat16)
    value_one_low = grad_value_one.astype(jnp.bfloat16)
    grad_qkv = jnp.concatenate(
        [query_one_low, grad_key_one.astype(jnp.bfloat16), value_one_low], axis=-1
    )
    self_qkv_term = weight_grad(hidden_one, grad_qkv)
    self_qv_term = jnp.concatenate([column_sums(query_one_low), column_sums(value_one_low)])
    back_one, gain_one_grad, shift_one_grad = norm_back(
        project_back(grad_qkv, self_back[2]),
        normed_one,
        inverse_one,
        self_back[0].astype(jnp.float32),
    )
    image_grad = grad_one + back_one
    self_grads = (
        lax.psum_scatter(gain_one_grad, ("dp", "seq"), scatter_dimension=0, tiled=True),
        lax.psum_scatter(shift_one_grad, ("dp", "seq"), scatter_dimension=0, tiled=True),
        lax.psum_scatter(self_qkv_term, ("dp", "seq"), scatter_dimension=0, tiled=True),
        lax.psum_scatter(self_qv_term, ("dp", "seq"), scatter_dimension=0, tiled=True),
        lax.psum_scatter(self_out_term, ("dp", "seq"), scatter_dimension=0, tiled=True),
        lax.psum_scatter(self_bias_term, ("dp", "seq"), scatter_dimension=0, tiled=True),
    )
    return (
        block_output,
        image_grad,
        text_grad,
        self_grads[0],
        self_grads[1],
        self_grads[2],
        self_grads[3],
        self_grads[4],
        self_grads[5],
        cross_grads[0],
        cross_grads[1],
        cross_grads[2],
        cross_grads[3],
        cross_grads[4],
        cross_grads[5],
        cross_grads[6],
        mlp_grads[0],
        mlp_grads[1],
        mlp_grads[2],
        mlp_grads[3],
        mlp_grads[4],
        mlp_grads[5],
    )


LOG2E = 1.4426950408889634
LN2 = 0.6931471805599453
QB = 256
PAIR = 2 * HEAD_DIM
NT = (((1,), (1,)), ((), ()))
NN = (((1,), (0,)), ((), ()))
TN = (((0,), (0,)), ((), ()))
BF16 = jnp.bfloat16
F32 = jnp.float32


def mm(left, right, dims=NN):
    return lax.dot_general(left, right, dims, preferred_element_type=F32)


def head_lanes(rows, head):
    lane = lax.broadcasted_iota(jnp.int32, rows.shape, 1)
    keep = (lane < HEAD_DIM) if head == 0 else (lane >= HEAD_DIM)
    return jnp.where(keep, rows, jnp.zeros_like(rows))


def ahead(items, start):
    later = start(items[0])
    for at, item in enumerate(items):
        value = later
        if at + 1 < len(items):
            later = start(items[at + 1])
        yield item, value


def whole(shape, index=None, single=True):
    where = index or (0,) * len(shape)
    mode = {"pipeline_mode": pl.Buffered(1)} if single else {}
    return pl.BlockSpec(shape, lambda *_: where, **mode)


def kernel_call(body, name, grid, ins, outs, shapes, args, scratch=(), flops=0, prefetch=0, moved=0, exps=0):
    return pl.pallas_call(
        body,
        grid_spec=pltpu.PrefetchScalarGridSpec(
            num_scalar_prefetch=prefetch,
            grid=grid,
            in_specs=ins,
            out_specs=outs,
            scratch_shapes=list(scratch),
        ),
        out_shape=[jax.ShapeDtypeStruct(s, d) for s, d in shapes],
        compiler_params=pltpu.CompilerParams(vmem_limit_bytes=VMEM),
        cost_estimate=pl.CostEstimate(flops=flops // 32, bytes_accessed=moved // 32, transcendentals=exps // 32),
        name=name,
    )(*args)


def attend_kernel(q_ref, k_ref, v_ref, o_ref, lse_ref, vx_ref):
    keys = k_ref.shape[0]
    length = q_ref.shape[0]
    block = min(QB, length)
    vx_ref[:, :PAIR] = v_ref[...]
    vx_ref[:, PAIR:] = jnp.ones((keys, PAIR), BF16)
    items = list(itertools.product(range(0, length, block), range(2)))

    def products(item):
        start, head = item
        rows = head_lanes(q_ref[start : start + block, :], head)
        return mm(rows, k_ref[: start + block, :], NT)

    for (start, head), scores in ahead(items, products):
        limit = start + block
        last = scores[:, start:]
        col = lax.broadcasted_iota(jnp.int32, last.shape, 1)
        row = lax.broadcasted_iota(jnp.int32, last.shape, 0)
        last = jnp.where(col <= row, last, NEGATIVE)
        scores = jnp.concatenate([scores[:, :start], last], axis=1) if start else last
        top = jnp.max(scores, axis=1, keepdims=True)
        weights = jnp.exp2(scores - top).astype(BF16)
        total = mm(weights, vx_ref[:limit, :])
        out = total[:, :PAIR] / total[:, PAIR:]
        stat = (top + jnp.log2(total[:, PAIR:])).T
        lse_ref[0, head : head + 1, start:limit] = stat[:1, :]
        if head == 0:
            kept = out
        else:
            lane = lax.broadcasted_iota(jnp.int32, out.shape, 1)
            o_ref[start:limit, :] = jnp.where(lane < HEAD_DIM, kept, out).astype(BF16)


def attend_back_kernel(
    q_ref, k_ref, v_ref, o_ref, do_ref, lse_ref, dq_ref, dk_ref, dv_ref, acc_ref
):
    keys = k_ref.shape[0]
    block = min(QB, keys)
    product = (do_ref[...].astype(F32) * o_ref[...].astype(F32)).T
    acc_ref[...] = jnp.zeros_like(acc_ref)
    delta = [
        jnp.sum(product[head * HEAD_DIM : (head + 1) * HEAD_DIM, :], axis=0, keepdims=True)
        for head in range(2)
    ]
    items = list(itertools.product(range(0, keys, block), range(2)))

    def products(item):
        start, head = item
        queries = head_lanes(q_ref[start:, :], head)
        grads = head_lanes(do_ref[start:, :], head)
        return (
            queries,
            grads,
            mm(k_ref[start : start + block, :], queries, NT),
            mm(v_ref[start : start + block, :], grads, NT),
        )

    for (start, head), (queries, grads, scores, back) in ahead(items, products):
        probs = jnp.exp2(scores - lse_ref[0, head : head + 1, start:])
        edge = probs[:, :block]
        row = lax.broadcasted_iota(jnp.int32, edge.shape, 0)
        col = lax.broadcasted_iota(jnp.int32, edge.shape, 1)
        edge = jnp.where(row <= col, edge, 0.0)
        if start + block < keys:
            probs = jnp.concatenate([edge, probs[:, block:]], axis=1)
        else:
            probs = edge
        scored = (probs * (back - delta[head][:, start:])).astype(BF16)
        term_v = mm(probs.astype(BF16), grads)
        term_k = mm(scored, queries)
        acc_ref[start:, :] += mm(scored, head_lanes(k_ref[start : start + block, :], head), TN)
        if head == 0:
            grad_keys, grad_values = (term_k, term_v)
        else:
            dk_ref[start : start + block, :] = ((grad_keys + term_k) * LN2).astype(BF16)
            dv_ref[start : start + block, :] = (grad_values + term_v).astype(BF16)
    dq_ref[...] = (acc_ref[...] * SCALING).astype(BF16)


def column_pair(rows, offset):
    return pl.BlockSpec((rows, PAIR), lambda i, *_: (0, i + offset))


def attend(qkv):
    length = qkv.shape[0]
    pairs = HEADS // 2
    return kernel_call(
        attend_kernel,
        "attend",
        (pairs,),
        [column_pair(length, pairs * i) for i in range(3)],
        [column_pair(length, 0), pl.BlockSpec((1, 2, length), lambda i, *_: (i, 0, 0))],
        [((length, D), BF16), ((pairs, 2, length), F32)],
        (qkv, qkv, qkv),
        scratch=[pltpu.VMEM((length, 2 * PAIR), BF16)],
        flops=length * length * HEADS * 512,
        moved=8 * length * D,
        exps=length * length * HEADS // 2,
    )


def attend_back(qkv, out, grad, lse, first, count):
    length = qkv.shape[0]
    pairs = HEADS // 2
    return kernel_call(
        attend_back_kernel,
        "attend_back",
        (count,),
        [column_pair(length, pairs * i + first) for i in range(3)]
        + [column_pair(length, first)] * 2
        + [pl.BlockSpec((1, 2, length), lambda i, *_: (i + first, 0, 0))],
        [column_pair(length, 0)] * 3,
        [((length, count * PAIR), BF16)] * 3,
        (qkv, qkv, qkv, out, grad, lse),
        scratch=[pltpu.VMEM((length, PAIR), F32)],
        flops=length * length * count * 2560,
        moved=2 * 8 * length * count * PAIR,
        exps=length * length * count,
    )


def normed_of(rows):
    center = rows - jnp.mean(rows, axis=1, keepdims=True)
    inverse = lax.rsqrt(jnp.mean(center * center, axis=1, keepdims=True) + EPSILON)
    return (center * inverse, inverse)


def norm_input_grad(grads, normed, inverse, gain):
    scaled = grads * gain
    return inverse * (
        scaled
        - jnp.mean(scaled, axis=1, keepdims=True)
        - normed * jnp.mean(scaled * normed, axis=1, keepdims=True)
    )


def sums(rows):
    return jnp.sum(rows, axis=0, keepdims=True)


def add_row(ref, at, value, first):
    @pl.when(first)
    def _():
        ref[at : at + 1, :] = value

    @pl.when(jnp.logical_not(first))
    def _():
        ref[at : at + 1, :] += value


def gelu_pair(values):
    root = 0.7978845608028654
    square = values * values
    part = 0.5 + 0.5 * jnp.tanh(values * (root + (0.044715 * root) * square))
    out = values * part
    slope = part + (out - out * part) * (2.0 * root + (0.26829 * root) * square)
    return (out, slope)


def qkv_kernel(x_ref, w_ref, vec_ref, h_ref, qkv_ref):
    normed, _ = normed_of(x_ref[0].astype(F32))
    low = (normed * vec_ref[0:1, :] + vec_ref[1:2, :]).astype(BF16)
    h_ref[...] = low
    for part in range(3):
        mixed = mm(low, w_ref[:, part * D : (part + 1) * D]) + vec_ref[2 + part : 3 + part, :]
        if part == 0:
            mixed = mixed * (SCALING * LOG2E)
        qkv_ref[:, part * D : (part + 1) * D] = mixed.astype(BF16)


def pair_keys(kv_ref, at, keys):
    block = kv_ref[:, at : at + PAIR]
    return jnp.concatenate([head_lanes(block, 0), head_lanes(block, 1)], axis=0)


def cross_kernel(
    len_ref, x_ref, o_ref, ws_ref, wq_ref, wc_ref, kv_ref, vec_ref,
    x1_ref, h2_ref, q2_ref, o2_ref, x2_ref, h3_ref, lse_ref,
):
    keys = kv_ref.shape[0]
    after = x_ref[0].astype(F32) + mm(o_ref[...], ws_ref[...]) + vec_ref[0:1, :]
    x1_ref[...] = after
    normed, _ = normed_of(after)
    low = (normed * vec_ref[1:2, :] + vec_ref[2:3, :]).astype(BF16)
    h2_ref[...] = low
    q2_ref[...] = ((mm(low, wq_ref[...]) + vec_ref[3:4, :]) * (SCALING * LOG2E)).astype(BF16)
    ones = jnp.ones((keys, PAIR), BF16)

    def products(at):
        return mm(q2_ref[:, at : at + PAIR], pair_keys(kv_ref, at, keys), NT)

    for at, scores in ahead(list(range(0, D, PAIR)), products):
        pair = at // PAIR
        col = lax.broadcasted_iota(jnp.int32, (scores.shape[0], keys), 1)
        inside = col < len_ref[0]
        halves, tops = ([], [])
        for head in range(2):
            part = jnp.where(inside, scores[:, head * keys : (head + 1) * keys], NEGATIVE)
            top = jnp.max(part, axis=1, keepdims=True)
            halves.append(jnp.exp2(part - top).astype(BF16))
            tops.append(top)
        values = kv_ref[:, D + at : D + at + PAIR]
        right = jnp.concatenate(
            [
                jnp.concatenate([head_lanes(values, h), head_lanes(ones, h)], axis=1)
                for h in range(2)
            ],
            axis=0,
        )
        total = mm(jnp.concatenate(halves, axis=1), right)
        o2_ref[:, at : at + PAIR] = (total[:, :PAIR] / total[:, PAIR:]).astype(BF16)
        lane = lax.broadcasted_iota(jnp.int32, (scores.shape[0], PAIR), 1)
        stat = (jnp.where(lane < HEAD_DIM, tops[0], tops[1]) + jnp.log2(total[:, PAIR:])).T
        lse_ref[2 * pair : 2 * pair + 1, :] = stat[:1, :]
        lse_ref[2 * pair + 1 : 2 * pair + 2, :] = stat[HEAD_DIM : HEAD_DIM + 1, :]
    after = after + mm(o2_ref[...], wc_ref[...]) + vec_ref[4:5, :]
    x2_ref[...] = after
    normed, _ = normed_of(after)
    h3_ref[...] = (normed * vec_ref[5:6, :] + vec_ref[6:7, :]).astype(BF16)


def mlp_kernel(h_ref, wi_ref, wo_ref, bias_ref, x2_ref, last_ref, act_ref, slope_ref, out_ref, acc_ref):
    step = pl.program_id(0)

    @pl.when(step == 0)
    def _():
        acc_ref[...] = x2_ref[...] + last_ref[...]

    tile = min(512, h_ref.shape[0])
    parts = [slice(at, at + tile) for at in range(0, h_ref.shape[0], tile)]
    for rows, mixed in ahead(parts, lambda rows: mm(h_ref[rows, :], wi_ref[...])):
        act, slope = gelu_pair(mixed + bias_ref[0])
        act = act.astype(BF16)
        act_ref[rows, :] = act
        slope_ref[rows, :] = slope.astype(BF16)
        acc_ref[rows, :] += mm(act, wo_ref[...])

    @pl.when(step == pl.num_programs(0) - 1)
    def _():
        out_ref[...] = acc_ref[...].astype(BF16)


def du_kernel(g_ref, wo_ref, slope_ref, du_ref, sum_ref):
    total = None
    parts = [slice(at, at + QB) for at in range(0, g_ref.shape[0], QB)]
    for rows, grad in ahead(parts, lambda rows: mm(g_ref[rows, :], wo_ref[...], NT)):
        low = (grad * slope_ref[rows, :].astype(F32)).astype(BF16)
        du_ref[rows, :] = low
        part = sums(low.astype(F32))
        total = part if total is None else total + part
    sum_ref[0] = total


def norm3_kernel(du_ref, wi_ref, g_ref, x2_ref, gain_ref, wc_ref, dx_ref, dc_ref, do_ref, vec_ref):
    first = pl.program_id(0) == 0
    grads = None
    for step in range(wi_ref.shape[1] // D):
        cols = slice(step * D, (step + 1) * D)
        term = mm(du_ref[:, cols], wi_ref[:, cols], NT)
        grads = term if grads is None else grads + term
    normed, inverse = normed_of(x2_ref[...])
    out = g_ref[...].astype(F32) + norm_input_grad(grads, normed, inverse, gain_ref[...])
    dx_ref[...] = out
    low = out.astype(BF16)
    dc_ref[...] = low
    do_ref[...] = mm(low, wc_ref[...], NT).astype(BF16)
    add_row(vec_ref, 0, sums(grads * normed), first)
    add_row(vec_ref, 1, sums(grads), first)
    add_row(vec_ref, 2, sums(low.astype(F32)), first)
    add_row(vec_ref, 3, sums(g_ref[...].astype(F32)), first)


def cross_back_kernel(
    len_ref, q_ref, kv_ref, o_ref, do_ref, lse_ref, wq_ref, ws_ref, x1_ref, dx2_ref, gain_ref,
    dq_ref, dkv_ref, dx_ref, da_ref, do1_ref, vec_ref, acc_ref,
):
    step = pl.program_id(0)
    first = step == 0
    keys = kv_ref.shape[0]

    @pl.when(first)
    def _():
        acc_ref[...] = jnp.zeros_like(acc_ref)

    lane = lax.broadcasted_iota(jnp.int32, (keys, PAIR), 1)

    def products(at):
        queries = q_ref[:, at : at + PAIR]
        grads = do_ref[:, at : at + PAIR]
        both_keys = pair_keys(kv_ref, at, keys)
        return (
            queries,
            grads,
            both_keys,
            mm(both_keys, queries, NT),
            mm(pair_keys(kv_ref, D + at, keys), grads, NT),
        )

    for at, (queries, grads, both_keys, scores, back) in ahead(list(range(0, D, PAIR)), products):
        pair = at // PAIR
        product = (grads.astype(F32) * o_ref[:, at : at + PAIR].astype(F32)).T
        row = lax.broadcasted_iota(jnp.int32, (keys, scores.shape[1]), 0)
        inside = row < len_ref[0]
        probs, scored = ([], [])
        for head in range(2):
            span = slice(head * keys, (head + 1) * keys)
            at_head = 2 * pair + head
            prob = jnp.exp2(scores[span, :] - lse_ref[at_head : at_head + 1, :])
            prob = jnp.where(inside, prob, 0.0)
            delta = sums(product[head * HEAD_DIM : (head + 1) * HEAD_DIM, :])
            probs.append(prob.astype(BF16))
            scored.append((prob * (back[span, :] - delta)).astype(BF16))
        probs, scored = (jnp.concatenate(probs, axis=0), jnp.concatenate(scored, axis=0))
        for base, left, right in ((0, scored, queries), (D, probs, grads)):
            both = mm(left, right)
            acc_ref[:, base + at : base + at + PAIR] += jnp.where(
                lane < HEAD_DIM, both[:keys, :], both[keys:, :]
            )
        dq_ref[:, at : at + PAIR] = (mm(scored, both_keys, TN) * SCALING).astype(BF16)

    @pl.when(step == pl.num_programs(0) - 1)
    def _():
        dkv_ref[:, :D] = (acc_ref[:, :D] * LN2).astype(BF16)
        dkv_ref[:, D:] = acc_ref[:, D:].astype(BF16)

    grads = mm(dq_ref[...], wq_ref[...], NT)
    normed, inverse = normed_of(x1_ref[...])
    out = dx2_ref[...] + norm_input_grad(grads, normed, inverse, gain_ref[...])
    dx_ref[...] = out
    low = out.astype(BF16)
    da_ref[...] = low
    do1_ref[...] = mm(low, ws_ref[...], NT).astype(BF16)
    add_row(vec_ref, 0, sums(grads * normed), first)
    add_row(vec_ref, 1, sums(grads), first)
    add_row(vec_ref, 2, sums(low.astype(F32)), first)
    add_row(vec_ref, 3, sums(dq_ref[...].astype(F32)), first)


def norm1_kernel(*refs):
    *grad_refs, w_ref, x_ref, dx1_ref, gain_ref, text_ref, out_ref, vec_ref = refs
    first = pl.program_id(0) == 0
    grads, at = (None, 0)
    groups = len(grad_refs) // 3
    rows_q, rows_v = ([], [])
    for group in range(groups):
        for part in range(3):
            ref = grad_refs[3 * group + part]
            wide = ref.shape[1]
            base = part * D + group * wide
            term = mm(ref[...], w_ref[:, base : base + wide], NT)
            grads = term if grads is None else grads + term
        rows_q.append(sums(grad_refs[3 * group][...].astype(F32)))
        rows_v.append(sums(grad_refs[3 * group + 2][...].astype(F32)))
    normed, inverse = normed_of(x_ref[0].astype(F32))
    back = norm_input_grad(grads, normed, inverse, gain_ref[...])
    tile = back.shape[0]
    out_ref[0, :tile, :] = (dx1_ref[...] + back).astype(BF16)
    out_ref[0, tile:, :] = text_ref[...]
    add_row(vec_ref, 0, sums(grads * normed), first)
    add_row(vec_ref, 1, sums(grads), first)
    add_row(vec_ref, 2, jnp.concatenate(rows_q, axis=1), first)
    add_row(vec_ref, 3, jnp.concatenate(rows_v, axis=1), first)


def weight_grad_kernel(units, count, scattered, place_ref, *refs):
    operands, (sent_ref, kept_ref, acc_ref) = (refs[:count], refs[count:])
    step = pl.program_id(0)
    block = acc_ref.shape[0] // 32
    known = sorted(set(units))
    for left, right in known:
        steps = [t for t, unit in enumerate(units) if unit == (left, right)]
        hit = step == steps[0]
        for t in steps[1:]:
            hit = jnp.logical_or(hit, step == t)

        @pl.when(hit)
        def _():
            acc_ref[...] = mm(operands[left][...], operands[right][...], TN)

    halves = ((sent_ref, 1 - place_ref[1]), (kept_ref, place_ref[1]))
    if not scattered:
        wide = 4 * block
        for z, (ref, core) in itertools.product(range(4), halves):
            row = pl.multiple_of((2 * z + core) * wide, wide)
            ref[z * wide : (z + 1) * wide, :] = acc_ref[pl.ds(row, wide), :].astype(BF16)
        return
    for order, far, near, low in itertools.product(range(2), repeat=4):
        z = place_ref[0] ^ (2 * order + low)
        y, x = (near, far) if order else (far, near)
        inner = (place_ref[2] ^ y) * 2 + (place_ref[3] ^ x)
        at = (((order * 2 + far) * 2 + near) * 2 + low) * block
        for ref, core in halves:
            row = pl.multiple_of(((z * 2 + core) * 4 + inner) * block, block)
            ref[at : at + block, :] = acc_ref[pl.ds(row, block), :].astype(BF16)


def weight_grads(places, operands, specs, units, width, name, scattered=True):
    steps = len(units)
    tokens = operands[0].shape[0]
    return kernel_call(
        functools.partial(weight_grad_kernel, tuple(units), len(operands), scattered),
        name,
        (steps,),
        specs,
        [pl.BlockSpec((D // 2, width), lambda t, *_: (0, t))] * 2,
        [((D // 2, steps * width), BF16)] * 2,
        (places, *operands),
        scratch=[pltpu.VMEM((D, width), F32)],
        flops=2 * tokens * D * width * steps,
        moved=2 * D * width * steps + 2 * tokens * D,
        prefetch=1,
    )


def place_kernel(per, place_ref, *refs):
    pieces, out_ref = (refs[:8], refs[8])
    for index, piece in enumerate(pieces):
        far_core, far_side, second = (index // 4, index % 2, (index // 2) % 2)
        for near in range(2):
            for low in range(2):
                z = 2 * second + low
                y, x = (near, far_side) if second else (far_side, near)
                row = (place_ref[0] ^ z) * 2 + (place_ref[1] ^ far_core)
                row = (row * 2 + (place_ref[2] ^ y)) * 2 + (place_ref[3] ^ x)
                row = pl.multiple_of(row * per, per)
                out_ref[pl.ds(row, per), :] = piece[near, low]


def put_in_order(places, pieces):
    near, low, per, width = pieces[0].shape
    wide = width // 5
    (out,) = kernel_call(
        functools.partial(place_kernel, per),
        "put_in_order",
        (5,),
        [pl.BlockSpec((near, low, per, wide), lambda t, *_: (0, 0, 0, t))] * 8,
        [pl.BlockSpec((per * 32, wide), lambda t, *_: (0, t))],
        [((per * 32, width), BF16)],
        (places, *pieces),
        moved=4 * per * 32 * width,
        prefetch=1,
    )
    return out


def total_of(*terms):
    total = terms[0].astype(F32)
    for term in terms[1:]:
        total = total + term.astype(F32)
    return total


AXES = ("z", "core", "seq")


class Ring:
    def __init__(self, mesh):
        self.count = mesh.size
        self.seq, self.z, self.c = (lax.axis_index(a) for a in ("seq", "z", "core"))
        self.x, self.y = (self.seq % 2, self.seq // 2)

    def swap(self, array, bits):
        return lax.ppermute(array, AXES, [(i, i ^ bits) for i in range(self.count)])


class Gather:
    def __init__(self, ring, shard):
        self.ring = ring
        self.hold = [shard] * 3
        self.own = shard
        self.bits = (8, 16, 24)

    def launch(self):
        self.hold = [self.ring.swap(array, bits) for array, bits in zip(self.hold, self.bits)]

    def near(self):
        self.pair = [jnp.stack([self.own, self.hold[0]]), jnp.stack(self.hold[1:])]
        self.hold, self.bits = (list(self.pair), (1, 2))

    def far(self):
        self.pair = [jnp.stack([mine, came]) for mine, came in zip(self.pair, self.hold)]
        self.hold, self.bits = (list(self.pair), (2, 1))

    def core(self):
        self.quad = [self.pair[0], self.hold[0], self.pair[1], self.hold[1]]
        self.hold, self.bits = (list(self.quad), (4,) * 4)

    def done(self, places):
        return put_in_order(places, self.quad + self.hold)


class Steps:
    def __init__(self, ring, halves):
        self.ring = ring
        shape = (2, 2, 2, 2, halves[0].shape[0] // 16, halves[0].shape[1])
        sent, self.kept = (half.reshape(shape) for half in halves)
        self.hold, self.bits = ([sent], (4,))

    def launch(self):
        self.hold = [self.ring.swap(array, bits) for array, bits in zip(self.hold, self.bits)]

    def near(self):
        (self.got,) = self.hold
        self.bits = (2, 1)
        self.hold = [total_of(self.kept[i, 1], self.got[i, 1]).astype(BF16) for i in range(2)]

    def far(self):
        parts = [(self.kept[i, 0], self.got[i, 0], self.hold[i]) for i in range(2)]
        self.bits = (1, 2)
        self.hold = [total_of(*(p[1] for p in parts[i])).astype(BF16) for i in range(2)]
        self.parts = [total_of(*(p[0] for p in parts[i])).astype(BF16) for i in range(2)]

    def deep(self):
        parts = [(self.parts[i], self.hold[i]) for i in range(2)]
        self.result = total_of(*(p[0] for p in parts[0]))
        self.bits = (8, 16, 24)
        self.hold = [
            total_of(*(p[step % 2] for p in parts[step // 2])).astype(BF16) for step in (1, 2, 3)
        ]

    def scatter(self):
        parts = [total_of(self.parts[i], self.hold[i]).astype(BF16) for i in range(2)]
        self.hold = [jnp.concatenate(parts).reshape(-1, self.kept.shape[-1])]

    def launch_scatter(self):
        self.result = lax.psum_scatter(self.hold[0], "z", scatter_dimension=0, tiled=True)
        self.hold = []

    def done(self):
        return total_of(self.result, *self.hold)


def at_once(*groups):
    arrays = [group if isinstance(group, list) else group.hold for group in groups]
    arrays = lax.optimization_barrier(arrays)
    for group, values in zip(groups, arrays):
        if isinstance(group, list):
            group[:] = values
        else:
            group.hold = list(values)


def whole_images(mesh, *args):
    (
        image_tokens, text_states, text_lengths, out_grad, norm1_gain, norm1_bias, self_qkv,
        self_bias_qv, self_out, self_out_bias, norm2_gain, norm2_bias, cross_query, cross_kv,
        cross_bias_qv, cross_out, cross_out_bias, norm3_gain, norm3_bias, mlp_in, mlp_in_bias,
        mlp_out, mlp_out_bias,
    ) = args
    n_seq = mesh.shape["seq"]
    ring = Ring(mesh)
    part, text_part = (image_tokens.shape[1], text_states.shape[1])
    rows = norm1_gain.shape[0]
    fours = mlp_out.shape[0] // rows
    length, prompt = (part * n_seq, text_part * n_seq)
    places = jnp.stack([ring.z, ring.c, ring.y, ring.x]).astype(jnp.int32)
    flat_places = places * jnp.array([0, 1, 1, 1], jnp.int32)

    def gather(shard):
        return lax.all_gather(shard, AXES, axis=0, tiled=True)

    def across(vectors):
        return jnp.concatenate([v.reshape(ring.count, -1) for v in vectors], axis=1)

    def line(*vectors):
        table = jnp.stack(vectors)
        return jnp.pad(table, ((0, -len(vectors) % 8), (0, 0)))

    in_shard = mlp_in.reshape(rows, ring.count, fours, rows).transpose(0, 2, 1, 3).reshape(rows, -1)
    out_shard = mlp_out.reshape(fours, rows, D).transpose(1, 0, 2).reshape(rows, -1)
    mlp = gather(jnp.concatenate([in_shard, out_shard], axis=1))
    vectors = [
        norm1_gain, norm1_bias, self_out_bias, norm2_gain, norm2_bias, cross_out_bias,
        norm3_gain, norm3_bias, mlp_out_bias, self_bias_qv, cross_bias_qv, mlp_in_bias,
    ]
    strip = jnp.concatenate(vectors).reshape(-1, rows)
    strip = jnp.pad(strip, ((0, 128 - strip.shape[0]), (0, 0))).T
    w_first = Gather(ring, jnp.concatenate([self_qkv, strip], axis=1))
    w_second = Gather(
        ring, jnp.concatenate([self_out, cross_query, cross_kv, cross_out], axis=1)
    )
    w_first.launch()
    now = [
        lax.all_to_all(
            jnp.concatenate([image_tokens, text_states], axis=1), "seq", 0, 0, tiled=True
        )
    ]
    at_once(now, w_first)
    (moved,) = now
    w_first.near()
    at_once(w_first, w_second)
    w_first.launch()
    w_second.launch()
    at_once(w_first)
    w_first.far()
    w_first.launch()
    at_once(w_first, w_second)
    w_first.core()
    w_second.near()
    at_once(w_first, w_second)
    w_first.launch()
    w_second.launch()
    at_once(w_first)
    first = w_first.done(places)

    texts = moved[:, part:].reshape(prompt, D)
    prompt_length = lax.dynamic_slice_in_dim(text_lengths, ring.seq, 1, 0)

    table = lax.optimization_barrier(first[:, 3 * D :]).T.astype(F32)
    full, at = ([], 0)
    for v in vectors[:-1]:
        wide = v.shape[0] // rows
        full.append(table[at : at + wide].reshape(wide, -1, rows).transpose(1, 0, 2).reshape(-1))
        at += wide
    bias_in = table[at : at + fours].reshape(fours, 1, D)
    (g1, b1, bias_out, g2, b2, bias_cross, g3, b3, bias_last, bias_qv, bias_qv2) = full
    zero = jnp.zeros((D,), F32)

    tile = part
    grid = (n_seq,)
    row_tile = pl.BlockSpec((tile, D), lambda i, *_: (i, 0))
    token_tile = pl.BlockSpec((1, tile, D), lambda i, *_: (i, 0, 0))
    vec8, vec1 = (whole((8, D)), whole((1, D)))
    sum8 = pl.BlockSpec((8, D), lambda *_: (0, 0))
    square = (D, D)
    flat = (length, D)

    def weight_block(index):
        return whole(square, (0, index))

    def streamed(offset):
        return pl.BlockSpec(square, lambda t, *_: (0, t + offset))

    def columns(width):
        return pl.BlockSpec((tile, width), lambda i, *_: (i, 0))

    stat_tile = pl.BlockSpec((HEADS, tile), lambda i, *_: (0, i))
    unit = 2 * length * D * D

    h1, qkv = kernel_call(
        qkv_kernel, "qkv", grid,
        [token_tile, whole((D, 3 * D)), vec8],
        [row_tile, columns(3 * D)],
        [(flat, BF16), ((length, 3 * D), BF16)],
        (moved, first, line(g1, b1, bias_qv[:D], zero, bias_qv[D:])),
        flops=3 * unit, moved=16 * length * D,
    )
    now = [qkv, h1]
    at_once(now, w_second)
    w_second.far()
    at_once(now, w_second)
    qkv, h1 = now
    w_second.launch()
    o1, lse1 = attend(qkv)
    now = [o1]
    at_once(now, w_second)
    w_second.core()
    w_second.launch()
    at_once(now, w_second)
    (o1,) = now
    second = w_second.done(places)
    kv2 = (mm(texts, second[:, 2 * D : 4 * D]) + jnp.concatenate([zero, bias_qv2[D:]])).astype(BF16)
    x1, h2, q2, o2, x2, h3, lse2 = kernel_call(
        cross_kernel, "cross", grid,
        [token_tile, row_tile, weight_block(0), weight_block(1), weight_block(4),
         whole((prompt, 2 * D)), vec8],
        [row_tile] * 6 + [stat_tile],
        [(flat, F32), (flat, BF16), (flat, BF16), (flat, BF16), (flat, F32), (flat, BF16),
         ((HEADS, length), F32)],
        (prompt_length, moved, o1, second, second, second, kv2,
         line(bias_out, g2, b2, bias_qv2[:D], bias_cross, g3, b3)),
        flops=5 * unit, moved=30 * length * D, prefetch=1,
    )
    out_grad, h3 = lax.optimization_barrier((out_grad, h3))
    grad_rows = lax.all_to_all(out_grad, "seq", 0, 0, tiled=True).reshape(flat)
    hidden = (length, fours * D)
    by_unit = pl.BlockSpec((length, D), lambda t, *_: (0, t))
    act, slope, out = kernel_call(
        mlp_kernel, "mlp", (fours,),
        [whole(flat), streamed(0), streamed(fours),
         pl.BlockSpec((1, 1, D), lambda t, *_: (t, 0, 0)), whole(flat), vec1],
        [by_unit, by_unit, whole(flat, single=False)],
        [(hidden, BF16), (hidden, BF16), (flat, BF16)],
        (h3, mlp, mlp, bias_in, x2, bias_last.reshape(1, D)),
        scratch=[pltpu.VMEM(flat, F32)],
        flops=2 * fours * unit, moved=40 * length * D,
    )

    full_flat = whole(flat)
    r_out = Steps(
        ring,
        weight_grads(
            flat_places, (act, grad_rows), [by_unit, full_flat], [(0, 1)] * fours, D, "d_mlp_out"
        ),
    )
    now = [out, slope, grad_rows]
    at_once(now, r_out)
    out, slope, grad_rows = now
    leaving_out = [lax.all_to_all(out.reshape(n_seq, part, D), "seq", 0, 0, tiled=True)]
    r_out.launch()
    du, du_sum = kernel_call(
        du_kernel, "du", (fours,),
        [full_flat, streamed(fours), by_unit],
        [by_unit, pl.BlockSpec((1, 1, D), lambda t, *_: (t, 0, 0))],
        [(hidden, BF16), ((fours, 1, D), F32)],
        (grad_rows, mlp, slope),
        flops=fours * unit, moved=26 * length * D,
    )
    now = [du, h3]
    at_once(now, r_out)
    r_out.near()
    at_once(now, r_out)
    r_out.launch()
    du, h3 = now
    r_in = Steps(
        ring,
        weight_grads(flat_places, (h3, du), [full_flat, by_unit], [(0, 1)] * fours, D, "d_mlp_in"),
    )
    now = [du]
    at_once(now, leaving_out, r_in)
    (du,) = now
    (block_output,) = leaving_out
    r_in.launch()
    dx2, dc, do2, sums3 = kernel_call(
        norm3_kernel, "norm3_back", grid,
        [columns(fours * D), whole((D, fours * D)), row_tile, row_tile, vec1, weight_block(4)],
        [row_tile] * 3 + [sum8],
        [(flat, F32), (flat, BF16), (flat, BF16), ((8, D), F32)],
        (du, mlp, grad_rows, x2, g3.reshape(1, D), second),
        flops=(fours + 1) * unit, moved=32 * length * D,
    )
    now = [dx2, dc, do2]
    at_once(now, r_in, r_out)
    r_out.far()
    r_in.near()
    at_once(now, r_in, r_out)
    r_out.launch()
    r_in.launch()
    dx2, dc, do2 = now
    dq2, dkv2, dx1, da, do1, sums2 = kernel_call(
        cross_back_kernel, "cross_back", grid,
        [row_tile, whole((prompt, 2 * D)), row_tile, row_tile, stat_tile,
         weight_block(1), weight_block(0), row_tile, row_tile, vec1],
        [row_tile, whole((prompt, 2 * D), single=False), row_tile, row_tile, row_tile, sum8],
        [(flat, BF16), ((prompt, 2 * D), BF16), (flat, F32), (flat, BF16), (flat, BF16), ((8, D), F32)],
        (prompt_length, q2, kv2, o2, do2, lse2, second, second, x1, dx2, g2.reshape(1, D)),
        scratch=[pltpu.VMEM((prompt, 2 * D), F32)],
        flops=5 * unit, moved=34 * length * D, prefetch=1,
    )
    text_block = [whole((prompt, D), (0, i)) for i in range(2)]
    r_mid = Steps(
        ring,
        weight_grads(
            places,
            (o1, da, o2, dc, h2, dq2, texts, dkv2, dkv2),
            [full_flat] * 6 + [whole((prompt, D))] + text_block,
            [(0, 1), (2, 3), (4, 5), (6, 7), (6, 8)],
            D,
            "d_mid",
        ),
    )
    now = [do1, dx1, dkv2]
    at_once(now, r_mid, r_in, r_out)
    r_in.far()
    r_out.scatter()
    at_once(now, r_mid, r_in, r_out)
    do1, dx1, dkv2 = now
    r_mid.launch()
    r_in.launch()
    r_out.launch_scatter()
    count = HEADS // 4
    back_a = list(attend_back(qkv, o1, do1, lse1, 0, count))
    now = [do1]
    at_once(now, back_a, r_mid, r_in)
    r_mid.near()
    r_in.scatter()
    at_once(now, back_a, r_mid, r_in)
    (do1,) = now
    r_mid.launch()
    r_in.launch_scatter()
    back_b = list(attend_back(qkv, o1, do1, lse1, count, count))
    narrow = [full_flat] + [whole((length, count * PAIR))] * 6
    r_qkv = Steps(
        ring,
        weight_grads(
            places, (h1, *back_a, *back_b), narrow, [(0, 1 + i) for i in range(6)],
            count * PAIR, "d_qkv",
        ),
    )
    at_once(back_b, r_qkv, r_mid)
    r_qkv.launch()
    r_mid.far()
    at_once(back_b, r_mid)
    r_mid.launch()
    dv2_sum = jnp.sum(dkv2[:, D:].astype(F32), axis=0)
    early = [
        sums2[2], sums2[0], sums2[1], sums3[2], sums3[0], sums3[1], sums3[3],
        jnp.concatenate([sums2[3], dv2_sum]),
        du_sum.reshape(fours, ring.count, rows).transpose(1, 0, 2).reshape(-1),
    ]
    early = [across(early)]
    text_grad = mm(dkv2, second[:, 2 * D : 4 * D], NT).astype(BF16)
    now = [text_grad]
    at_once(back_b, r_qkv, r_mid, early, now)
    r_qkv.near()
    r_mid.deep()
    at_once(back_b, r_qkv, r_mid, early, now)
    (text_grad,) = now
    r_qkv.launch()
    r_mid.launch()
    leaving, sums1 = kernel_call(
        norm1_kernel, "norm1_back", grid,
        [columns(count * PAIR)] * 6 + [whole((D, 3 * D)), token_tile, row_tile, vec1]
        + [pl.BlockSpec((text_part, D), lambda i, *_: (i, 0))],
        [pl.BlockSpec((1, part + text_part, D), lambda i, *_: (i, 0, 0)), sum8],
        [(moved.shape, BF16), ((8, D), F32)],
        (*back_a, *back_b, first, moved, dx1, g1.reshape(1, D), text_grad),
        flops=3 * unit, moved=18 * length * D,
    )
    leaving = [lax.all_to_all(leaving, "seq", 0, 0, tiled=True)]
    at_once(r_qkv)
    r_qkv.far()
    at_once(r_qkv)
    r_qkv.launch()
    late = [across([sums1[0], sums1[1], jnp.concatenate([sums1[2], sums1[3]])])]
    mlp_out_grad = r_out.done().reshape(rows, fours, D).transpose(1, 0, 2).reshape(-1, D)
    mlp_in_grad = r_in.done().reshape(rows, fours, ring.count, rows)
    mlp_in_grad = mlp_in_grad.transpose(0, 2, 1, 3).reshape(rows, -1)
    now = [mlp_out_grad, mlp_in_grad]
    at_once(r_qkv, r_mid, late, leaving, now)
    mlp_out_grad, mlp_in_grad = now
    r_qkv.deep()
    at_once(r_qkv, late, early)
    r_qkv.launch()
    small = jnp.concatenate([early[0], late[0]], axis=1)
    small = jnp.sum(lax.all_to_all(small, AXES, 0, 0, tiled=True), axis=0)
    leaving = leaving[0].astype(F32)
    mid, last = (r_mid.done(), r_qkv.done())
    wide = count * PAIR
    self_qkv_grad = jnp.concatenate(
        [last[:, (3 * j + i) * wide : (3 * j + i + 1) * wide] for i in range(3) for j in range(2)],
        axis=1,
    )

    def mine(total, at, wide):
        return total[at * rows : at * rows + wide]

    two = 2 * rows
    return (
        block_output,
        leaving[:, :part],
        leaving[:, part:],
        mine(small, 9 + fours, rows),
        mine(small, 10 + fours, rows),
        self_qkv_grad,
        mine(small, 11 + fours, two),
        mid[:, :D],
        mine(small, 0, rows),
        mine(small, 1, rows),
        mine(small, 2, rows),
        mid[:, 2 * D : 3 * D],
        mid[:, 3 * D :],
        mine(small, 7, two),
        mid[:, D : 2 * D],
        mine(small, 3, rows),
        mine(small, 4, rows),
        mine(small, 5, rows),
        mlp_in_grad,
        mine(small, 9, fours * rows),
        mlp_out_grad,
        mine(small, 6, rows),
    )


def places_of(images, rows):
    ins = (
        P(images, "seq", None),
        P(images, "seq", None),
        P(images),
        P(images, "seq", None),
        P(rows),
        P(rows),
        P(rows, None),
        P(rows),
        P(rows, None),
        P(rows),
        P(rows),
        P(rows),
        P(rows, None),
        P(rows, None),
        P(rows),
        P(rows, None),
        P(rows),
        P(rows),
        P(rows),
        P(rows, None),
        P(rows),
        P(rows, None),
        P(rows),
    )
    outs = (
            P(images, "seq", None),
            P(images, "seq", None),
            P(images, "seq", None),
            P(rows),
            P(rows),
            P(rows, None),
            P(rows),
            P(rows, None),
            P(rows),
            P(rows),
            P(rows),
            P(rows, None),
            P(rows, None),
            P(rows),
            P(rows, None),
            P(rows),
            P(rows),
            P(rows),
            P(rows, None),
            P(rows),
            P(rows, None),
            P(rows),
        )
    return (ins, outs)


def solution(mesh):
    n_dp, n_seq = (mesh.shape["dp"], mesh.shape["seq"])
    spread = places_of("dp", ("dp", "seq"))
    single = places_of(("z", "core"), AXES)

    def layer(*args):
        images = args[0].shape[0] // n_dp
        if images == n_seq and (n_dp, n_seq) == (8, 4):
            fine = Mesh(mesh.devices.reshape(n_dp // 2, 2, n_seq), AXES)
            plan, place, grid = (functools.partial(whole_images, fine), single, fine)
        else:
            plan, place, grid = (per_device, spread, mesh)
        return jax.shard_map(
            plan, mesh=grid, in_specs=place[0], out_specs=place[1], check_vma=False
        )(*args)

    return layer
```
